32 devices in a mesh: groups: 2 (over y), row: 16 (over z, x, core).
Axes of the slice: x: 2, y: 2, z: 4, core: 2. Of those that a mesh axis runs over, the one named last changes fastest.
Arguments:
- object_tiles: bfloat16 [8192, 2, 2048], P(('groups', 'row')), parts along dimension 0, may hold values from -4 to 4
- probe: float32 [4, 256, 2, 256], replicated, may hold values from -3 to 3
- measured: bfloat16 [192, 256, 256], P(('groups', 'row')), parts along dimension 0, may hold values from 0.19921875 to 2.5
- offset_row: int32 [192], P(('groups', 'row')), parts along dimension 0, may hold values from 0 to 255
- offset_col: int32 [192], P(('groups', 'row')), parts along dimension 0, may hold values from 0 to 1791
- subpixel: int32 [192], P(('groups', 'row')), parts along dimension 0, may hold values from 0 to 15
- live_count: int32 [32], P(('groups', 'row')), parts along dimension 0, may hold values from 1 to 6, 48 in all
Outputs:
- object_grad: float32 [8192, 2, 2048], P(('groups', 'row')), parts along dimension 0
- probe_grad: float32 [8, 256, 2, 256], P('groups'), parts along dimension 0
- position_grad: float32 [2, 192], P(None, ('groups', 'row')), parts along dimension 1
The draws below stay inside these ranges and needn't reach their ends.
There are 2 independent parts, one for each index of `groups`. The reference program is written for one: setup_inputs(seed, part) draws one part's arguments, and reference() takes and returns one part's arrays. A program takes and returns all parts, laid end to end along the dimension named above; an argument that names none is the same for every part. Nothing has to cross between parts.
Inputs may be any that keep to these rules, and one draw needn't show every extreme that they name: Device d's live slots are its first live_count[d] slots; live_count sums to 48 and reaches 6 on some device.
All inputs are finite; a program needn't handle non-finite values.
Results may differ from the reference program's by a relative error of at most 0.0099.
Values may be sent and summed in bfloat16 or wider, within the bound.
No kernel may reach another device: no remote copies, remote signals or barrier semaphores. Data moves between devices by JAX's collectives and lax.ppermute only.
A program may use at most 128 MiB of HBM per device.

```python
import math
import jax
import jax.numpy as jnp
import numpy as np
from jax import lax

PATCH = 256
MODES = 4
ROWS_DEV = 256
OW = 2048
SLOTS = 6
OH = 4096
NPOS = 96
MINI = 48
N_ROW = 16


def set_ends(array, key, low, high):
    dims = array.shape
    spot = [jax.random.randint(jax.random.fold_in(key, axis), (), 0, dims[axis]) for axis in range(len(dims))]
    array = array.at[tuple(spot)].set(low)
    longest = dims.index(max(dims))
    spot[longest] = (spot[longest] + 1) % dims[longest]
    return array.at[tuple(spot)].set(high)


def block_scale(rng, dims, shards, least, high):
    factor_of = 1.0
    for dim, shards_of in shards:
        heights = jax.random.uniform(jax.random.fold_in(jax.random.fold_in(rng, 6), dim), (shards_of,), jnp.float32, least / len(shards), high / len(shards))
        factor_of = factor_of * jnp.repeat(jnp.exp(heights), dims[dim] // shards_of).reshape((-1,) + (1,) * (len(dims) - 1 - dim))
    return factor_of


def split_up(number_of, total, reach, lean):
    portions = [(1 << 20) // math.isqrt(grade ** lean) + 1 for grade in range(2, number_of + 1)]
    spare, counts = total - reach - (number_of - 1), [1] * (number_of - 1)
    while spare > 0:
        movable = [i for i in range(number_of - 1) if counts[i] < reach]
        mass, budget = sum([portions[i] for i in movable]), spare
        for i in movable:
            more = min(reach - counts[i], max(1, budget * portions[i] // mass), spare)
            counts[i] = counts[i] + more
            spare = spare - more
    return np.array([reach] + counts)


def uneven(stream_key, amount, total, most, lean):
    if amount == 2:
        one = jax.random.randint(stream_key, (), max(1, total - most), min(most, total - 1) + 1)
        return jnp.stack([one, total - one])
    tallies = jnp.asarray(split_up(amount, total, most, lean), jnp.int32)
    pairs = (amount - 1) // 2
    source_of, sink = tallies[1:1 + 2 * pairs:2], tallies[2:2 + 2 * pairs:2]
    slack = jnp.minimum(source_of - 1, most - sink)
    moved = jax.random.randint(jax.random.fold_in(stream_key, 1), (pairs,), 0, 1 << 20) % (slack + 1)
    tallies = tallies.at[1:1 + 2 * pairs:2].set(source_of - moved).at[2:2 + 2 * pairs:2].set(sink + moved)
    return tallies[jax.random.permutation(jax.random.fold_in(stream_key, 2), amount)]


def centred(stream_key, extent, width, most, pieces=(), held_as=jnp.bfloat16):
    entries = jax.random.normal(stream_key, extent, jnp.float32) * width
    if len(pieces) > 0:
        entries = block_scale(stream_key, extent, pieces, -0.22, 0.18) * entries
    return jnp.clip(entries, min=-most, max=most).astype(held_as)


def setup_inputs(seed: int = 0, part: int = 0) -> dict:
    key_of = jax.random.split(jax.random.key(seed), 8)
    part_splits = jax.random.split(jax.random.fold_in(key_of[7], part), 8)
    object_tiles = centred(part_splits[0], (OH, 2, OW), 0.7, 4.0, ((0, 16),))
    probe = centred(key_of[1], (MODES, PATCH, 2, PATCH), 0.5, 3.0, (), jnp.float32)
    measured = jnp.clip(0.19921875 + 2.3007812 * jax.random.uniform(part_splits[2], (NPOS, PATCH, PATCH), jnp.float32) ** block_scale(part_splits[2], (NPOS, PATCH, PATCH), ((0, 16),), -0.2, 0.2), 0.19921875, 2.5).astype(jnp.bfloat16)
    offset_row = set_ends(jax.random.randint(part_splits[3], (NPOS,), 0, ROWS_DEV), jax.random.fold_in(part_splits[3], 1), 0, ROWS_DEV - 1).astype(jnp.int32)
    offset_col = set_ends(jax.random.randint(part_splits[4], (NPOS,), 0, OW - PATCH), jax.random.fold_in(part_splits[4], 1), 0, (OW - PATCH) - 1).astype(jnp.int32)
    subpixel = set_ends(jax.random.randint(part_splits[5], (NPOS,), 0, 16), jax.random.fold_in(part_splits[5], 1), 0, 15).astype(jnp.int32)
    live_count = uneven(part_splits[6], N_ROW, MINI, SLOTS, 2).astype(jnp.int32)
    return {"object_tiles": object_tiles, "probe": probe, "measured": measured, "offset_row": offset_row, "offset_col": offset_col, "subpixel": subpixel, "live_count": live_count}


def dft_tables(patch):
    index = jnp.arange(patch, dtype=jnp.int32)
    phase = index[:, None] * index[None, :] % patch
    angle = phase.astype(jnp.float32) * (2.0 * math.pi / patch)
    scale = 1.0 / math.sqrt(patch)
    cosine = (jnp.cos(angle) * scale).astype(jnp.bfloat16)
    sine = (jnp.sin(angle) * scale).astype(jnp.bfloat16)
    along_x = jnp.concatenate([jnp.concatenate([cosine, -sine], 1), jnp.concatenate([sine, cosine], 1)], 0)
    along_y = jnp.concatenate([jnp.stack([cosine, sine], -1).reshape(patch, 2 * patch), jnp.stack([-sine, cosine], -1).reshape(patch, 2 * patch)], 0)
    inverse_y = jnp.stack([jnp.concatenate([cosine, -sine], 1), jnp.concatenate([sine, cosine], 1)], 1).reshape(2 * patch, 2 * patch)
    inverse_x = jnp.concatenate([jnp.concatenate([cosine, sine], 1), jnp.concatenate([-sine, cosine], 1)], 0)
    return (along_x, along_y, inverse_y, inverse_x)

def fractions(code):
    return ((code // 4).astype(jnp.float32) * 0.25, (code % 4).astype(jnp.float32) * 0.25)

def interpolate(window, code):
    frac_y, frac_x = fractions(code)
    cells = window.astype(jnp.float32)
    size = cells.shape[0] - 1
    upper = (1.0 - frac_x) * cells[:size, :, :size] + frac_x * cells[:size, :, 1:]
    lower = (1.0 - frac_x) * cells[1:, :, :size] + frac_x * cells[1:, :, 1:]
    return (1.0 - frac_y) * upper + frac_y * lower

def spread(grad_patch, frac_y, frac_x):

    def sideways(part):
        return jnp.pad((1.0 - frac_x) * part, ((0, 0), (0, 0), (0, 1))) + jnp.pad(frac_x * part, ((0, 0), (0, 0), (1, 0)))
    upper = sideways((1.0 - frac_y) * grad_patch)
    lower = sideways(frac_y * grad_patch)
    return jnp.pad(upper, ((0, 1), (0, 0), (0, 0))) + jnp.pad(lower, ((1, 0), (0, 0), (0, 0)))

def slopes(window, grad_patch, frac_y, frac_x):
    cells = window.astype(jnp.float32)
    size = cells.shape[0] - 1
    down = cells[1:] - cells[:size]
    slope_y = (1.0 - frac_x) * down[:, :, :size] + frac_x * down[:, :, 1:]
    across = cells[:, :, 1:] - cells[:, :, :size]
    slope_x = (1.0 - frac_y) * across[:size] + frac_y * across[1:]
    return (jnp.sum(grad_patch * slope_y) / size, jnp.sum(grad_patch * slope_x) / size)

def matmul(left, right):
    return jnp.dot(left.astype(jnp.float32), right.astype(jnp.float32), precision=lax.Precision.HIGHEST)

def batched(left, right):
    return jnp.einsum('ab,mbk->mak', left.astype(jnp.float32), right.astype(jnp.float32), precision=lax.Precision.HIGHEST)

def project(patch_obj, amplitude, probe, tables):
    along_x, along_y, inverse_y, inverse_x = tables
    modes = probe.shape[0]
    size = probe.shape[1]
    preal = probe[:, :, 0, :]
    pimag = probe[:, :, 1, :]
    oreal = patch_obj[:, 0, :]
    oimag = patch_obj[:, 1, :]
    wave = jnp.stack([preal * oreal - pimag * oimag, preal * oimag + pimag * oreal], axis=2).astype(jnp.bfloat16)
    first = matmul(wave.reshape(modes * size, 2 * size), along_x).astype(jnp.bfloat16)
    far = batched(along_y, first.reshape(modes, 2 * size, size)).reshape(modes, 2, size, size)
    modulus = jnp.maximum(jnp.sqrt(lax.optimization_barrier(jnp.sum(far * far, axis=(0, 1)))), 0.5)
    ratio = 1.0 - amplitude.astype(jnp.float32) / modulus
    error = (far * ratio).astype(jnp.bfloat16)
    back = batched(inverse_y, error.reshape(modes, 2 * size, size)).astype(jnp.bfloat16)
    exit_grad = matmul(back.reshape(modes * size, 2 * size), inverse_x).reshape(modes, size, 2, size)
    ureal = exit_grad[:, :, 0, :]
    uimag = exit_grad[:, :, 1, :]
    obj_grad = jnp.stack([lax.optimization_barrier(jnp.sum(preal * ureal + pimag * uimag, 0)), lax.optimization_barrier(jnp.sum(preal * uimag - pimag * ureal, 0))], axis=1)
    probe_term = jnp.stack([oreal * ureal + oimag * uimag, oreal * uimag - oimag * ureal], axis=2)
    return (obj_grad, probe_term)

def reference(object_tiles, probe, measured, offset_row, offset_col, subpixel, live_count):
    size = PATCH
    padded = jnp.concatenate([object_tiles, jnp.zeros((size, 2, OW), object_tiles.dtype)], axis=0)
    tables = dft_tables(size)
    start = (jnp.zeros((OH + size, 2, OW), jnp.float32), jnp.zeros(probe.shape, jnp.float32), jnp.zeros((2, NPOS), jnp.float32))

    def device_pass(device, carry):
        device = jnp.asarray(device).astype(jnp.int32)

        def slot_pass(slot, inner):
            grad, probe_acc, moved = inner
            index = device * SLOTS + jnp.asarray(slot).astype(jnp.int32)
            top = (device * ROWS_DEV + offset_row[index]).astype(jnp.int32)
            left = offset_col[index].astype(jnp.int32)
            corner = (top, jnp.int32(0), left)
            window = lax.dynamic_slice(padded, corner, (size + 1, 2, size + 1))
            code = subpixel[index]
            frac_y, frac_x = fractions(code)
            obj_grad, probe_term = project(interpolate(window, code), measured[index], probe, tables)
            region = lax.dynamic_slice(grad, corner, (size + 1, 2, size + 1))
            grad = lax.dynamic_update_slice(grad, region + spread(obj_grad, frac_y, frac_x), corner)
            slope_y, slope_x = slopes(window, obj_grad, frac_y, frac_x)
            moved = moved.at[:, index].set(jnp.stack([slope_y, slope_x]))
            return (grad, probe_acc + probe_term, moved)
        return lax.fori_loop(0, live_count[device], slot_pass, carry)
    grad, probe_acc, moved = lax.fori_loop(0, N_ROW, device_pass, start)
    return (grad[:OH], probe_acc, moved)
```

```python
import functools
import math

import jax
import jax.numpy as jnp
import ml_dtypes
import numpy as np
from jax import lax
from jax.experimental import pallas as pl
from jax.experimental.pallas import tpu as pltpu
from jax.sharding import PartitionSpec as P

F32 = jnp.float32
BF16 = jnp.bfloat16
LANES = 128
VMEM_BYTES = 56 * 2**20


def dft_tables(size):
    half = size // 2
    index = np.arange(size)
    angle = (index[:, None] * index[None, :] % size) * (2.0 * math.pi / size)
    scale = 1.0 / math.sqrt(size)
    cosine = (np.cos(angle) * scale).astype(ml_dtypes.bfloat16)
    sine = (np.sin(angle) * scale).astype(ml_dtypes.bfloat16)
    tables = []
    for parity in (0, 1):
        c, s = cosine[:half, parity::2], sine[:half, parity::2]
        tables.append(np.block([[c, -s], [s, c]]))
    order = np.zeros((size, size), ml_dtypes.bfloat16)
    order[2 * index[:half], index[:half]] = 1
    order[2 * index[:half] + 1, half + index[:half]] = 1
    even, odd = tables
    return tuple(jnp.asarray(t) for t in (even, odd, even.T.copy(), odd.T.copy(), order, order.T.copy()))


def dot(left, right):
    return jnp.dot(left, right, preferred_element_type=F32)


def fractions(code):
    return (code // 4).astype(F32) * 0.25, (code % 4).astype(F32) * 0.25


def project_kernel(
    slots, size, width, places, own, rim, probe, measured, even, odd, even_t, odd_t, order, order_t,
    grads, probe_acc, moved,
    cells, mixed, patch, folded, half_u, half_v, far, power, error, back, patch_grad, sems,
):
    half = size // 2
    modes = probe.shape[0]
    rows = own.shape[0]
    copies = [
        pltpu.make_async_copy(own, cells.at[pl.ds(0, rows)], sems.at[0]),
        pltpu.make_async_copy(rim, cells.at[pl.ds(rows, size)], sems.at[1]),
    ]
    for copy in copies:
        copy.start()
    probe_acc[...] = jnp.zeros_like(probe_acc)
    cells[rows + size :] = jnp.zeros((cells.shape[0] - rows - size, cells.shape[1]), BF16)
    for slot in range(slots):
        moved[0, slot] = 0.0
        moved[1, slot] = 0.0
    for copy in copies:
        copy.wait()
    span = mixed.shape[1]
    reach = size + LANES
    block = 32

    def one_slot(slot, _):
        top = places[0, slot]
        left = places[1, slot]
        frac_y, frac_x = fractions(places[2, slot])
        row0 = pl.multiple_of((top // 16) * 16, 16)
        col0 = pl.multiple_of((left // LANES) * LANES, LANES)
        down = top - row0
        across = left - col0
        source = lax.broadcasted_iota(jnp.int32, (reach, size), 0)
        target = lax.broadcasted_iota(jnp.int32, (reach, size), 1) + across
        here = (source == target).astype(F32)
        after = (source == target + 1).astype(F32)
        blend = jnp.concatenate([(1.0 - frac_x) * here + frac_x * after, after - here], axis=1).astype(BF16)
        source = lax.broadcasted_iota(jnp.int32, (span, size + 32), 1)
        target = lax.broadcasted_iota(jnp.int32, (span, size + 32), 0) + down
        lift = (source == target).astype(F32).astype(BF16)
        for part in range(2):
            start = pl.multiple_of(col0 + part * width, LANES)
            window = dot(lift, cells[pl.ds(row0, size + 32), pl.ds(start, reach)]).astype(BF16)
            mixed[part] = dot(window, blend)
        for part in range(2):
            for b in range(0, size, block):
                upper = mixed[part, pl.ds(b, block), :size]
                lower = mixed[part, pl.ds(b + 1, block), :size]
                patch[pl.ds(b, block), part * size : (part + 1) * size] = (1.0 - frac_y) * upper + frac_y * lower

        power[...] = jnp.zeros_like(power)

        def forward(mode, _):
            for b in range(0, size, block):
                at = pl.ds(b, block)
                preal, pimag = probe[mode, at, :size], probe[mode, at, size:]
                oreal, oimag = patch[at, :size], patch[at, size:]
                wreal = preal * oreal - pimag * oimag
                wimag = preal * oimag + pimag * oreal
                for part, wave in enumerate((wreal, wimag)):
                    folded[at, part * half : (part + 1) * half] = (wave[:, :half] + wave[:, half:]).astype(BF16)
                    folded[at, size + part * half : size + (part + 1) * half] = (wave[:, :half] - wave[:, half:]).astype(BF16)
            step = 64
            for b in range(0, half, step):
                for k, table in enumerate((even, odd)):
                    upper = dot(folded[b : b + step, k * size : (k + 1) * size], table[...])
                    lower = dot(folded[half + b : half + b + step, k * size : (k + 1) * size], table[...])
                    plus, minus = (upper + lower).astype(BF16), (upper - lower).astype(BF16)
                    for part in range(2):
                        to = slice(part * half + b, part * half + b + step)
                        cols = slice(part * half, (part + 1) * half)
                        half_u[to, k * half : (k + 1) * half] = plus[:, cols]
                        half_v[to, k * half : (k + 1) * half] = minus[:, cols]
            for k, (table, data) in enumerate(((even_t, half_u), (odd_t, half_v))):
                for c in range(0, size, half):
                    out = dot(table[...], data[:, c : c + half])
                    far[mode, k, :, c : c + half] = out
                    power[k * half : (k + 1) * half, c : c + half] += out[:half] * out[:half] + out[half:] * out[half:]
            return 0

        lax.fori_loop(0, modes, forward, 0)

        amplitude = dot(dot(order_t[...], measured[slot]).astype(BF16), order[...])
        power[...] = 1.0 - amplitude / jnp.maximum(jnp.sqrt(power[...]), 0.5)
        patch_grad[...] = jnp.zeros_like(patch_grad)

        def backward(mode, _):
            for k in range(2):
                for b in range(0, half, block):
                    ratio = power[k * half + b : k * half + b + block, :]
                    for part in range(2):
                        at = slice(part * half + b, part * half + b + block)
                        error[k, at, :] = (far[mode, k, at, :] * ratio).astype(BF16)
            for c in range(2):
                cols = slice(c * half, (c + 1) * half)
                first = dot(even[...], error[0, :, cols])
                second = dot(odd[...], error[1, :, cols])
                plus, minus = (first + second).astype(BF16), (first - second).astype(BF16)
                for part in range(2):
                    to = slice(c * size + part * half, c * size + (part + 1) * half)
                    back[:half, to] = plus[part * half : (part + 1) * half]
                    back[half:, to] = minus[part * half : (part + 1) * half]
            for b in range(0, size, block):
                at = pl.ds(b, block)
                first = dot(back[at, :size], even_t[...])
                second = dot(back[at, size:], odd_t[...])
                plus, minus = first + second, first - second
                for h, piece in enumerate((plus, minus)):
                    ureal, uimag = piece[:, :half], piece[:, half:]
                    re = slice(h * half, (h + 1) * half)
                    im = slice(size + h * half, size + (h + 1) * half)
                    preal, pimag = probe[mode, at, re], probe[mode, at, im]
                    oreal, oimag = patch[at, re], patch[at, im]
                    patch_grad[at, re] += preal * ureal + pimag * uimag
                    patch_grad[at, im] += preal * uimag - pimag * ureal
                    probe_acc[mode, at, re] += oreal * ureal + oimag * uimag
                    probe_acc[mode, at, im] += oreal * uimag - oimag * ureal
            return 0

        lax.fori_loop(0, modes, backward, 0)
        grads[slot] = patch_grad[...].astype(BF16)
        total_y = jnp.zeros((block, size), F32)
        total_x = jnp.zeros((block, size), F32)
        for part in range(2):
            for b in range(0, size, block):
                upper = mixed[part, pl.ds(b, block), :]
                lower = mixed[part, pl.ds(b + 1, block), :]
                grad = patch_grad[pl.ds(b, block), part * size : (part + 1) * size]
                total_y += grad * (lower[:, :size] - upper[:, :size])
                total_x += grad * ((1.0 - frac_y) * upper[:, size:] + frac_y * lower[:, size:])
        moved[0, slot] = jnp.sum(total_y) / size
        moved[1, slot] = jnp.sum(total_x) / size
        return 0

    lax.fori_loop(0, places[3, 0], one_slot, 0)


def project(places, own, rim, probe, measured, tables, width):
    slots, size, _ = measured.shape
    modes = probe.shape[0]
    span = size + 16
    reach = size + LANES
    vmem = pl.BlockSpec(memory_space=pltpu.VMEM)
    smem = pl.BlockSpec(memory_space=pltpu.SMEM)
    hbm = pl.BlockSpec(memory_space=pl.ANY)
    return pl.pallas_call(
        functools.partial(project_kernel, slots, size, width),
        in_specs=[smem, hbm, hbm] + [vmem] * 8,
        out_specs=[vmem, vmem, smem],
        out_shape=[
            jax.ShapeDtypeStruct((slots, size, 2 * size), BF16),
            jax.ShapeDtypeStruct(probe.shape, F32),
            jax.ShapeDtypeStruct((2, slots), F32),
        ],
        scratch_shapes=[
            pltpu.VMEM((own.shape[0] + size + 32, 2 * width), BF16),
            pltpu.VMEM((2, span, 2 * size), F32),
            pltpu.VMEM((size, 2 * size), F32),
            pltpu.VMEM((size, 2 * size), BF16),
            pltpu.VMEM((size, size), BF16),
            pltpu.VMEM((size, size), BF16),
            pltpu.VMEM((modes, 2, size, size), F32),
            pltpu.VMEM((size, size), F32),
            pltpu.VMEM((2, size, size), BF16),
            pltpu.VMEM((size, 2 * size), BF16),
            pltpu.VMEM((size, 2 * size), F32),
            pltpu.SemaphoreType.DMA((2,)),
        ],
        compiler_params=pltpu.CompilerParams(vmem_limit_bytes=VMEM_BYTES),
        name="project",
    )(places, own, rim, probe, measured, *tables)


def settle_kernel(size, width, places, grads, own, below, total):
    rows = own.shape[0]
    total[...] = jnp.zeros_like(total)
    reach = size + LANES
    span = size + 16

    def one_slot(slot, _):
        top = places[0, slot]
        left = places[1, slot]
        frac_y, frac_x = fractions(places[2, slot])
        row0 = pl.multiple_of((top // 8) * 8, 8)
        col0 = pl.multiple_of((left // LANES) * LANES, LANES)
        source = lax.broadcasted_iota(jnp.int32, (size, reach), 0) + (left - col0)
        target = lax.broadcasted_iota(jnp.int32, (size, reach), 1)
        along = jnp.where(source == target, 1.0 - frac_x, 0.0) + jnp.where(source + 1 == target, frac_x, 0.0)
        source = lax.broadcasted_iota(jnp.int32, (span, size), 1) + (top - row0)
        target = lax.broadcasted_iota(jnp.int32, (span, size), 0)
        down = jnp.where(source == target, 1.0 - frac_y, 0.0) + jnp.where(source + 1 == target, frac_y, 0.0)
        for part in range(2):
            wide = dot(grads[slot, :, part * size : (part + 1) * size], along.astype(BF16)).astype(BF16)
            start = pl.multiple_of(col0 + part * width, LANES)
            total[pl.ds(row0, span), pl.ds(start, reach)] += dot(down.astype(BF16), wide)
        return 0

    lax.fori_loop(0, places[3, 0], one_slot, 0)
    own[...] = total[:rows]
    below[...] = total[rows : rows + size].astype(BF16)


def settle(places, grads, rows, width):
    _, size, _ = grads.shape
    vmem = pl.BlockSpec(memory_space=pltpu.VMEM)
    smem = pl.BlockSpec(memory_space=pltpu.SMEM)
    return pl.pallas_call(
        functools.partial(settle_kernel, size, width),
        in_specs=[smem, vmem],
        out_specs=[vmem, vmem],
        out_shape=[
            jax.ShapeDtypeStruct((rows, 2 * width), F32),
            jax.ShapeDtypeStruct((size, 2 * width), BF16),
        ],
        scratch_shapes=[pltpu.VMEM((rows + size + 16, 2 * width), F32)],
        compiler_params=pltpu.CompilerParams(vmem_limit_bytes=VMEM_BYTES),
        name="settle",
    )(places, grads)


def passed_along(x, axis, by):
    length = lax.axis_size(axis)
    pairs = [(i, i + by) for i in range(length) if 0 <= i + by < length]
    return lax.ppermute(x, axis, pairs)


def summed(x, axis):
    length = lax.axis_size(axis)
    chips = length // 2
    me = lax.axis_index(axis)
    chip, core = me // 2, me % 2
    across = [(i, i ^ 1) for i in range(length)]
    x = x.reshape((2, x.shape[0] // 2) + x.shape[1:])
    mine = lax.dynamic_index_in_dim(x, core, 0, False)
    given = lax.dynamic_index_in_dim(x, 1 - core, 0, False).astype(BF16)
    mine = mine + lax.ppermute(given, axis, across).astype(F32)
    parts = mine.astype(BF16).reshape((chips, mine.shape[0] // chips) + mine.shape[1:])

    def ring(shift):
        return [(i, (i + 2 * shift) % length) for i in range(length)]

    got = [
        lax.ppermute(lax.dynamic_index_in_dim(parts, (chip + s) % chips, 0, False), axis, ring(s)) for s in range(1, chips)
    ]
    total = lax.dynamic_index_in_dim(mine.reshape(parts.shape), chip, 0, False)
    for piece in got:
        total = total + piece.astype(F32)
    total = total.astype(BF16)
    held = [total] + [lax.ppermute(total, axis, ring(s)) for s in range(1, chips)]
    whole = jnp.concatenate(held[::-1], axis=0)
    whole = jnp.concatenate([whole, whole], axis=0)
    size = total.shape[0]
    whole = lax.dynamic_slice_in_dim(whole, (chips - 1 - chip) * size, chips * size, 0)
    other = lax.ppermute(whole, axis, across)
    first = jnp.where(core == 0, whole, other)
    second = jnp.where(core == 0, other, whole)
    return jnp.concatenate([first, second], axis=0).astype(F32)


def shards(object_tiles, probe, measured, offset_row, offset_col, subpixel, live_count):
    rows, _, width = object_tiles.shape
    modes, size = probe.shape[:2]
    tables = dft_tables(size)
    rim = passed_along(object_tiles[:size], "row", -1)
    places = jnp.stack([offset_row, offset_col, subpixel, jnp.broadcast_to(live_count, offset_row.shape)])
    probe_flat = probe.reshape(modes, size, 2 * size)
    grads, probe_acc, moved = project(
        places, object_tiles.reshape(rows, 2 * width), rim.reshape(size, 2 * width), probe_flat, measured, tables, width
    )
    own, below = settle(places, grads, rows, width)
    below = passed_along(below, "row", 1)
    probe_grad = summed(probe_acc.reshape(modes * size, 2 * size), "row").reshape(probe.shape)
    object_grad = own.at[:size].add(below.astype(F32)).reshape(rows, 2, width)
    return object_grad, probe_grad, moved


def solution(mesh):
    in_specs = (
        P(("groups", "row"), None, None),
        P(),
        P(("groups", "row"), None, None),
        P(("groups", "row")),
        P(("groups", "row")),
        P(("groups", "row")),
        P(("groups", "row")),
    )
    out_specs = (
        P(("groups", "row"), None, None),
        P("groups", None, None, None),
        P(None, ("groups", "row")),
    )
    return jax.shard_map(shards, mesh=mesh, in_specs=in_specs, out_specs=out_specs, check_vma=False)
```

```python
import functools
import math

import jax
import jax.numpy as jnp
import ml_dtypes
import numpy as np
from jax import lax
from jax.experimental import pallas as pl
from jax.experimental.pallas import tpu as pltpu
from jax.sharding import PartitionSpec as P

F32 = jnp.float32
BF16 = jnp.bfloat16
LANES = 128
VMEM_BYTES = 56 * 2**20


def dft_tables(size):
    half = size // 2
    index = np.arange(size)
    angle = (index[:, None] * index[None, :] % size) * (2.0 * math.pi / size)
    scale = 1.0 / math.sqrt(size)
    cosine = (np.cos(angle) * scale).astype(ml_dtypes.bfloat16)
    sine = (np.sin(angle) * scale).astype(ml_dtypes.bfloat16)
    tables = []
    for parity in (0, 1):
        c, s = cosine[:half, parity::2], sine[:half, parity::2]
        tables.append(np.block([[c, -s], [s, c]]))
    order = np.zeros((size, size), ml_dtypes.bfloat16)
    order[2 * index[:half], index[:half]] = 1
    order[2 * index[:half] + 1, half + index[:half]] = 1
    even, odd = tables
    return tuple(jnp.asarray(t) for t in (even, odd, even.T.copy(), odd.T.copy(), order, order.T.copy()))


def dot(left, right):
    return jnp.dot(left, right, preferred_element_type=F32)


def fractions(code):
    return (code // 4).astype(F32) * 0.25, (code % 4).astype(F32) * 0.25


def project_kernel(size, width, bounds, stage, places, *refs):
    first_stage, last_stage = stage == 0, stage == len(bounds) - 2
    refs = list(refs)
    own, rim = refs.pop(0), refs.pop(0)
    rim_before = None if first_stage else refs.pop(0)
    probe_in, measured_in = refs.pop(0), refs.pop(0)
    even, odd, even_t, odd_t, order, order_t = refs[:6]
    refs = refs[6:]
    if not first_stage:
        sums_in, _, moved_in = refs[:3]
        refs = refs[3:]
    grads, moved = refs[:2]
    refs = refs[2:]
    if last_stage:
        keep, give = refs[:2]
        refs = refs[2:]
    else:
        sums_out = refs.pop(0)
    cells, mixed, patch, folded, half_u, half_v, far, error, back, probe, measured, probe_acc, held, sems, slot_sems = refs
    if last_stage:
        probe_acc, given = probe_acc
    half = size // 2
    modes = probe.shape[0]
    slots = measured.shape[0]
    rows = own.shape[0]
    low, high = bounds[stage], bounds[stage + 1]
    base = 0 if first_stage else low - size
    extent = high - base
    count = places[3, 0]
    copies = []

    def load(source, target):
        copies.append(pltpu.make_async_copy(source, target, sems.at[len(copies)]))

    for part in range(2):
        load(
            own.at[:, pl.ds(part * width + base, extent)],
            cells.at[pl.ds(0, rows), pl.ds(part * extent, extent)],
        )
        load(
            rim.at[:, pl.ds(part * (high - low), high - low)],
            cells.at[pl.ds(rows, size), pl.ds(part * extent + low - base, high - low)],
        )
        if not first_stage:
            before = low - bounds[stage - 1]
            load(
                rim_before.at[:, pl.ds((part + 1) * before - size, size)],
                cells.at[pl.ds(rows, size), pl.ds(part * extent, size)],
            )
    n_cells = len(copies)
    load(probe_in, probe)
    load(measured_in, measured)
    if not first_stage:
        load(sums_in, probe_acc)
    for copy in copies:
        copy.start()
    if first_stage:
        probe_acc[...] = jnp.zeros_like(probe_acc)
    cells[rows + size :] = jnp.zeros((cells.shape[0] - rows - size, cells.shape[1]), BF16)
    for slot in range(slots):
        for axis in range(2):
            moved[axis, slot] = 0.0 if first_stage else moved_in[axis, slot]
    for copy in copies:
        copy.wait()

    def sent_out(slot):
        return pltpu.make_async_copy(held.at[slot], grads.at[slot], slot_sems.at[slot])

    block = 16
    blocks = size // block
    lift_rows = half + 8
    lift_from = half + 32

    def one_slot(slot):
        top = places[0, slot]
        left = places[1, slot]
        frac_y, frac_x = fractions(places[2, slot])
        row0 = pl.multiple_of((top // 16) * 16, 16)
        col0 = pl.multiple_of((left // LANES) * LANES - base, LANES)
        down = top - row0
        across = left - base - col0
        source = lax.broadcasted_iota(jnp.int32, (2 * LANES, LANES), 0)
        target = lax.broadcasted_iota(jnp.int32, (2 * LANES, LANES), 1) + across
        here = (source == target).astype(F32)
        after = (source == target + 1).astype(F32)
        blend = jnp.concatenate([(1.0 - frac_x) * here + frac_x * after, after - here], axis=1).astype(BF16)
        source = lax.broadcasted_iota(jnp.int32, (lift_rows, lift_from), 1)
        target = lax.broadcasted_iota(jnp.int32, (lift_rows, lift_from), 0) + down
        lifts = [(source == target + shift).astype(F32).astype(BF16) for shift in (0, 8)]
        for part in range(2):
            start = pl.multiple_of(col0 + part * extent, LANES)
            for piece in range(2):
                taken = pl.ds(pl.multiple_of(row0 + piece * half, 16), lift_from)
                window = dot(lifts[piece], cells[taken, pl.ds(start, size + LANES)]).astype(BF16)
                for h in range(size // LANES):
                    mixed[part, pl.ds(piece * lift_rows, lift_rows), h * size : (h + 1) * size] = dot(
                        window[:, h * LANES : (h + 2) * LANES], blend
                    )
        for part in range(2):
            for h in range(size // LANES):
                cols = slice(h * size, h * size + LANES)
                for b in range(0, size, block):
                    upper = mixed[part, pl.ds(b, block), cols]
                    lower = mixed[part, pl.ds(b + 1, block), cols]
                    to = slice(part * size + h * LANES, part * size + (h + 1) * LANES)
                    patch[pl.ds(b, block), to] = (1.0 - frac_y) * upper + frac_y * lower

        for mode in range(modes):
            for b in range(blocks):
                at = slice(b * block, (b + 1) * block)
                spot = (2 * b if b < blocks // 2 else 2 * b + 1 - blocks) * block
                to = slice(spot, spot + block)
                preal, pimag = probe[mode, at, :size], probe[mode, at, size:]
                oreal, oimag = patch[at, :size], patch[at, size:]
                wreal = preal * oreal - pimag * oimag
                wimag = preal * oimag + pimag * oreal
                for part, wave in enumerate((wreal, wimag)):
                    folded[mode, to, part * half : (part + 1) * half] = (wave[:, :half] + wave[:, half:]).astype(BF16)
                    folded[mode, to, size + part * half : size + (part + 1) * half] = (
                        wave[:, :half] - wave[:, half:]
                    ).astype(BF16)
            for k, table in enumerate((even, odd)):
                out = dot(folded[mode, :, k * size : (k + 1) * size], table[...])
                for b in range(blocks // 2):
                    upper = out[2 * b * block : (2 * b + 1) * block]
                    lower = out[(2 * b + 1) * block : (2 * b + 2) * block]
                    plus, minus = (upper + lower).astype(BF16), (upper - lower).astype(BF16)
                    for part in range(2):
                        to = slice(part * half + b * block, part * half + (b + 1) * block)
                        cols = slice(part * half, (part + 1) * half)
                        half_u[mode, to, k * half : (k + 1) * half] = plus[:, cols]
                        half_v[mode, to, k * half : (k + 1) * half] = minus[:, cols]
            far[mode, 0] = dot(even_t[...], half_u[mode])
            far[mode, 1] = dot(odd_t[...], half_v[mode])

        amplitude = dot(dot(order_t[...], measured[slot]).astype(BF16), order[...])
        for k in range(2):
            for b in range(0, half, block):
                pieces = [
                    [far[mode, k, part * half + b : part * half + b + block, :] for part in range(2)]
                    for mode in range(modes)
                ]
                power = sum(p * p for pair in pieces for p in pair)
                level = amplitude[k * half + b : k * half + b + block]
                ratio = 1.0 - level / jnp.maximum(jnp.sqrt(power), 0.5)
                for mode in range(modes):
                    for part in range(2):
                        to = slice(part * half + b, part * half + b + block)
                        error[mode, k, to, :] = (pieces[mode][part] * ratio).astype(BF16)

        for mode in range(modes):
            first = dot(even[...], error[mode, 0])
            second = dot(odd[...], error[mode, 1])
            plus, minus = (first + second).astype(BF16), (first - second).astype(BF16)
            for part in range(2):
                for b in range(blocks):
                    pick = part * half + (b % (blocks // 2)) * block
                    piece = (plus if b < blocks // 2 else minus)[pick : pick + block]
                    to = slice((b * modes + mode) * block, (b * modes + mode + 1) * block)
                    for c in range(2):
                        cols = slice(c * size + part * half, c * size + (part + 1) * half)
                        back[to, cols] = piece[:, c * half : (c + 1) * half]

        total_y = jnp.zeros((block, half), F32)
        total_x = jnp.zeros((block, half), F32)
        group = size // (modes * block)
        for g in range(blocks // group):
            span = slice(g * size, (g + 1) * size)
            first = dot(back[span, :size], even_t[...])
            second = dot(back[span, size:], odd_t[...])
            for r in range(group):
                at = slice((g * group + r) * block, (g * group + r + 1) * block)
                below = slice(at.start + 1, at.stop + 1)
                for h in range(2):
                    re = slice(h * half, (h + 1) * half)
                    im = slice(size + h * half, size + (h + 1) * half)
                    oreal, oimag = patch[at, re], patch[at, im]
                    greal = jnp.zeros((block, half), F32)
                    gimag = jnp.zeros((block, half), F32)
                    for mode in range(modes):
                        part = slice((r * modes + mode) * block, (r * modes + mode + 1) * block)
                        piece = first[part] + second[part] if h == 0 else first[part] - second[part]
                        ureal, uimag = piece[:, :half], piece[:, half:]
                        preal, pimag = probe[mode, at, re], probe[mode, at, im]
                        greal += preal * ureal + pimag * uimag
                        gimag += preal * uimag - pimag * ureal
                        probe_acc[mode, at, re] += oreal * ureal + oimag * uimag
                        probe_acc[mode, at, im] += oreal * uimag - oimag * ureal
                    held[slot, at, re] = greal.astype(BF16)
                    held[slot, at, im] = gimag.astype(BF16)
                    for part, grad in enumerate((greal, gimag)):
                        cols = slice(h * size, h * size + LANES)
                        total_y += grad * (mixed[part, below, cols] - mixed[part, at, cols])
                        cols = slice(h * size + LANES, (h + 1) * size)
                        total_x += grad * ((1.0 - frac_y) * mixed[part, at, cols] + frac_y * mixed[part, below, cols])
        moved[0, slot] = jnp.sum(total_y) / size
        moved[1, slot] = jnp.sum(total_x) / size
        sent_out(slot).start()


    def mine(slot):
        end = places[1, slot] + size + 1
        return jnp.logical_and(slot < count, jnp.logical_and(end > low if not first_stage else True, end <= high))

    @pl.loop(0, slots)
    def _(slot):
        pl.when(mine(slot))(functools.partial(one_slot, slot))

    if last_stage:
        core = places[4, 0]
        share = modes // 2
        given[...] = probe_acc[pl.ds((1 - core) * share, share)].astype(BF16)
        outs = [
            pltpu.make_async_copy(probe_acc.at[pl.ds(core * share, share)], keep, sems.at[0]),
            pltpu.make_async_copy(given, give, sems.at[1]),
        ]
    else:
        outs = [pltpu.make_async_copy(probe_acc, sums_out, sems.at[0])]
    for out in outs:
        out.start()

    @pl.loop(0, slots)
    def _(slot):
        @pl.when(mine(slot))
        def _():
            sent_out(slot).wait()

    for out in outs:
        out.wait()


def project(stage, bounds, places, own, rims, probe, measured, tables, width, carried):
    slots, size, _ = measured.shape
    modes = probe.shape[0]
    vmem = pl.BlockSpec(memory_space=pltpu.VMEM)
    smem = pl.BlockSpec(memory_space=pltpu.SMEM)
    hbm = pl.BlockSpec(memory_space=pl.ANY)
    first_stage, last_stage = stage == 0, stage == len(bounds) - 2
    low, high = bounds[stage], bounds[stage + 1]
    extent = high - (0 if first_stage else low - size)
    inputs = [places, own, rims[stage]] + ([] if first_stage else [rims[stage - 1]]) + [probe, measured, *tables]
    specs = [smem] + [hbm] * (len(inputs) - 1 - len(tables)) + [vmem] * len(tables)
    outs = [jax.ShapeDtypeStruct((slots, size, 2 * size), BF16), jax.ShapeDtypeStruct((2, slots), F32)]
    out_specs = [hbm, smem]
    aliases = {}
    if not first_stage:
        grads, moved, sums = carried
        aliases = {len(inputs) + 1: 0}
        if not last_stage:
            aliases[len(inputs)] = 2
        inputs += [sums, grads, moved]
        specs += [hbm, hbm, smem]
    if last_stage:
        share = (modes // 2,) + probe.shape[1:]
        outs += [jax.ShapeDtypeStruct(share, F32), jax.ShapeDtypeStruct(share, BF16)]
        out_specs += [hbm, hbm]
        sums_scratch = (pltpu.VMEM(probe.shape, F32), pltpu.VMEM(share, BF16))
    else:
        outs += [jax.ShapeDtypeStruct(probe.shape, F32)]
        out_specs += [hbm]
        sums_scratch = pltpu.VMEM(probe.shape, F32)
    return pl.pallas_call(
        functools.partial(project_kernel, size, width, bounds, stage),
        in_specs=specs,
        out_specs=out_specs,
        out_shape=outs,
        input_output_aliases=aliases,
        scratch_shapes=[
            pltpu.VMEM((own.shape[0] + size + 32, 2 * extent), BF16),
            pltpu.VMEM((2, size + 16, 2 * size), F32),
            pltpu.VMEM((size, 2 * size), F32),
            pltpu.VMEM((modes, size, 2 * size), BF16),
            pltpu.VMEM((modes, size, size), BF16),
            pltpu.VMEM((modes, size, size), BF16),
            pltpu.VMEM((modes, 2, size, size), F32),
            pltpu.VMEM((modes, 2, size, size), BF16),
            pltpu.VMEM((modes * size, 2 * size), BF16),
            pltpu.VMEM(probe.shape, F32),
            pltpu.VMEM(measured.shape, BF16),
            sums_scratch,
            pltpu.VMEM((slots, size, 2 * size), BF16),
            pltpu.SemaphoreType.DMA((9,)),
            pltpu.SemaphoreType.DMA((slots,)),
        ],
        compiler_params=pltpu.CompilerParams(vmem_limit_bytes=VMEM_BYTES),
        cost_estimate=pl.CostEstimate(flops=4 * 10**9, bytes_accessed=12 * 2**20, transcendentals=0),
        name=f"project_{stage}",
    )(*inputs)


def spread_wide(size, places, slot, grads, part):
    reach = size + LANES
    left = places[1, slot]
    _, frac_x = fractions(places[2, slot])
    source = lax.broadcasted_iota(jnp.int32, (size, reach), 0) + left % LANES
    target = lax.broadcasted_iota(jnp.int32, (size, reach), 1)
    along = jnp.where(source == target, 1.0 - frac_x, 0.0) + jnp.where(source + 1 == target, frac_x, 0.0)
    return dot(grads[slot, :, part * size : (part + 1) * size], along.astype(BF16)).astype(BF16)


def spread_down(size, places, slot, shift):
    frac_y, _ = fractions(places[2, slot])
    source = lax.broadcasted_iota(jnp.int32, (size, size), 1) + (places[0, slot] - shift)
    target = lax.broadcasted_iota(jnp.int32, (size, size), 0)
    down = jnp.where(source == target, 1.0 - frac_y, 0.0) + jnp.where(source + 1 == target, frac_y, 0.0)
    return down.astype(BF16)


def add_slots(size, width, places, grads, total, shift):
    reach = size + LANES

    def one_slot(slot, _):
        down = spread_down(size, places, slot, shift)
        col0 = (places[1, slot] // LANES) * LANES
        for part in range(2):
            start = pl.multiple_of(col0 + part * width, LANES)
            total[:, pl.ds(start, reach)] += dot(down, spread_wide(size, places, slot, grads, part))
        return 0

    lax.fori_loop(0, places[3, 0], one_slot, 0)


def below_kernel(size, width, places, grads, below, total):
    total[...] = jnp.zeros_like(total)
    add_slots(size, width, places, grads, total, size)
    below[...] = total[...].astype(BF16)


def below_rows(places, grads, width):
    _, size, _ = grads.shape
    vmem = pl.BlockSpec(memory_space=pltpu.VMEM)
    smem = pl.BlockSpec(memory_space=pltpu.SMEM)
    return pl.pallas_call(
        functools.partial(below_kernel, size, width),
        in_specs=[smem, vmem],
        out_specs=vmem,
        out_shape=jax.ShapeDtypeStruct((size, 2 * width), BF16),
        scratch_shapes=[pltpu.VMEM((size, 2 * width), F32)],
        compiler_params=pltpu.CompilerParams(vmem_limit_bytes=VMEM_BYTES),
        cost_estimate=pl.CostEstimate(flops=10**9, bytes_accessed=8 * 2**20, transcendentals=0),
        name="below_rows",
    )(places, grads)


def own_kernel(size, width, places, grads, above, out, total, sems):
    total[...] = above[...].astype(F32)
    add_slots(size, width, places, grads, total, 0)
    copies = [
        pltpu.make_async_copy(total.at[:, pl.ds(part * width, width)], out.at[:, part, :], sems.at[part]) for part in range(2)
    ]
    for copy in copies:
        copy.start()
    for copy in copies:
        copy.wait()


def own_rows(places, grads, above, width):
    _, size, _ = grads.shape
    vmem = pl.BlockSpec(memory_space=pltpu.VMEM)
    smem = pl.BlockSpec(memory_space=pltpu.SMEM)
    return pl.pallas_call(
        functools.partial(own_kernel, size, width),
        in_specs=[smem, vmem, vmem],
        out_specs=pl.BlockSpec(memory_space=pl.ANY),
        out_shape=jax.ShapeDtypeStruct((above.shape[0], 2, width), F32),
        scratch_shapes=[pltpu.VMEM(above.shape, F32), pltpu.SemaphoreType.DMA((2,))],
        compiler_params=pltpu.CompilerParams(vmem_limit_bytes=VMEM_BYTES),
        cost_estimate=pl.CostEstimate(flops=10**9, bytes_accessed=8 * 2**20, transcendentals=0),
        name="own_rows",
    )(places, grads, above)


def passed_along(x, axis, by):
    length = lax.axis_size(axis)
    pairs = [(i, i + by) for i in range(length) if 0 <= i + by < length]
    return lax.ppermute(x, axis, pairs)


def unpack_kernel(order, *refs):
    pieces, out, wide, sems = refs[:-3], refs[-3], refs[-2], refs[-1]
    rows = pieces[0].shape[0]
    modes, size, _, _ = out.shape
    copies = []
    for i, piece in enumerate(pieces):
        wide[i * rows : (i + 1) * rows] = piece[...].astype(F32)
        mode = order[i] // (size // rows)
        at = pl.multiple_of(order[i] % (size // rows) * rows, 8)
        for part in range(2):
            copy = pltpu.make_async_copy(
                wide.at[pl.ds(i * rows, rows), pl.ds(part * size, size)],
                out.at[mode, pl.ds(at, rows), part, :],
                sems.at[2 * i + part],
            )
            copy.start()
            copies.append(copy)
    for copy in copies:
        copy.wait()


def unpacked(pieces, order, shape):
    vmem = pl.BlockSpec(memory_space=pltpu.VMEM)
    smem = pl.BlockSpec(memory_space=pltpu.SMEM)
    return pl.pallas_call(
        unpack_kernel,
        in_specs=[smem] + [vmem] * len(pieces),
        out_specs=pl.BlockSpec(memory_space=pl.ANY),
        out_shape=jax.ShapeDtypeStruct(shape, F32),
        scratch_shapes=[
            pltpu.VMEM((len(pieces) * pieces[0].shape[0], pieces[0].shape[1]), F32),
            pltpu.SemaphoreType.DMA((2 * len(pieces),)),
        ],
        compiler_params=pltpu.CompilerParams(vmem_limit_bytes=VMEM_BYTES),
        name="unpack",
    )(order, *pieces)


def summed(keep, give, axis, shape):
    length = lax.axis_size(axis)
    chips = length // 2
    near = min(4, chips)
    far = chips // near
    me = lax.axis_index(axis)
    core, chip = me % 2, me // 2
    across = [(i, i ^ 1) for i in range(length)]

    def hop(shift, stride):
        return [(i, i ^ (2 * stride * shift)) for i in range(length)]

    size, columns = keep.shape[1:]
    mine = keep + lax.ppermute(give, axis, across).astype(F32)
    rows = mine.shape[0] * size // near
    mine = mine.reshape(near, rows, columns)
    parts = mine.astype(BF16)
    spot = chip % near
    got = [
        lax.ppermute(lax.dynamic_index_in_dim(parts, spot ^ s, 0, False), axis, hop(s, 1)) for s in range(1, near)
    ]
    total = lax.dynamic_index_in_dim(mine, spot, 0, False)
    for piece in got:
        total = total + piece.astype(F32)
    sent = total.astype(BF16)
    for s in range(1, far):
        total = total + lax.ppermute(sent, axis, hop(s, near)).astype(F32)
    total = total.astype(BF16)
    pieces = [total] + [lax.ppermute(total, axis, hop(s, 1)) for s in range(1, near)]
    others = [lax.ppermute(piece, axis, across) for piece in pieces]
    order = [core * near + (spot ^ s) for s in range(near)] + [(1 - core) * near + (spot ^ s) for s in range(near)]
    return unpacked(pieces + others, jnp.stack(order), shape)


def column_bounds(width, size):
    cuts = [0] + [round(width * share / LANES) * LANES for share in (0.375, 0.625, 0.8125)] + [width]
    return tuple(cuts)


def shards(object_tiles, probe, measured, offset_row, offset_col, subpixel, live_count):
    rows, _, width = object_tiles.shape
    modes, size = probe.shape[:2]
    tables = dft_tables(size)
    bounds = column_bounds(width, size)
    rims = [
        passed_along(object_tiles[:size, :, low:high].reshape(size, 2 * (high - low)), "row", -1)
        for low, high in zip(bounds[:-1], bounds[1:])
    ]
    core = lax.axis_index("row") % 2
    places = jnp.stack(
        [offset_row, offset_col, subpixel] + [jnp.broadcast_to(x, offset_row.shape) for x in (live_count, core)]
    )
    own = object_tiles.reshape(rows, 2 * width)
    flat = probe.reshape(modes, size, 2 * size)
    carried = None
    for stage in range(len(bounds) - 1):
        carried = project(stage, bounds, places, own, rims, flat, measured, tables, width, carried)
    grads, moved, keep, give = carried
    above = passed_along(below_rows(places, grads, width), "row", 1)
    probe_grad = summed(keep, give, "row", probe.shape)
    object_grad = own_rows(places, grads, above, width)
    return object_grad, probe_grad, moved


def solution(mesh):
    in_specs = (
        P(("groups", "row"), None, None),
        P(),
        P(("groups", "row"), None, None),
        P(("groups", "row")),
        P(("groups", "row")),
        P(("groups", "row")),
        P(("groups", "row")),
    )
    out_specs = (
        P(("groups", "row"), None, None),
        P("groups", None, None, None),
        P(None, ("groups", "row")),
    )
    return jax.shard_map(shards, mesh=mesh, in_specs=in_specs, out_specs=out_specs, check_vma=False)
```

```python
import functools
import math

import jax
import jax.numpy as jnp
import ml_dtypes
import numpy as np
from jax import lax
from jax.experimental import pallas as pl
from jax.experimental.pallas import tpu as pltpu
from jax.sharding import PartitionSpec as P

F32 = jnp.float32
BF16 = jnp.bfloat16
LANES = 128
VMEM_BYTES = 56 * 2**20


def dft_tables(size):
    half = size // 2
    index = np.arange(size)
    angle = (index[:, None] * index[None, :] % size) * (2.0 * math.pi / size)
    scale = 1.0 / math.sqrt(size)
    cosine = (np.cos(angle) * scale).astype(ml_dtypes.bfloat16)
    sine = (np.sin(angle) * scale).astype(ml_dtypes.bfloat16)
    tables = []
    for parity in (0, 1):
        c, s = cosine[:half, parity::2], sine[:half, parity::2]
        tables.append(np.block([[c, -s], [s, c]]))
    order = np.zeros((size, size), ml_dtypes.bfloat16)
    order[2 * index[:half], index[:half]] = 1
    order[2 * index[:half] + 1, half + index[:half]] = 1
    even, odd = tables
    return jnp.asarray(np.stack([even, odd, even.T, odd.T, order, order.T]))


def dot(left, right):
    return jnp.dot(left, right, preferred_element_type=F32)


def fractions(code):
    return (code // 4).astype(F32) * 0.25, (code % 4).astype(F32) * 0.25


def project_kernel(size, width, bounds, stage, places, *refs):
    first_stage, last_stage = stage == 0, stage == len(bounds) - 2
    refs = list(refs)
    own, rim = refs[:2]
    rim_before = None if first_stage else refs[2]
    refs = refs[2:] if first_stage else refs[3:]
    probe_in, measured_in, tables_in = refs[:3]
    refs = refs[3:]
    if not first_stage:
        moved_in, sums_in, border_in = refs[:3]
        refs = refs[3:]
    moved, own_part, below = refs[:3]
    refs = refs[3:]
    if last_stage:
        keep, give = refs[:2]
    else:
        sums_out, border_out = refs[:2]
    refs = refs[2:]
    cells, mixed, patch, folded, half_u, half_v, far, error, back, probe, measured, tables, probe_acc = refs[:13]
    held, total, below_wide, sems = refs[13:17]
    if last_stage and not first_stage:
        sums, given = refs[17:]
    elif last_stage:
        given = refs[17]
    even, odd, even_t, odd_t, order, order_t = [tables.at[i] for i in range(6)]
    half = size // 2
    modes = probe.shape[0]
    slots = measured.shape[0]
    rows = own.shape[0]
    low, high = bounds[stage], bounds[stage + 1]
    base = 0 if first_stage else low - size
    extent = high - base
    settled = extent if last_stage else extent - size
    count = places[3, 0]
    copies = []

    def load(source, target):
        copies.append(pltpu.make_async_copy(source, target, sems.at[len(copies)]))

    for part in range(2):
        load(
            own.at[:, pl.ds(part * width + base, extent)],
            cells.at[pl.ds(0, rows), pl.ds(part * extent, extent)],
        )
        load(
            rim.at[:, pl.ds(part * (high - low), high - low)],
            cells.at[pl.ds(rows, size), pl.ds(part * extent + low - base, high - low)],
        )
        if not first_stage:
            before = low - bounds[stage - 1]
            load(
                rim_before.at[:, pl.ds((part + 1) * before - size, size)],
                cells.at[pl.ds(rows, size), pl.ds(part * extent, size)],
            )
    n_cells = len(copies)
    load(tables_in, tables)
    load(probe_in, probe)
    load(measured_in, measured)
    if not first_stage:
        for part in range(2):
            load(
                border_in.at[:, pl.ds(part * size, size)],
                total.at[pl.ds(0, rows + size), pl.ds(part * extent, size)],
            )
    n_later = len(copies)
    if not first_stage:
        load(sums_in, sums if last_stage else probe_acc)
    for copy in copies:
        copy.start()
    if last_stage or first_stage:
        probe_acc[...] = jnp.zeros_like(probe_acc)
    for part in range(2):
        fresh = slice(part * extent + (0 if first_stage else size), (part + 1) * extent)
        total[:, fresh] = jnp.zeros((total.shape[0], fresh.stop - fresh.start), F32)
    cells[rows + size :] = jnp.zeros((cells.shape[0] - rows - size, cells.shape[1]), BF16)
    for slot in range(slots):
        for axis in range(2):
            moved[axis, slot] = 0.0 if first_stage else moved_in[axis, slot]
    for copy in copies[:n_cells]:
        copy.wait()

    def wait_later():
        for copy in copies[n_cells : n_later if last_stage else len(copies)]:
            copy.wait()

    def mine(slot):
        end = places[1, slot] + size + 1
        return jnp.logical_and(slot < count, jnp.logical_and(end > low if not first_stage else True, end <= high))

    first_slot = jnp.int32(slots)
    for slot in reversed(range(slots)):
        first_slot = jnp.where(mine(slot), slot, first_slot)

    block = 16
    blocks = size // block
    lift_rows = half + 8
    lift_from = half + 32

    def one_slot(slot):
        top = places[0, slot]
        left = places[1, slot]
        frac_y, frac_x = fractions(places[2, slot])
        row0 = pl.multiple_of((top // 16) * 16, 16)
        col0 = pl.multiple_of((left // LANES) * LANES - base, LANES)
        down = top - row0
        across = left - base - col0
        source = lax.broadcasted_iota(jnp.int32, (2 * LANES, LANES), 0)
        target = lax.broadcasted_iota(jnp.int32, (2 * LANES, LANES), 1) + across
        here = (source == target).astype(F32)
        after = (source == target + 1).astype(F32)
        blend = jnp.concatenate([(1.0 - frac_x) * here + frac_x * after, after - here], axis=1).astype(BF16)
        source = lax.broadcasted_iota(jnp.int32, (lift_rows, lift_from), 1)
        target = lax.broadcasted_iota(jnp.int32, (lift_rows, lift_from), 0) + down
        lifts = [(source == target + shift).astype(F32).astype(BF16) for shift in (0, 8)]
        for part in range(2):
            start = pl.multiple_of(col0 + part * extent, LANES)
            for piece in range(2):
                taken = pl.ds(pl.multiple_of(row0 + piece * half, 16), lift_from)
                window = dot(lifts[piece], cells[taken, pl.ds(start, size + LANES)]).astype(BF16)
                for h in range(size // LANES):
                    mixed[part, pl.ds(piece * lift_rows, lift_rows), h * size : (h + 1) * size] = dot(
                        window[:, h * LANES : (h + 2) * LANES], blend
                    )
        for part in range(2):
            for h in range(size // LANES):
                cols = slice(h * size, h * size + LANES)
                for b in range(0, size, block):
                    upper = mixed[part, pl.ds(b, block), cols]
                    lower = mixed[part, pl.ds(b + 1, block), cols]
                    to = slice(part * size + h * LANES, part * size + (h + 1) * LANES)
                    patch[pl.ds(b, block), to] = (1.0 - frac_y) * upper + frac_y * lower
        pl.when(slot == first_slot)(wait_later)

        for mode in range(modes):
            for b in range(blocks):
                at = slice(b * block, (b + 1) * block)
                spot = (2 * b if b < blocks // 2 else 2 * b + 1 - blocks) * block
                to = slice(spot, spot + block)
                preal, pimag = probe[mode, at, :size], probe[mode, at, size:]
                oreal, oimag = patch[at, :size], patch[at, size:]
                wreal = preal * oreal - pimag * oimag
                wimag = preal * oimag + pimag * oreal
                for part, wave in enumerate((wreal, wimag)):
                    folded[mode, to, part * half : (part + 1) * half] = (wave[:, :half] + wave[:, half:]).astype(BF16)
                    folded[mode, to, size + part * half : size + (part + 1) * half] = (
                        wave[:, :half] - wave[:, half:]
                    ).astype(BF16)
        for mode in range(modes):
            for k, table in enumerate((even, odd)):
                out = dot(folded[mode, :, k * size : (k + 1) * size], table[...])
                for b in range(blocks // 2):
                    upper = out[2 * b * block : (2 * b + 1) * block]
                    lower = out[(2 * b + 1) * block : (2 * b + 2) * block]
                    plus, minus = (upper + lower).astype(BF16), (upper - lower).astype(BF16)
                    for part in range(2):
                        to = slice(part * half + b * block, part * half + (b + 1) * block)
                        cols = slice(part * half, (part + 1) * half)
                        half_u[mode, to, k * half : (k + 1) * half] = plus[:, cols]
                        half_v[mode, to, k * half : (k + 1) * half] = minus[:, cols]
        for mode in range(modes):
            far[mode, 0] = dot(even_t[...], half_u[mode])
            far[mode, 1] = dot(odd_t[...], half_v[mode])

        amplitude = dot(dot(order_t[...], measured[slot]).astype(BF16), order[...])
        for k in range(2):
            for b in range(0, half, block):
                pieces = [
                    [far[mode, k, part * half + b : part * half + b + block, :] for part in range(2)]
                    for mode in range(modes)
                ]
                power = sum(p * p for pair in pieces for p in pair)
                level = amplitude[k * half + b : k * half + b + block]
                ratio = 1.0 - level / jnp.maximum(jnp.sqrt(power), 0.5)
                for mode in range(modes):
                    for part in range(2):
                        to = slice(part * half + b, part * half + b + block)
                        error[mode, k, to, :] = (pieces[mode][part] * ratio).astype(BF16)

        for mode in range(modes):
            first = dot(even[...], error[mode, 0])
            second = dot(odd[...], error[mode, 1])
            plus, minus = (first + second).astype(BF16), (first - second).astype(BF16)
            for part in range(2):
                for b in range(blocks):
                    pick = part * half + (b % (blocks // 2)) * block
                    piece = (plus if b < blocks // 2 else minus)[pick : pick + block]
                    to = slice((b * modes + mode) * block, (b * modes + mode + 1) * block)
                    for c in range(2):
                        cols = slice(c * size + part * half, c * size + (part + 1) * half)
                        back[to, cols] = piece[:, c * half : (c + 1) * half]

        total_y = jnp.zeros((block, half), F32)
        total_x = jnp.zeros((block, half), F32)
        group = size // (modes * block)
        for g in range(blocks // group):
            span = slice(g * size, (g + 1) * size)
            first = dot(back[span, :size], even_t[...])
            second = dot(back[span, size:], odd_t[...])
            for r in range(group):
                at = slice((g * group + r) * block, (g * group + r + 1) * block)
                below = slice(at.start + 1, at.stop + 1)
                for h in range(2):
                    re = slice(h * half, (h + 1) * half)
                    im = slice(size + h * half, size + (h + 1) * half)
                    oreal, oimag = patch[at, re], patch[at, im]
                    greal = jnp.zeros((block, half), F32)
                    gimag = jnp.zeros((block, half), F32)
                    for mode in range(modes):
                        part = slice((r * modes + mode) * block, (r * modes + mode + 1) * block)
                        piece = first[part] + second[part] if h == 0 else first[part] - second[part]
                        ureal, uimag = piece[:, :half], piece[:, half:]
                        preal, pimag = probe[mode, at, re], probe[mode, at, im]
                        greal += preal * ureal + pimag * uimag
                        gimag += preal * uimag - pimag * ureal
                        probe_acc[mode, at, re] += oreal * ureal + oimag * uimag
                        probe_acc[mode, at, im] += oreal * uimag - oimag * ureal
                    held[at, re] = greal.astype(BF16)
                    held[at, im] = gimag.astype(BF16)
                    for part, grad in enumerate((greal, gimag)):
                        cols = slice(h * size, h * size + LANES)
                        total_y += grad * (mixed[part, below, cols] - mixed[part, at, cols])
                        cols = slice(h * size + LANES, (h + 1) * size)
                        total_x += grad * ((1.0 - frac_y) * mixed[part, at, cols] + frac_y * mixed[part, below, cols])
        moved[0, slot] = jnp.sum(total_y) / size
        moved[1, slot] = jnp.sum(total_x) / size

        source = lax.broadcasted_iota(jnp.int32, (size, size + LANES), 0) + across
        target = lax.broadcasted_iota(jnp.int32, (size, size + LANES), 1)
        along = jnp.where(source == target, 1.0 - frac_x, 0.0) + jnp.where(source + 1 == target, frac_x, 0.0)
        along = along.astype(BF16)
        spread = size + 16
        row8 = pl.multiple_of((top // 8) * 8, 8)
        source = lax.broadcasted_iota(jnp.int32, (spread, size), 1) + (top - row8)
        target = lax.broadcasted_iota(jnp.int32, (spread, size), 0)
        drop = jnp.where(source == target, 1.0 - frac_y, 0.0) + jnp.where(source + 1 == target, frac_y, 0.0)
        drop = drop.astype(BF16)
        for part in range(2):
            wide = dot(held[:, part * size : (part + 1) * size], along).astype(BF16)
            start = pl.multiple_of(col0 + part * extent, LANES)
            total[pl.ds(row8, spread), pl.ds(start, size + LANES)] += dot(drop, wide)

    @pl.loop(0, slots)
    def _(slot):
        pl.when(mine(slot))(functools.partial(one_slot, slot))

    pl.when(first_slot == slots)(wait_later)
    outs = []

    def store(source, target):
        outs.append(pltpu.make_async_copy(source, target, sems.at[len(outs)]))
        outs[-1].start()

    if last_stage:
        core = places[4, 0]
        share = modes // 2
        give_from = (1 - core) * share
        keep_from = core * share
        if first_stage:
            given[...] = probe_acc[pl.ds(give_from, share)].astype(BF16)
        else:
            copies[-1].wait()
            given[...] = (probe_acc[pl.ds(give_from, share)] + sums[pl.ds(give_from, share)]).astype(BF16)
        store(given, give)
        if not first_stage:
            probe_acc[pl.ds(keep_from, share)] += sums[pl.ds(keep_from, share)]
        store(probe_acc.at[pl.ds(keep_from, share)], keep)
    else:
        store(probe_acc, sums_out)
        for part in range(2):
            store(
                total.at[pl.ds(0, rows + size), pl.ds(part * extent + settled, size)],
                border_out.at[:, pl.ds(part * size, size)],
            )
    for part in range(2):
        here = slice(part * extent, part * extent + settled)
        below_wide[:, part * settled : (part + 1) * settled] = total[rows : rows + size, here].astype(BF16)
    store(below_wide, below)
    for part in range(2):
        store(
            total.at[pl.ds(0, rows), pl.ds(part * extent, settled)],
            own_part.at[:, pl.ds(part * settled, settled)],
        )
    for out in outs:
        out.wait()


def project(stage, bounds, places, own, rims, probe, measured, tables, width, carried):
    slots, size, _ = measured.shape
    modes = probe.shape[0]
    rows = own.shape[0]
    smem = pl.BlockSpec(memory_space=pltpu.SMEM)
    hbm = pl.BlockSpec(memory_space=pl.ANY)
    first_stage, last_stage = stage == 0, stage == len(bounds) - 2
    low, high = bounds[stage], bounds[stage + 1]
    extent = high - (0 if first_stage else low - size)
    settled = extent if last_stage else extent - size
    inputs = [places, own, rims[stage]] + ([] if first_stage else [rims[stage - 1]]) + [probe, measured, tables]
    specs = [smem] + [hbm] * (len(inputs) - 1)
    outs = [
        jax.ShapeDtypeStruct((2, slots), F32),
        jax.ShapeDtypeStruct((rows, 2 * settled), F32),
        jax.ShapeDtypeStruct((size, 2 * settled), BF16),
    ]
    share = (modes // 2,) + probe.shape[1:]
    if not first_stage:
        inputs += list(carried)
        specs += [smem, hbm, hbm]
    if last_stage:
        outs += [jax.ShapeDtypeStruct(share, F32), jax.ShapeDtypeStruct(share, BF16)]
    else:
        outs += [jax.ShapeDtypeStruct(probe.shape, F32), jax.ShapeDtypeStruct((rows + size, 2 * size), F32)]
    scratch = [
        pltpu.VMEM((rows + size + 32, 2 * extent), BF16),
        pltpu.VMEM((2, size + 16, 2 * size), F32),
        pltpu.VMEM((size, 2 * size), F32),
        pltpu.VMEM((modes, size, 2 * size), BF16),
        pltpu.VMEM((modes, size, size), BF16),
        pltpu.VMEM((modes, size, size), BF16),
        pltpu.VMEM((modes, 2, size, size), F32),
        pltpu.VMEM((modes, 2, size, size), BF16),
        pltpu.VMEM((modes * size, 2 * size), BF16),
        pltpu.VMEM(probe.shape, F32),
        pltpu.VMEM(measured.shape, BF16),
        pltpu.VMEM(tables.shape, BF16),
        pltpu.VMEM(probe.shape, F32),
        pltpu.VMEM((size, 2 * size), BF16),
        pltpu.VMEM((rows + size + 16, 2 * extent), F32),
        pltpu.VMEM((size, 2 * settled), BF16),
        pltpu.SemaphoreType.DMA((12,)),
    ]
    if last_stage and not first_stage:
        scratch.append(pltpu.VMEM(probe.shape, F32))
    if last_stage:
        scratch.append(pltpu.VMEM(share, BF16))
    return pl.pallas_call(
        functools.partial(project_kernel, size, width, bounds, stage),
        in_specs=specs,
        out_specs=[smem] + [hbm] * (len(outs) - 1),
        out_shape=outs,
        scratch_shapes=scratch,
        compiler_params=pltpu.CompilerParams(vmem_limit_bytes=VMEM_BYTES),
        cost_estimate=pl.CostEstimate(flops=8 * 10**9, bytes_accessed=16 * 2**20, transcendentals=0),
        name=f"project_{stage}",
    )(*inputs)


def finish_kernel(lows, highs, n, *refs):
    owns, aboves = refs[:n], refs[n : 2 * n]
    out, wides, adds, sems = refs[-3 - 2 * n], refs[-2 - 2 * n : -2 - n], refs[-2 - n : -2], refs[-2:]
    outs = []
    loads = []
    for i in range(n):
        loads.append(pltpu.make_async_copy(owns[i], wides[i], sems[0].at[2 * i]))
        loads.append(pltpu.make_async_copy(aboves[i], adds[i], sems[0].at[2 * i + 1]))
    for copy in loads:
        copy.start()
    for i in range(n):
        loads[2 * i].wait()
        loads[2 * i + 1].wait()
        length = highs[i] - lows[i]
        for part in range(2):
            cols = slice(part * length, (part + 1) * length)
            wides[i][:, cols] += adds[i][:, cols].astype(F32)
            copy = pltpu.make_async_copy(
                wides[i].at[:, pl.ds(part * length, length)],
                out.at[:, part, pl.ds(lows[i], length)],
                sems[1].at[2 * i + part],
            )
            copy.start()
            outs.append(copy)
    for copy in outs:
        copy.wait()


def finish(owns, aboves, lows, highs, width):
    n = len(owns)
    hbm = pl.BlockSpec(memory_space=pl.ANY)
    rows = owns[0].shape[0]
    return pl.pallas_call(
        functools.partial(finish_kernel, lows, highs, n),
        in_specs=[hbm] * (2 * n),
        out_specs=hbm,
        out_shape=jax.ShapeDtypeStruct((rows, 2, width), F32),
        scratch_shapes=[pltpu.VMEM(x.shape, F32) for x in owns]
        + [pltpu.VMEM(x.shape, BF16) for x in aboves]
        + [pltpu.SemaphoreType.DMA((2 * n,)), pltpu.SemaphoreType.DMA((2 * n,))],
        compiler_params=pltpu.CompilerParams(vmem_limit_bytes=VMEM_BYTES),
        name="finish",
    )(*owns, *aboves)


def passed_along(x, axis, by):
    length = lax.axis_size(axis)
    pairs = [(i, i + by) for i in range(length) if 0 <= i + by < length]
    return lax.ppermute(x, axis, pairs)


def unpack_kernel(order, *refs):
    pieces, out, wide, sems = refs[:-3], refs[-3], refs[-2], refs[-1]
    rows = pieces[0].shape[0]
    modes, size, _, _ = out.shape
    copies = []
    for i, piece in enumerate(pieces):
        wide[i * rows : (i + 1) * rows] = piece[...].astype(F32)
        mode = order[i] // (size // rows)
        at = pl.multiple_of(order[i] % (size // rows) * rows, 8)
        for part in range(2):
            copy = pltpu.make_async_copy(
                wide.at[pl.ds(i * rows, rows), pl.ds(part * size, size)],
                out.at[mode, pl.ds(at, rows), part, :],
                sems.at[2 * i + part],
            )
            copy.start()
            copies.append(copy)
    for copy in copies:
        copy.wait()


def unpacked(pieces, order, shape):
    vmem = pl.BlockSpec(memory_space=pltpu.VMEM)
    smem = pl.BlockSpec(memory_space=pltpu.SMEM)
    return pl.pallas_call(
        unpack_kernel,
        in_specs=[smem] + [vmem] * len(pieces),
        out_specs=pl.BlockSpec(memory_space=pl.ANY),
        out_shape=jax.ShapeDtypeStruct(shape, F32),
        scratch_shapes=[
            pltpu.VMEM((len(pieces) * pieces[0].shape[0], pieces[0].shape[1]), F32),
            pltpu.SemaphoreType.DMA((2 * len(pieces),)),
        ],
        compiler_params=pltpu.CompilerParams(vmem_limit_bytes=VMEM_BYTES),
        name="unpack",
    )(order, *pieces)


def piece_order(axis):
    length = lax.axis_size(axis)
    near = min(4, length // 2)
    me = lax.axis_index(axis)
    core, spot = me % 2, me // 2 % near
    return jnp.stack(
        [core * near + (spot ^ s) for s in range(near)] + [(1 - core) * near + (spot ^ s) for s in range(near)]
    )


def summed(keep, give, axis, shape, order, late):
    length = lax.axis_size(axis)
    chips = length // 2
    near = min(4, chips)
    far = chips // near
    me = lax.axis_index(axis)
    core, chip = me % 2, me // 2
    across = [(i, i ^ 1) for i in range(length)]

    def hop(shift, stride):
        return [(i, i ^ (2 * stride * shift)) for i in range(length)]

    size, columns = keep.shape[1:]
    mine = keep + lax.ppermute(give, axis, across).astype(F32)
    rows = mine.shape[0] * size // near
    mine = mine.reshape(near, rows, columns)
    parts = mine.astype(BF16)
    spot = chip % near
    got = [
        lax.ppermute(lax.dynamic_index_in_dim(parts, spot ^ s, 0, False), axis, hop(s, 1)) for s in range(1, near)
    ]
    total = lax.dynamic_index_in_dim(mine, spot, 0, False)
    for piece in got:
        total = total + piece.astype(F32)
    sent = total.astype(BF16)
    sent, late = lax.optimization_barrier((sent, late))
    for s in range(1, far):
        total = total + lax.ppermute(sent, axis, hop(s, near)).astype(F32)
    total = total.astype(BF16)
    pieces = [total] + [lax.ppermute(total, axis, hop(s, 1)) for s in range(1, near)]
    others = [lax.ppermute(piece, axis, across) for piece in pieces]
    return unpacked(pieces + others, order, shape), late


def column_bounds(width, shares):
    return tuple([0] + [round(width * share / LANES) * LANES for share in shares] + [width])


def shards(object_tiles, probe, measured, offset_row, offset_col, subpixel, live_count):
    rows, _, width = object_tiles.shape
    modes, size = probe.shape[:2]
    tables = dft_tables(size)
    bounds = column_bounds(width, (0.5625,))
    stages = len(bounds) - 1
    rims = [
        passed_along(object_tiles[:size, :, low:high].reshape(size, 2 * (high - low)), "row", -1)
        for low, high in zip(bounds[:-1], bounds[1:])
    ]
    core = lax.axis_index("row") % 2
    places = jnp.stack(
        [offset_row, offset_col, subpixel] + [jnp.broadcast_to(x, offset_row.shape) for x in (live_count, core)]
    )
    places, order = lax.optimization_barrier((places, piece_order("row")))
    own = object_tiles.reshape(rows, 2 * width)
    flat = probe.reshape(modes, size, 2 * size)
    carried = None
    owns, belows = [], []
    for stage in range(stages):
        moved, own_part, below, *rest = project(
            stage, bounds, places, own, rims, flat, measured, tables, width, carried
        )
        carried = [moved] + rest
        owns.append(own_part)
        belows.append(below)
    _, keep, give = carried
    edges = [0] + [bound - size for bound in bounds[1:-1]] + [width]
    aboves = [passed_along(below, "row", 1) for below in belows[:-1]]
    probe_grad, late = summed(keep, give, "row", probe.shape, order, belows[-1])
    aboves.append(passed_along(late, "row", 1))
    object_grad = finish(owns, aboves, edges[:-1], edges[1:], width)
    return object_grad, probe_grad, moved


def solution(mesh):
    in_specs = (
        P(("groups", "row"), None, None),
        P(),
        P(("groups", "row"), None, None),
        P(("groups", "row")),
        P(("groups", "row")),
        P(("groups", "row")),
        P(("groups", "row")),
    )
    out_specs = (
        P(("groups", "row"), None, None),
        P("groups", None, None, None),
        P(None, ("groups", "row")),
    )
    return jax.shard_map(shards, mesh=mesh, in_specs=in_specs, out_specs=out_specs, check_vma=False)
```

```python
import functools
import math

import jax
import jax.numpy as jnp
import ml_dtypes
import numpy as np
from jax import lax
from jax.experimental import pallas as pl
from jax.experimental.pallas import tpu as pltpu
from jax.sharding import PartitionSpec as P

F32 = jnp.float32
BF16 = jnp.bfloat16
LANES = 128
VMEM_BYTES = 36 * 2**20
VMEM_SMALL = 20 * 2**20


def dft_tables(size):
    half = size // 2
    index = np.arange(size)
    angle = (index[:, None] * index[None, :] % size) * (2.0 * math.pi / size)
    scale = 1.0 / math.sqrt(size)
    cosine = (np.cos(angle) * scale).astype(ml_dtypes.bfloat16)
    sine = (np.sin(angle) * scale).astype(ml_dtypes.bfloat16)
    tables = []
    for parity in (0, 1):
        c, s = cosine[:half, parity::2], sine[:half, parity::2]
        tables.append(np.block([[c, -s], [s, c]]))
    order = np.zeros((size, size), ml_dtypes.bfloat16)
    order[2 * index[:half], index[:half]] = 1
    order[2 * index[:half] + 1, half + index[:half]] = 1
    even, odd = tables
    return jnp.asarray(np.stack([even, odd, even.T, odd.T, order, order.T]))


def dot(left, right):
    return jnp.dot(left, right, preferred_element_type=F32)


def fractions(code):
    return (code // 4).astype(F32) * 0.25, (code % 4).astype(F32) * 0.25


def in_stage(places, slot, bounds, stage, size):
    end = places[1, slot] + size + 1
    here = end <= bounds[stage + 1]
    if stage > 0:
        here = jnp.logical_and(here, end > bounds[stage])
    return jnp.logical_and(slot < places[3, 0], here)


def project_kernel(size, width, bounds, stage, places, *refs):
    first_stage, last_stage = stage == 0, stage == len(bounds) - 2
    refs = list(refs)
    own, rim = refs[:2]
    rim_before = None if first_stage else refs[2]
    refs = refs[2:] if first_stage else refs[3:]
    probe_in, measured_in, tables_in = refs[:3]
    refs = refs[3:]
    if not first_stage:
        moved_in, sums_in = refs[:2]
        refs = refs[2:]
    moved, grads = refs[:2]
    refs = refs[2:]
    if last_stage:
        keep, give = refs[:2]
        refs = refs[2:]
    else:
        sums_out = refs.pop(0)
    cells, mixed, patch, folded, half_u, half_v, far, error, back, probe, measured, tables, probe_acc, held = refs[:14]
    sems, slot_sems = refs[14:16]
    if last_stage and not first_stage:
        sums, given = refs[16:]
    elif last_stage:
        given = refs[16]
    even, odd, even_t, odd_t, order, order_t = [tables.at[i] for i in range(6)]
    half = size // 2
    modes = probe.shape[0]
    slots = measured.shape[0]
    rows = own.shape[0]
    low, high = bounds[stage], bounds[stage + 1]
    base = 0 if first_stage else low - size
    extent = high - base
    count = places[3, 0]
    copies = []

    def load(source, target):
        copies.append(pltpu.make_async_copy(source, target, sems.at[len(copies)]))

    for part in range(2):
        load(
            own.at[:, pl.ds(part * width + base, extent)],
            cells.at[pl.ds(0, rows), pl.ds(part * extent, extent)],
        )
        load(
            rim.at[:, pl.ds(part * (high - low), high - low)],
            cells.at[pl.ds(rows, size), pl.ds(part * extent + low - base, high - low)],
        )
        if not first_stage:
            before = low - bounds[stage - 1]
            load(
                rim_before.at[:, pl.ds((part + 1) * before - size, size)],
                cells.at[pl.ds(rows, size), pl.ds(part * extent, size)],
            )
    n_cells = len(copies)
    load(tables_in, tables)
    load(probe_in, probe)
    load(measured_in, measured)
    n_later = len(copies)
    if not first_stage:
        load(sums_in, sums if last_stage else probe_acc)
    for copy in copies:
        copy.start()
    if last_stage or first_stage:
        probe_acc[...] = jnp.zeros_like(probe_acc)
    cells[rows + size :] = jnp.zeros((cells.shape[0] - rows - size, cells.shape[1]), BF16)
    for slot in range(slots):
        for axis in range(2):
            moved[axis, slot] = 0.0 if first_stage else moved_in[axis, slot]
    for copy in copies[:n_cells]:
        copy.wait()

    def wait_later():
        for copy in copies[n_cells : n_later if last_stage else len(copies)]:
            copy.wait()

    def mine(slot):
        return in_stage(places, slot, bounds, stage, size)

    def sent_out(slot):
        return pltpu.make_async_copy(held.at[slot], grads.at[slot], slot_sems.at[slot])

    first_slot = jnp.int32(slots)
    for slot in reversed(range(slots)):
        first_slot = jnp.where(mine(slot), slot, first_slot)

    block = 16
    blocks = size // block
    lift_rows = half + 8
    lift_from = half + 32

    def one_slot(slot):
        top = places[0, slot]
        left = places[1, slot]
        frac_y, frac_x = fractions(places[2, slot])
        row0 = pl.multiple_of((top // 16) * 16, 16)
        col0 = pl.multiple_of((left // LANES) * LANES - base, LANES)
        down = top - row0
        across = left - base - col0
        source = lax.broadcasted_iota(jnp.int32, (2 * LANES, LANES), 0)
        target = lax.broadcasted_iota(jnp.int32, (2 * LANES, LANES), 1) + across
        here = (source == target).astype(F32)
        after = (source == target + 1).astype(F32)
        blend = jnp.concatenate([(1.0 - frac_x) * here + frac_x * after, after - here], axis=1).astype(BF16)
        source = lax.broadcasted_iota(jnp.int32, (lift_rows, lift_from), 1)
        target = lax.broadcasted_iota(jnp.int32, (lift_rows, lift_from), 0) + down
        lifts = [(source == target + shift).astype(F32).astype(BF16) for shift in (0, 8)]
        for part in range(2):
            start = pl.multiple_of(col0 + part * extent, LANES)
            for piece in range(2):
                taken = pl.ds(pl.multiple_of(row0 + piece * half, 16), lift_from)
                window = dot(lifts[piece], cells[taken, pl.ds(start, size + LANES)]).astype(BF16)
                for h in range(size // LANES):
                    mixed[part, pl.ds(piece * lift_rows, lift_rows), h * size : (h + 1) * size] = dot(
                        window[:, h * LANES : (h + 2) * LANES], blend
                    )
        for part in range(2):
            for h in range(size // LANES):
                cols = slice(h * size, h * size + LANES)
                for b in range(0, size, block):
                    upper = mixed[part, pl.ds(b, block), cols]
                    lower = mixed[part, pl.ds(b + 1, block), cols]
                    to = slice(part * size + h * LANES, part * size + (h + 1) * LANES)
                    patch[pl.ds(b, block), to] = (1.0 - frac_y) * upper + frac_y * lower
        pl.when(slot == first_slot)(wait_later)

        for mode in range(modes):
            for b in range(blocks):
                at = slice(b * block, (b + 1) * block)
                spot = (2 * b if b < blocks // 2 else 2 * b + 1 - blocks) * block
                to = slice(spot, spot + block)
                preal, pimag = probe[mode, at, :size], probe[mode, at, size:]
                oreal, oimag = patch[at, :size], patch[at, size:]
                wreal = preal * oreal - pimag * oimag
                wimag = preal * oimag + pimag * oreal
                for part, wave in enumerate((wreal, wimag)):
                    folded[mode, to, part * half : (part + 1) * half] = (wave[:, :half] + wave[:, half:]).astype(BF16)
                    folded[mode, to, size + part * half : size + (part + 1) * half] = (
                        wave[:, :half] - wave[:, half:]
                    ).astype(BF16)
        for mode in range(modes):
            for k, table in enumerate((even, odd)):
                out = dot(folded[mode, :, k * size : (k + 1) * size], table[...])
                for b in range(blocks // 2):
                    upper = out[2 * b * block : (2 * b + 1) * block]
                    lower = out[(2 * b + 1) * block : (2 * b + 2) * block]
                    plus, minus = (upper + lower).astype(BF16), (upper - lower).astype(BF16)
                    for part in range(2):
                        to = slice(part * half + b * block, part * half + (b + 1) * block)
                        cols = slice(part * half, (part + 1) * half)
                        half_u[mode, to, k * half : (k + 1) * half] = plus[:, cols]
                        half_v[mode, to, k * half : (k + 1) * half] = minus[:, cols]
        for mode in range(modes):
            far[mode, 0] = dot(even_t[...], half_u[mode])
            far[mode, 1] = dot(odd_t[...], half_v[mode])

        amplitude = dot(dot(order_t[...], measured[slot]).astype(BF16), order[...])
        for k in range(2):
            for b in range(0, half, block):
                pieces = [
                    [far[mode, k, part * half + b : part * half + b + block, :] for part in range(2)]
                    for mode in range(modes)
                ]
                power = sum(p * p for pair in pieces for p in pair)
                level = amplitude[k * half + b : k * half + b + block]
                ratio = 1.0 - level / jnp.maximum(jnp.sqrt(power), 0.5)
                for mode in range(modes):
                    for part in range(2):
                        to = slice(part * half + b, part * half + b + block)
                        error[mode, k, to, :] = (pieces[mode][part] * ratio).astype(BF16)

        for mode in range(modes):
            first = dot(even[...], error[mode, 0])
            second = dot(odd[...], error[mode, 1])
            plus, minus = (first + second).astype(BF16), (first - second).astype(BF16)
            for part in range(2):
                for b in range(blocks):
                    pick = part * half + (b % (blocks // 2)) * block
                    piece = (plus if b < blocks // 2 else minus)[pick : pick + block]
                    to = slice((b * modes + mode) * block, (b * modes + mode + 1) * block)
                    for c in range(2):
                        cols = slice(c * size + part * half, c * size + (part + 1) * half)
                        back[to, cols] = piece[:, c * half : (c + 1) * half]

        total_y = jnp.zeros((block, half), F32)
        total_x = jnp.zeros((block, half), F32)
        group = size // (modes * block)
        for g in range(blocks // group):
            span = slice(g * size, (g + 1) * size)
            first = dot(back[span, :size], even_t[...])
            second = dot(back[span, size:], odd_t[...])
            for r in range(group):
                at = slice((g * group + r) * block, (g * group + r + 1) * block)
                below = slice(at.start + 1, at.stop + 1)
                for h in range(2):
                    re = slice(h * half, (h + 1) * half)
                    im = slice(size + h * half, size + (h + 1) * half)
                    oreal, oimag = patch[at, re], patch[at, im]
                    greal = jnp.zeros((block, half), F32)
                    gimag = jnp.zeros((block, half), F32)
                    for mode in range(modes):
                        part = slice((r * modes + mode) * block, (r * modes + mode + 1) * block)
                        piece = first[part] + second[part] if h == 0 else first[part] - second[part]
                        ureal, uimag = piece[:, :half], piece[:, half:]
                        preal, pimag = probe[mode, at, re], probe[mode, at, im]
                        greal += preal * ureal + pimag * uimag
                        gimag += preal * uimag - pimag * ureal
                        probe_acc[mode, at, re] += oreal * ureal + oimag * uimag
                        probe_acc[mode, at, im] += oreal * uimag - oimag * ureal
                    held[slot, at, re] = greal.astype(BF16)
                    held[slot, at, im] = gimag.astype(BF16)
                    for part, grad in enumerate((greal, gimag)):
                        cols = slice(h * size, h * size + LANES)
                        total_y += grad * (mixed[part, below, cols] - mixed[part, at, cols])
                        cols = slice(h * size + LANES, (h + 1) * size)
                        total_x += grad * ((1.0 - frac_y) * mixed[part, at, cols] + frac_y * mixed[part, below, cols])
        moved[0, slot] = jnp.sum(total_y) / size
        moved[1, slot] = jnp.sum(total_x) / size

        sent_out(slot).start()

    @pl.loop(0, slots)
    def _(slot):
        pl.when(mine(slot))(functools.partial(one_slot, slot))

    pl.when(first_slot == slots)(wait_later)
    outs = []

    def store(source, target):
        outs.append(pltpu.make_async_copy(source, target, sems.at[len(outs)]))
        outs[-1].start()

    if last_stage:
        if first_stage:
            given[...] = probe_acc[...].astype(BF16)
            store(given, give)
        else:
            copies[-1].wait()
            for mode in range(modes):
                probe_acc[mode] += sums[mode]
                given[mode] = probe_acc[mode].astype(BF16)
            store(given, give)
        store(probe_acc, keep)
    else:
        store(probe_acc, sums_out)

    @pl.loop(0, slots)
    def _(slot):
        @pl.when(mine(slot))
        def _():
            sent_out(slot).wait()

    for out in outs:
        out.wait()


def project(stage, bounds, places, own, rims, probe, measured, tables, width, carried):
    slots, size, _ = measured.shape
    modes = probe.shape[0]
    rows = own.shape[0]
    smem = pl.BlockSpec(memory_space=pltpu.SMEM)
    hbm = pl.BlockSpec(memory_space=pl.ANY)
    first_stage, last_stage = stage == 0, stage == len(bounds) - 2
    low, high = bounds[stage], bounds[stage + 1]
    extent = high - (0 if first_stage else low - size)
    inputs = [places, own, rims[stage]] + ([] if first_stage else [rims[stage - 1]]) + [probe, measured, tables]
    specs = [smem] + [hbm] * (len(inputs) - 1)
    outs = [
        jax.ShapeDtypeStruct((2, slots), F32),
        jax.ShapeDtypeStruct((slots, size, 2 * size), BF16),
        jax.ShapeDtypeStruct(probe.shape, F32),
    ]
    if not first_stage:
        inputs += list(carried)
        specs += [smem, hbm]
    if last_stage:
        outs += [jax.ShapeDtypeStruct(probe.shape, BF16)]
    scratch = [
        pltpu.VMEM((rows + size + 32, 2 * extent), BF16),
        pltpu.VMEM((2, size + 16, 2 * size), F32),
        pltpu.VMEM((size, 2 * size), F32),
        pltpu.VMEM((modes, size, 2 * size), BF16),
        pltpu.VMEM((modes, size, size), BF16),
        pltpu.VMEM((modes, size, size), BF16),
        pltpu.VMEM((modes, 2, size, size), F32),
        pltpu.VMEM((modes, 2, size, size), BF16),
        pltpu.VMEM((modes * size, 2 * size), BF16),
        pltpu.VMEM(probe.shape, F32),
        pltpu.VMEM(measured.shape, BF16),
        pltpu.VMEM(tables.shape, BF16),
        pltpu.VMEM(probe.shape, F32),
        pltpu.VMEM((slots, size, 2 * size), BF16),
        pltpu.SemaphoreType.DMA((12,)),
        pltpu.SemaphoreType.DMA((slots,)),
    ]
    if last_stage and not first_stage:
        scratch.append(pltpu.VMEM(probe.shape, F32))
    if last_stage:
        scratch.append(pltpu.VMEM(probe.shape, BF16))
    return pl.pallas_call(
        functools.partial(project_kernel, size, width, bounds, stage),
        in_specs=specs,
        out_specs=[smem] + [hbm] * (len(outs) - 1),
        out_shape=outs,
        scratch_shapes=scratch,
        compiler_params=pltpu.CompilerParams(vmem_limit_bytes=VMEM_BYTES),
        cost_estimate=pl.CostEstimate(flops=8 * 10**9, bytes_accessed=16 * 2**20, transcendentals=0),
        name=f"project_{stage}",
    )(*inputs)


def settle_kernel(size, bounds, low, high, shift, places, *refs):
    grads = refs[: len(refs) - 5]
    out, total, held, sems, out_sems = refs[len(refs) - 5 :]
    slots = held.shape[0]
    reach = size + LANES
    base = max(low - size, 0)
    extent = total.shape[1] // 2
    length = high - low

    def taken(stage, slot):
        left = places[1, slot]
        within = jnp.logical_and(left < high, left + size + 1 > low)
        return jnp.logical_and(within, in_stage(places, slot, bounds, stage, size))

    def fetch(stage, slot):
        return pltpu.make_async_copy(grads[stage].at[slot], held.at[slot], sems.at[slot])

    for stage in range(len(grads)):

        @pl.loop(0, slots)
        def _(slot, stage=stage):
            @pl.when(taken(stage, slot))
            def _():
                fetch(stage, slot).start()

    total[...] = jnp.zeros_like(total)

    def one_slot(stage, slot):
        left = places[1, slot]
        frac_y, frac_x = fractions(places[2, slot])
        col0 = (left // LANES) * LANES
        ahead = lax.broadcasted_iota(jnp.int32, (size, reach), 1) - lax.broadcasted_iota(jnp.int32, (size, reach), 0)
        ahead = ahead - (left - col0)
        along = jnp.where(ahead == 0, 1.0 - frac_x, jnp.where(ahead == 1, frac_x, 0.0)).astype(BF16)
        ahead = lax.broadcasted_iota(jnp.int32, (size, size), 0) - lax.broadcasted_iota(jnp.int32, (size, size), 1)
        ahead = ahead - (places[0, slot] - shift)
        down = jnp.where(ahead == 0, 1.0 - frac_y, jnp.where(ahead == 1, frac_y, 0.0)).astype(BF16)
        fetch(stage, slot).wait()
        for part in range(2):
            wide = dot(held[slot, :, part * size : (part + 1) * size], along).astype(BF16)
            start = pl.multiple_of(col0 - base + part * extent, LANES)
            total[:, pl.ds(start, reach)] += dot(down, wide)

    for stage in range(len(grads)):

        @pl.loop(0, slots)
        def _(slot, stage=stage):
            pl.when(taken(stage, slot))(functools.partial(one_slot, stage, slot))

    copies = []
    for part in range(2):
        here = slice(part * extent + low - base, part * extent + low - base + length)
        there = slice(part * length, (part + 1) * length)
        if out.dtype == F32:
            copies.append(
                pltpu.make_async_copy(
                    total.at[:, pl.ds(here.start, length)], out.at[:, pl.ds(there.start, length)], out_sems.at[part]
                )
            )
            copies[-1].start()
        else:
            out[:, there] = total[:, here].astype(out.dtype)
    for copy in copies:
        copy.wait()


def settle(places, grads, bounds, low, high, shift, dtype, width, name):
    slots, size, _ = grads[0].shape
    base, end = max(low - size, 0), min(high + size, width)
    hbm = pl.BlockSpec(memory_space=pl.ANY)
    return pl.pallas_call(
        functools.partial(settle_kernel, size, bounds, low, high, shift),
        in_specs=[pl.BlockSpec(memory_space=pltpu.SMEM)] + [hbm] * len(grads),
        out_specs=hbm if dtype == F32 else pl.BlockSpec(memory_space=pltpu.VMEM),
        out_shape=jax.ShapeDtypeStruct((size, 2 * (high - low)), dtype),
        scratch_shapes=[
            pltpu.VMEM((size, 2 * (end - base)), F32),
            pltpu.VMEM(grads[0].shape, BF16),
            pltpu.SemaphoreType.DMA((slots,)),
            pltpu.SemaphoreType.DMA((2,)),
        ],
        compiler_params=pltpu.CompilerParams(vmem_limit_bytes=VMEM_SMALL),
        cost_estimate=pl.CostEstimate(flops=10**9, bytes_accessed=8 * 2**20, transcendentals=0),
        name=name,
    )(places, *grads)


def finish_kernel(edges, n, own, *refs):
    aboves, out = refs[:n], refs[n]
    wides, adds, sems = refs[n + 1 : 2 * n + 1], refs[2 * n + 1 : 3 * n + 1], refs[3 * n + 1]
    width = out.shape[2]
    loads, outs = [], []

    def copied(source, target, to):
        to.append(pltpu.make_async_copy(source, target, sems.at[len(loads) + len(outs)]))
        to[-1].start()

    for i in range(n):
        length = edges[i + 1] - edges[i]
        for part in range(2):
            copied(
                own.at[:, pl.ds(part * width + edges[i], length)], wides[i].at[:, pl.ds(part * length, length)], loads
            )
        copied(aboves[i], adds[i], loads)
    for i in range(n):
        for copy in loads[3 * i : 3 * i + 3]:
            copy.wait()
        length = edges[i + 1] - edges[i]
        for part in range(2):
            cols = slice(part * length, (part + 1) * length)
            wides[i][:, cols] += adds[i][:, cols].astype(F32)
            copied(wides[i].at[:, pl.ds(part * length, length)], out.at[:, part, pl.ds(edges[i], length)], outs)
    for copy in outs:
        copy.wait()


def finish(own, aboves, edges, width):
    n = len(aboves)
    hbm = pl.BlockSpec(memory_space=pl.ANY)
    return pl.pallas_call(
        functools.partial(finish_kernel, edges, n),
        in_specs=[hbm] * (n + 1),
        out_specs=hbm,
        out_shape=jax.ShapeDtypeStruct((own.shape[0], 2, width), F32),
        scratch_shapes=[pltpu.VMEM(x.shape, F32) for x in aboves]
        + [pltpu.VMEM(x.shape, BF16) for x in aboves]
        + [pltpu.SemaphoreType.DMA((5 * n,))],
        compiler_params=pltpu.CompilerParams(vmem_limit_bytes=VMEM_SMALL),
        cost_estimate=pl.CostEstimate(flops=10**6, bytes_accessed=10 * 2**20, transcendentals=0),
        name="finish",
    )(own, *aboves)


def passed_along(x, axis, by):
    length = lax.axis_size(axis)
    pairs = [(i, i + by) for i in range(length) if 0 <= i + by < length]
    return lax.ppermute(x, axis, pairs)


def unpack_kernel(order, *refs):
    n = (len(refs) - 4) // 2
    out, wide, narrow, sems = refs[2 * n :]
    rows = wide.shape[1]
    size = out.shape[1]
    span = min(rows, size)
    for core in range(2):

        @pl.when(order[n] == core)
        def _():
            for i in range(n):
                pltpu.make_async_copy(refs[core * n + i], narrow.at[i], sems.at[0, i]).start()

    copies = []
    for i in range(n):
        pltpu.make_async_copy(refs[i], narrow.at[i], sems.at[0, i]).wait()
        wide[i] = narrow[i].astype(F32)
        for j in range(rows // span):
            line = order[i] * rows + j * span
            mode = line // size
            at = pl.multiple_of(line % size, 8)
            for part in range(2):
                copies.append(
                    pltpu.make_async_copy(
                        wide.at[i, pl.ds(j * span, span), pl.ds(part * size, size)],
                        out.at[mode, pl.ds(at, span), part, :],
                        sems.at[1, len(copies)],
                    )
                )
                copies[-1].start()
    for copy in copies:
        copy.wait()


def unpacked(pieces, others, order, shape):
    n = len(pieces)
    rows, columns = pieces[0].shape
    hbm = pl.BlockSpec(memory_space=pl.ANY)
    return pl.pallas_call(
        unpack_kernel,
        in_specs=[pl.BlockSpec(memory_space=pltpu.SMEM)] + [hbm] * (2 * n),
        out_specs=hbm,
        out_shape=jax.ShapeDtypeStruct(shape, F32),
        scratch_shapes=[
            pltpu.VMEM((n, rows, columns), F32),
            pltpu.VMEM((n, rows, columns), BF16),
            pltpu.SemaphoreType.DMA((2, 2 * n * max(1, rows // shape[1]))),
        ],
        compiler_params=pltpu.CompilerParams(vmem_limit_bytes=VMEM_SMALL),
        cost_estimate=pl.CostEstimate(flops=10**6, bytes_accessed=4 * 2**20, transcendentals=0),
        name="unpack",
    )(order, *pieces, *others)


def near_chips(axis):
    return min(4, lax.axis_size(axis) // 2)


def piece_order(axis):
    near = near_chips(axis)
    me = lax.axis_index(axis)
    core, spot = me % 2, me // 2 % near
    return jnp.stack([spot ^ s for s in range(near)] + [core])


def hop(axis, shift, stride):
    return [(i, i ^ (2 * stride * shift)) for i in range(0, lax.axis_size(axis), 2)]


def summed(keep, give, axis, shape, order, first, between, after):
    length = lax.axis_size(axis)
    near = near_chips(axis)
    far = length // 2 // near
    inward = [(i + 1, i) for i in range(0, length, 2)]
    outward = [(i, i + 1) for i in range(0, length, 2)]
    modes, size, columns = keep.shape
    spot = lax.axis_index(axis) // 2 % near
    mine = keep + lax.ppermute(give, axis, inward).astype(F32)
    mine = first(mine)
    mine = mine.reshape(near, modes * size // near, columns)
    parts = mine.astype(BF16)
    got = [
        lax.ppermute(lax.dynamic_index_in_dim(parts, spot ^ s, 0, False), axis, hop(axis, s, 1)) for s in range(1, near)
    ]
    total = lax.dynamic_index_in_dim(mine, spot, 0, False)
    for piece in got:
        total = total + piece.astype(F32)
    total = between(total)
    sent = total.astype(BF16)
    for s in range(1, far):
        total = total + lax.ppermute(sent, axis, hop(axis, s, near)).astype(F32)
    total = after(total.astype(BF16))
    pieces = [total] + [lax.ppermute(total, axis, hop(axis, s, 1)) for s in range(1, near)]
    others = [lax.ppermute(piece, axis, outward) for piece in pieces]
    return unpacked(pieces, others, order, shape)


def column_bounds(width, shares):
    return tuple([0] + [round(width * share / LANES) * LANES for share in shares] + [width])


def shards(object_tiles, probe, measured, offset_row, offset_col, subpixel, live_count):
    rows, _, width = object_tiles.shape
    modes, size = probe.shape[:2]
    tables = dft_tables(size)
    bounds = column_bounds(width, (0.5625,))
    stages = len(bounds) - 1
    rims = [
        passed_along(object_tiles[:size, :, low:high].reshape(size, 2 * (high - low)), "row", -1)
        for low, high in zip(bounds[:-1], bounds[1:])
    ]
    core = lax.axis_index("row") % 2
    places = jnp.stack(
        [offset_row, offset_col, subpixel] + [jnp.broadcast_to(x, offset_row.shape) for x in (live_count, core)]
    )
    places, order = lax.optimization_barrier((places, piece_order("row")))
    own = object_tiles.reshape(rows, 2 * width)
    flat = probe.reshape(modes, size, 2 * size)
    carried = None
    grads, aboves = [], []
    edges = [0] + [bound - size for bound in bounds[1:-1]] + [width]
    for stage in range(stages):
        moved, grad, *rest = project(stage, bounds, places, own, rims, flat, measured, tables, width, carried)
        grads.append(grad)
        carried = [moved] + rest
        below = settle(places, grads, bounds, edges[stage], edges[stage + 1], size, BF16, width, f"below_{stage}")
        if stage < stages - 1:
            places, below = lax.optimization_barrier((places, below))
        aboves.append(passed_along(below, "row", 1))
    _, keep, give = carried
    give, aboves[0] = lax.optimization_barrier((give, aboves[0]))
    held = {}

    def between(x):
        own_rows = settle(places, grads, bounds, 0, width, 0, F32, width, "own_rows")
        x, held["own"] = lax.optimization_barrier((x, own_rows))
        return x

    probe_grad = summed(keep, give, "row", probe.shape, order, lambda x: x, between, lambda x: x)
    object_grad = finish(held["own"], aboves, edges, width)
    return object_grad, probe_grad, moved


def solution(mesh):
    in_specs = (
        P(("groups", "row"), None, None),
        P(),
        P(("groups", "row"), None, None),
        P(("groups", "row")),
        P(("groups", "row")),
        P(("groups", "row")),
        P(("groups", "row")),
    )
    out_specs = (
        P(("groups", "row"), None, None),
        P("groups", None, None, None),
        P(None, ("groups", "row")),
    )
    return jax.shard_map(shards, mesh=mesh, in_specs=in_specs, out_specs=out_specs, check_vma=False)
```

```python
import functools
import math

import jax
import jax.numpy as jnp
import ml_dtypes
import numpy as np
from jax import lax
from jax.experimental import pallas as pl
from jax.experimental.pallas import tpu as pltpu
from jax.sharding import PartitionSpec as P

F32 = jnp.float32
BF16 = jnp.bfloat16
LANES = 128
VMEM_BYTES = 36 * 2**20
VMEM_SMALL = 20 * 2**20


def dft_tables(size):
    half = size // 2
    index = np.arange(size)
    angle = (index[:, None] * index[None, :] % size) * (2.0 * math.pi / size)
    scale = 1.0 / math.sqrt(size)
    cosine = (np.cos(angle) * scale).astype(ml_dtypes.bfloat16)
    sine = (np.sin(angle) * scale).astype(ml_dtypes.bfloat16)
    tables = []
    for parity in (0, 1):
        c, s = cosine[:half, parity::2], sine[:half, parity::2]
        tables.append(np.block([[c, -s], [s, c]]))
    order = np.zeros((size, size), ml_dtypes.bfloat16)
    order[2 * index[:half], index[:half]] = 1
    order[2 * index[:half] + 1, half + index[:half]] = 1
    even, odd = tables
    return jnp.asarray(np.stack([even, odd, even.T, odd.T, order, order.T]))


def dot(left, right):
    return jnp.dot(left, right, preferred_element_type=F32)


def fractions(code):
    return (code // 4).astype(F32) * 0.25, (code % 4).astype(F32) * 0.25


def in_stage(places, slot, bounds, stage, size):
    end = places[1, slot] + size + 1
    here = end <= bounds[stage + 1]
    if stage > 0:
        here = jnp.logical_and(here, end > bounds[stage])
    return jnp.logical_and(slot < places[3, 0], here)


def project_kernel(size, width, bounds, stage, places, *refs):
    first_stage, last_stage = stage == 0, stage == len(bounds) - 2
    refs = list(refs)
    own, rim = refs[:2]
    rim_before = None if first_stage else refs[2]
    refs = refs[2:] if first_stage else refs[3:]
    probe_in, measured_in, tables_in = refs[:3]
    refs = refs[3:]
    if not first_stage:
        moved_in, sums_in = refs[:2]
        refs = refs[2:]
    moved, grads = refs[:2]
    refs = refs[2:]
    sums_out = refs.pop(0)
    cells, mixed, patch, folded, half_u, half_v, far, error, back, probe, measured, tables, probe_acc, held = refs[:14]
    sems, slot_sems = refs[14:16]
    if last_stage and not first_stage:
        sums, given = refs[16:]
    elif last_stage:
        given = refs[16]
    even, odd, even_t, odd_t, order, order_t = [tables.at[i] for i in range(6)]
    half = size // 2
    modes = probe.shape[0]
    slots = measured.shape[0]
    rows = own.shape[0]
    low, high = bounds[stage], bounds[stage + 1]
    base = 0 if first_stage else low - size
    extent = high - base
    count = places[3, 0]
    copies = []

    def load(source, target):
        copies.append(pltpu.make_async_copy(source, target, sems.at[len(copies)]))

    for part in range(2):
        load(
            own.at[:, pl.ds(part * width + base, extent)],
            cells.at[pl.ds(0, rows), pl.ds(part * extent, extent)],
        )
        load(
            rim.at[:, pl.ds(part * (high - low), high - low)],
            cells.at[pl.ds(rows, size), pl.ds(part * extent + low - base, high - low)],
        )
        if not first_stage:
            before = low - bounds[stage - 1]
            load(
                rim_before.at[:, pl.ds((part + 1) * before - size, size)],
                cells.at[pl.ds(rows, size), pl.ds(part * extent, size)],
            )
    n_cells = len(copies)
    load(tables_in, tables)
    load(probe_in, probe)
    load(measured_in, measured)
    n_later = len(copies)
    if not first_stage:
        load(sums_in, sums if last_stage else probe_acc)
    for copy in copies:
        copy.start()
    if last_stage or first_stage:
        probe_acc[...] = jnp.zeros_like(probe_acc)
    cells[rows + size :] = jnp.zeros((cells.shape[0] - rows - size, cells.shape[1]), BF16)
    for slot in range(slots):
        for axis in range(2):
            moved[axis, slot] = 0.0 if first_stage else moved_in[axis, slot]
    for copy in copies[:n_cells]:
        copy.wait()

    def wait_later():
        for copy in copies[n_cells : n_later if last_stage else len(copies)]:
            copy.wait()

    def mine(slot):
        return in_stage(places, slot, bounds, stage, size)

    def sent_out(slot):
        return pltpu.make_async_copy(held.at[slot], grads.at[slot], slot_sems.at[slot])

    first_slot = jnp.int32(slots)
    for slot in reversed(range(slots)):
        first_slot = jnp.where(mine(slot), slot, first_slot)

    block = 16
    blocks = size // block
    lift_rows = half + 8
    lift_from = half + 32

    def one_slot(slot):
        top = places[0, slot]
        left = places[1, slot]
        frac_y, frac_x = fractions(places[2, slot])
        row0 = pl.multiple_of((top // 16) * 16, 16)
        col0 = pl.multiple_of((left // LANES) * LANES - base, LANES)
        down = top - row0
        across = left - base - col0
        source = lax.broadcasted_iota(jnp.int32, (2 * LANES, LANES), 0)
        target = lax.broadcasted_iota(jnp.int32, (2 * LANES, LANES), 1) + across
        here = (source == target).astype(F32)
        after = (source == target + 1).astype(F32)
        blend = jnp.concatenate([(1.0 - frac_x) * here + frac_x * after, after - here], axis=1).astype(BF16)
        source = lax.broadcasted_iota(jnp.int32, (lift_rows, lift_from), 1)
        target = lax.broadcasted_iota(jnp.int32, (lift_rows, lift_from), 0) + down
        lifts = [(source == target + shift).astype(F32).astype(BF16) for shift in (0, 8)]
        for part in range(2):
            start = pl.multiple_of(col0 + part * extent, LANES)
            for piece in range(2):
                taken = pl.ds(pl.multiple_of(row0 + piece * half, 16), lift_from)
                window = dot(lifts[piece], cells[taken, pl.ds(start, size + LANES)]).astype(BF16)
                for h in range(size // LANES):
                    mixed[part, pl.ds(piece * lift_rows, lift_rows), h * size : (h + 1) * size] = dot(
                        window[:, h * LANES : (h + 2) * LANES], blend
                    )
        for part in range(2):
            for h in range(size // LANES):
                cols = slice(h * size, h * size + LANES)
                for b in range(0, size, block):
                    upper = mixed[part, pl.ds(b, block), cols]
                    lower = mixed[part, pl.ds(b + 1, block), cols]
                    to = slice(part * size + h * LANES, part * size + (h + 1) * LANES)
                    patch[pl.ds(b, block), to] = (1.0 - frac_y) * upper + frac_y * lower
        pl.when(slot == first_slot)(wait_later)

        for mode in range(modes):
            for b in range(blocks):
                at = slice(b * block, (b + 1) * block)
                spot = (2 * b if b < blocks // 2 else 2 * b + 1 - blocks) * block
                to = slice(spot, spot + block)
                preal, pimag = probe[mode, at, :size], probe[mode, at, size:]
                oreal, oimag = patch[at, :size], patch[at, size:]
                wreal = preal * oreal - pimag * oimag
                wimag = preal * oimag + pimag * oreal
                for part, wave in enumerate((wreal, wimag)):
                    folded[mode, to, part * half : (part + 1) * half] = (wave[:, :half] + wave[:, half:]).astype(BF16)
                    folded[mode, to, size + part * half : size + (part + 1) * half] = (
                        wave[:, :half] - wave[:, half:]
                    ).astype(BF16)
        for mode in range(modes):
            for k, table in enumerate((even, odd)):
                out = dot(folded[mode, :, k * size : (k + 1) * size], table[...])
                for b in range(blocks // 2):
                    upper = out[2 * b * block : (2 * b + 1) * block]
                    lower = out[(2 * b + 1) * block : (2 * b + 2) * block]
                    plus, minus = (upper + lower).astype(BF16), (upper - lower).astype(BF16)
                    for part in range(2):
                        to = slice(part * half + b * block, part * half + (b + 1) * block)
                        cols = slice(part * half, (part + 1) * half)
                        half_u[mode, to, k * half : (k + 1) * half] = plus[:, cols]
                        half_v[mode, to, k * half : (k + 1) * half] = minus[:, cols]
        for mode in range(modes):
            far[mode, 0] = dot(even_t[...], half_u[mode])
            far[mode, 1] = dot(odd_t[...], half_v[mode])

        amplitude = dot(dot(order_t[...], measured[slot]).astype(BF16), order[...])
        for k in range(2):
            for b in range(0, half, block):
                pieces = [
                    [far[mode, k, part * half + b : part * half + b + block, :] for part in range(2)]
                    for mode in range(modes)
                ]
                power = sum(p * p for pair in pieces for p in pair)
                level = amplitude[k * half + b : k * half + b + block]
                ratio = 1.0 - level / jnp.maximum(jnp.sqrt(power), 0.5)
                for mode in range(modes):
                    for part in range(2):
                        to = slice(part * half + b, part * half + b + block)
                        error[mode, k, to, :] = (pieces[mode][part] * ratio).astype(BF16)

        for mode in range(modes):
            first = dot(even[...], error[mode, 0])
            second = dot(odd[...], error[mode, 1])
            plus, minus = (first + second).astype(BF16), (first - second).astype(BF16)
            for part in range(2):
                for b in range(blocks):
                    pick = part * half + (b % (blocks // 2)) * block
                    piece = (plus if b < blocks // 2 else minus)[pick : pick + block]
                    to = slice((b * modes + mode) * block, (b * modes + mode + 1) * block)
                    for c in range(2):
                        cols = slice(c * size + part * half, c * size + (part + 1) * half)
                        back[to, cols] = piece[:, c * half : (c + 1) * half]

        total_y = jnp.zeros((block, half), F32)
        total_x = jnp.zeros((block, half), F32)
        group = size // (modes * block)
        for g in range(blocks // group):
            span = slice(g * size, (g + 1) * size)
            first = dot(back[span, :size], even_t[...])
            second = dot(back[span, size:], odd_t[...])
            for r in range(group):
                at = slice((g * group + r) * block, (g * group + r + 1) * block)
                below = slice(at.start + 1, at.stop + 1)
                for h in range(2):
                    re = slice(h * half, (h + 1) * half)
                    im = slice(size + h * half, size + (h + 1) * half)
                    oreal, oimag = patch[at, re], patch[at, im]
                    greal = jnp.zeros((block, half), F32)
                    gimag = jnp.zeros((block, half), F32)
                    for mode in range(modes):
                        part = slice((r * modes + mode) * block, (r * modes + mode + 1) * block)
                        piece = first[part] + second[part] if h == 0 else first[part] - second[part]
                        ureal, uimag = piece[:, :half], piece[:, half:]
                        preal, pimag = probe[mode, at, re], probe[mode, at, im]
                        greal += preal * ureal + pimag * uimag
                        gimag += preal * uimag - pimag * ureal
                        probe_acc[mode, at, re] += oreal * ureal + oimag * uimag
                        probe_acc[mode, at, im] += oreal * uimag - oimag * ureal
                    held[slot, at, re] = greal.astype(BF16)
                    held[slot, at, im] = gimag.astype(BF16)
                    for part, grad in enumerate((greal, gimag)):
                        cols = slice(h * size, h * size + LANES)
                        total_y += grad * (mixed[part, below, cols] - mixed[part, at, cols])
                        cols = slice(h * size + LANES, (h + 1) * size)
                        total_x += grad * ((1.0 - frac_y) * mixed[part, at, cols] + frac_y * mixed[part, below, cols])
        moved[0, slot] = jnp.sum(total_y) / size
        moved[1, slot] = jnp.sum(total_x) / size

        sent_out(slot).start()

    @pl.loop(0, slots)
    def _(slot):
        pl.when(mine(slot))(functools.partial(one_slot, slot))

    pl.when(first_slot == slots)(wait_later)
    outs = []

    def store(source, target):
        outs.append(pltpu.make_async_copy(source, target, sems.at[len(outs)]))
        outs[-1].start()

    if last_stage:
        if first_stage:
            given[...] = probe_acc[...].astype(BF16)
        else:
            copies[-1].wait()
            for mode in range(modes):
                given[mode] = (probe_acc[mode] + sums[mode]).astype(BF16)
        store(given, sums_out)
    else:
        store(probe_acc, sums_out)

    @pl.loop(0, slots)
    def _(slot):
        @pl.when(mine(slot))
        def _():
            sent_out(slot).wait()

    for out in outs:
        out.wait()


def project(stage, bounds, places, own, rims, probe, measured, tables, width, carried):
    slots, size, _ = measured.shape
    modes = probe.shape[0]
    rows = own.shape[0]
    smem = pl.BlockSpec(memory_space=pltpu.SMEM)
    hbm = pl.BlockSpec(memory_space=pl.ANY)
    first_stage, last_stage = stage == 0, stage == len(bounds) - 2
    low, high = bounds[stage], bounds[stage + 1]
    extent = high - (0 if first_stage else low - size)
    inputs = [places, own, rims[stage]] + ([] if first_stage else [rims[stage - 1]]) + [probe, measured, tables]
    specs = [smem] + [hbm] * (len(inputs) - 1)
    outs = [
        jax.ShapeDtypeStruct((2, slots), F32),
        jax.ShapeDtypeStruct((slots, size, 2 * size), BF16),
        jax.ShapeDtypeStruct(probe.shape, BF16 if last_stage else F32),
    ]
    if not first_stage:
        inputs += list(carried)
        specs += [smem, hbm]
    scratch = [
        pltpu.VMEM((rows + size + 32, 2 * extent), BF16),
        pltpu.VMEM((2, size + 16, 2 * size), F32),
        pltpu.VMEM((size, 2 * size), F32),
        pltpu.VMEM((modes, size, 2 * size), BF16),
        pltpu.VMEM((modes, size, size), BF16),
        pltpu.VMEM((modes, size, size), BF16),
        pltpu.VMEM((modes, 2, size, size), F32),
        pltpu.VMEM((modes, 2, size, size), BF16),
        pltpu.VMEM((modes * size, 2 * size), BF16),
        pltpu.VMEM(probe.shape, F32),
        pltpu.VMEM(measured.shape, BF16),
        pltpu.VMEM(tables.shape, BF16),
        pltpu.VMEM(probe.shape, F32),
        pltpu.VMEM((slots, size, 2 * size), BF16),
        pltpu.SemaphoreType.DMA((12,)),
        pltpu.SemaphoreType.DMA((slots,)),
    ]
    if last_stage and not first_stage:
        scratch.append(pltpu.VMEM(probe.shape, F32))
    if last_stage:
        scratch.append(pltpu.VMEM(probe.shape, BF16))
    return pl.pallas_call(
        functools.partial(project_kernel, size, width, bounds, stage),
        in_specs=specs,
        out_specs=[smem] + [hbm] * (len(outs) - 1),
        out_shape=outs,
        scratch_shapes=scratch,
        compiler_params=pltpu.CompilerParams(vmem_limit_bytes=VMEM_BYTES),
        cost_estimate=pl.CostEstimate(flops=8 * 10**9, bytes_accessed=16 * 2**20, transcendentals=0),
        name=f"project_{stage}",
    )(*inputs)


def settle_kernel(size, bounds, low, high, shift, places, *refs):
    grads = refs[: len(refs) - 5]
    out, total, held, sems, out_sems = refs[len(refs) - 5 :]
    slots = held.shape[0]
    reach = size + LANES
    base = max(low - size, 0)
    extent = total.shape[1] // 2
    length = high - low

    def taken(stage, slot):
        left = places[1, slot]
        within = jnp.logical_and(left < high, left + size + 1 > low)
        return jnp.logical_and(within, in_stage(places, slot, bounds, stage, size))

    def fetch(stage, slot):
        return pltpu.make_async_copy(grads[stage].at[slot], held.at[slot], sems.at[slot])

    for stage in range(len(grads)):

        @pl.loop(0, slots)
        def _(slot, stage=stage):
            @pl.when(taken(stage, slot))
            def _():
                fetch(stage, slot).start()

    total[...] = jnp.zeros_like(total)

    def one_slot(stage, slot):
        left = places[1, slot]
        frac_y, frac_x = fractions(places[2, slot])
        col0 = (left // LANES) * LANES
        ahead = lax.broadcasted_iota(jnp.int32, (size, reach), 1) - lax.broadcasted_iota(jnp.int32, (size, reach), 0)
        ahead = ahead - (left - col0)
        along = jnp.where(ahead == 0, 1.0 - frac_x, jnp.where(ahead == 1, frac_x, 0.0)).astype(BF16)
        ahead = lax.broadcasted_iota(jnp.int32, (size, size), 0) - lax.broadcasted_iota(jnp.int32, (size, size), 1)
        ahead = ahead - (places[0, slot] - shift)
        down = jnp.where(ahead == 0, 1.0 - frac_y, jnp.where(ahead == 1, frac_y, 0.0)).astype(BF16)
        fetch(stage, slot).wait()
        for part in range(2):
            wide = dot(held[slot, :, part * size : (part + 1) * size], along).astype(BF16)
            start = pl.multiple_of(col0 - base + part * extent, LANES)
            total[:, pl.ds(start, reach)] += dot(down, wide)

    for stage in range(len(grads)):

        @pl.loop(0, slots)
        def _(slot, stage=stage):
            pl.when(taken(stage, slot))(functools.partial(one_slot, stage, slot))

    copies = []
    for part in range(2):
        here = slice(part * extent + low - base, part * extent + low - base + length)
        there = slice(part * length, (part + 1) * length)
        if out.dtype == F32:
            copies.append(
                pltpu.make_async_copy(
                    total.at[:, pl.ds(here.start, length)], out.at[:, pl.ds(there.start, length)], out_sems.at[part]
                )
            )
            copies[-1].start()
        else:
            out[:, there] = total[:, here].astype(out.dtype)
    for copy in copies:
        copy.wait()


def settle(places, grads, bounds, low, high, shift, dtype, width, name):
    slots, size, _ = grads[0].shape
    base, end = max(low - size, 0), min(high + size, width)
    hbm = pl.BlockSpec(memory_space=pl.ANY)
    return pl.pallas_call(
        functools.partial(settle_kernel, size, bounds, low, high, shift),
        in_specs=[pl.BlockSpec(memory_space=pltpu.SMEM)] + [hbm] * len(grads),
        out_specs=hbm if dtype == F32 else pl.BlockSpec(memory_space=pltpu.VMEM),
        out_shape=jax.ShapeDtypeStruct((size, 2 * (high - low)), dtype),
        scratch_shapes=[
            pltpu.VMEM((size, 2 * (end - base)), F32),
            pltpu.VMEM(grads[0].shape, BF16),
            pltpu.SemaphoreType.DMA((slots,)),
            pltpu.SemaphoreType.DMA((2,)),
        ],
        compiler_params=pltpu.CompilerParams(vmem_limit_bytes=VMEM_SMALL),
        cost_estimate=pl.CostEstimate(flops=10**9, bytes_accessed=8 * 2**20, transcendentals=0),
        name=name,
    )(places, *grads)


def finish_kernel(edges, n, own, *refs):
    aboves, out = refs[:n], refs[n]
    wides, adds, sems = refs[n + 1 : 2 * n + 1], refs[2 * n + 1 : 3 * n + 1], refs[3 * n + 1]
    width = out.shape[2]
    loads, outs = [], []

    def copied(source, target, to):
        to.append(pltpu.make_async_copy(source, target, sems.at[len(loads) + len(outs)]))
        to[-1].start()

    for i in range(n):
        length = edges[i + 1] - edges[i]
        for part in range(2):
            copied(
                own.at[:, pl.ds(part * width + edges[i], length)], wides[i].at[:, pl.ds(part * length, length)], loads
            )
        copied(aboves[i], adds[i], loads)
    for i in range(n):
        for copy in loads[3 * i : 3 * i + 3]:
            copy.wait()
        length = edges[i + 1] - edges[i]
        for part in range(2):
            cols = slice(part * length, (part + 1) * length)
            wides[i][:, cols] += adds[i][:, cols].astype(F32)
            copied(wides[i].at[:, pl.ds(part * length, length)], out.at[:, part, pl.ds(edges[i], length)], outs)
    for copy in outs:
        copy.wait()


def finish(own, aboves, edges, width):
    n = len(aboves)
    hbm = pl.BlockSpec(memory_space=pl.ANY)
    return pl.pallas_call(
        functools.partial(finish_kernel, edges, n),
        in_specs=[hbm] * (n + 1),
        out_specs=hbm,
        out_shape=jax.ShapeDtypeStruct((own.shape[0], 2, width), F32),
        scratch_shapes=[pltpu.VMEM(x.shape, F32) for x in aboves]
        + [pltpu.VMEM(x.shape, BF16) for x in aboves]
        + [pltpu.SemaphoreType.DMA((5 * n,))],
        compiler_params=pltpu.CompilerParams(vmem_limit_bytes=VMEM_SMALL),
        cost_estimate=pl.CostEstimate(flops=10**6, bytes_accessed=10 * 2**20, transcendentals=0),
        name="finish",
    )(own, *aboves)


def passed_along(x, axis, by):
    length = lax.axis_size(axis)
    pairs = [(i, i + by) for i in range(length) if 0 <= i + by < length]
    return lax.ppermute(x, axis, pairs)


def unpack_kernel(order, *refs):
    n = (len(refs) - 4) // 2
    out, wide, narrow, sems = refs[2 * n :]
    rows = wide.shape[1]
    size = out.shape[1]
    span = min(rows, size)
    for core in range(2):

        @pl.when(order[n] == core)
        def _():
            for i in range(n):
                pltpu.make_async_copy(refs[core * n + i], narrow.at[i], sems.at[0, i]).start()

    copies = []
    for i in range(n):
        pltpu.make_async_copy(refs[i], narrow.at[i], sems.at[0, i]).wait()
        wide[i] = narrow[i].astype(F32)
        for j in range(rows // span):
            line = order[i] * rows + j * span
            mode = line // size
            at = pl.multiple_of(line % size, 8)
            for part in range(2):
                copies.append(
                    pltpu.make_async_copy(
                        wide.at[i, pl.ds(j * span, span), pl.ds(part * size, size)],
                        out.at[mode, pl.ds(at, span), part, :],
                        sems.at[1, len(copies)],
                    )
                )
                copies[-1].start()
    for copy in copies:
        copy.wait()


def unpacked(pieces, others, order, shape):
    n = len(pieces)
    rows, columns = pieces[0].shape
    hbm = pl.BlockSpec(memory_space=pl.ANY)
    return pl.pallas_call(
        unpack_kernel,
        in_specs=[pl.BlockSpec(memory_space=pltpu.SMEM)] + [hbm] * (2 * n),
        out_specs=hbm,
        out_shape=jax.ShapeDtypeStruct(shape, F32),
        scratch_shapes=[
            pltpu.VMEM((n, rows, columns), F32),
            pltpu.VMEM((n, rows, columns), BF16),
            pltpu.SemaphoreType.DMA((2, 2 * n * max(1, rows // shape[1]))),
        ],
        compiler_params=pltpu.CompilerParams(vmem_limit_bytes=VMEM_SMALL),
        cost_estimate=pl.CostEstimate(flops=10**6, bytes_accessed=4 * 2**20, transcendentals=0),
        name="unpack",
    )(order, *pieces, *others)


def near_chips(axis):
    return min(4, lax.axis_size(axis) // 2)


def piece_order(axis):
    near = near_chips(axis)
    me = lax.axis_index(axis)
    core, spot = me % 2, me // 2 % near
    return jnp.stack([spot ^ s for s in range(near)] + [core])


def hop(axis, shift, stride):
    return [(i, i ^ (2 * stride * shift)) for i in range(0, lax.axis_size(axis), 2)]


def summed(given, axis, shape, order, beside, between):
    length = lax.axis_size(axis)
    near = near_chips(axis)
    far = length // 2 // near
    inward = [(i + 1, i) for i in range(0, length, 2)]
    outward = [(i, i + 1) for i in range(0, length, 2)]
    modes, size, columns = given.shape
    spot = lax.axis_index(axis) // 2 % near
    sibling = beside(lax.ppermute(given, axis, inward))
    parts = (given.astype(F32) + sibling.astype(F32)).astype(BF16).reshape(near, modes * size // near, columns)
    got = [
        lax.ppermute(lax.dynamic_index_in_dim(parts, spot ^ s, 0, False), axis, hop(axis, s, 1)) for s in range(1, near)
    ]
    total = lax.dynamic_index_in_dim(parts, spot, 0, False).astype(F32)
    for piece in got:
        total = total + piece.astype(F32)
    sent = total.astype(BF16)
    others = [lax.ppermute(sent, axis, hop(axis, s, near)) for s in range(1, far)]
    if others:
        others[0] = between(others[0])
    for piece in others:
        total = total + piece.astype(F32)
    total = total.astype(BF16)
    pieces = [total] + [lax.ppermute(total, axis, hop(axis, s, 1)) for s in range(1, near)]
    others = [lax.ppermute(piece, axis, outward) for piece in pieces]
    return unpacked(pieces, others, order, shape)


def column_bounds(width, shares):
    return tuple([0] + [round(width * share / LANES) * LANES for share in shares] + [width])


def shards(object_tiles, probe, measured, offset_row, offset_col, subpixel, live_count):
    rows, _, width = object_tiles.shape
    modes, size = probe.shape[:2]
    tables = dft_tables(size)
    bounds = column_bounds(width, (0.5625,))
    stages = len(bounds) - 1
    rims = [
        passed_along(object_tiles[:size, :, low:high].reshape(size, 2 * (high - low)), "row", -1)
        for low, high in zip(bounds[:-1], bounds[1:])
    ]
    core = lax.axis_index("row") % 2
    places = jnp.stack(
        [offset_row, offset_col, subpixel] + [jnp.broadcast_to(x, offset_row.shape) for x in (live_count, core)]
    )
    places, order = lax.optimization_barrier((places, piece_order("row")))
    own = object_tiles.reshape(rows, 2 * width)
    flat = probe.reshape(modes, size, 2 * size)
    carried = None
    grads = []
    for stage in range(stages):
        moved, grad, *rest = project(stage, bounds, places, own, rims, flat, measured, tables, width, carried)
        grads.append(grad)
        carried = [moved] + rest
    given = carried[1]
    below = settle(places, grads, bounds, 0, width, size, BF16, width, "below_rows")
    held = {}

    def beside(x):
        x, held["below"] = lax.optimization_barrier((x, below))
        return x

    def between(x):
        own_rows = settle(places, grads, bounds, 0, width, 0, F32, width, "own_rows")
        x, held["own"] = lax.optimization_barrier((x, own_rows))
        return x

    probe_grad = summed(given, "row", probe.shape, order, beside, between)
    above = passed_along(held["below"], "row", 1)
    object_grad = finish(held["own"], [above], (0, width), width)
    return object_grad, probe_grad, moved


def solution(mesh):
    in_specs = (
        P(("groups", "row"), None, None),
        P(),
        P(("groups", "row"), None, None),
        P(("groups", "row")),
        P(("groups", "row")),
        P(("groups", "row")),
        P(("groups", "row")),
    )
    out_specs = (
        P(("groups", "row"), None, None),
        P("groups", None, None, None),
        P(None, ("groups", "row")),
    )
    return jax.shard_map(shards, mesh=mesh, in_specs=in_specs, out_specs=out_specs, check_vma=False)
```

```python
import functools
import math

import jax
import jax.numpy as jnp
import ml_dtypes
import numpy as np
from jax import lax
from jax.experimental import pallas as pl
from jax.experimental.pallas import tpu as pltpu
from jax.sharding import PartitionSpec as P

F32 = jnp.float32
BF16 = jnp.bfloat16
LANES = 128
VMEM_BYTES = 26 * 2**20
VMEM_SMALL = 16 * 2**20


def dft_tables(size):
    half = size // 2
    index = np.arange(size)
    angle = (index[:, None] * index[None, :] % size) * (2.0 * math.pi / size)
    scale = 1.0 / math.sqrt(size)
    cosine = (np.cos(angle) * scale).astype(ml_dtypes.bfloat16)
    sine = (np.sin(angle) * scale).astype(ml_dtypes.bfloat16)
    tables = []
    for parity in (0, 1):
        c, s = cosine[:half, parity::2], sine[:half, parity::2]
        tables.append(np.block([[c, -s], [s, c]]))
    order = np.zeros((size, size), ml_dtypes.bfloat16)
    order[2 * index[:half], index[:half]] = 1
    order[2 * index[:half] + 1, half + index[:half]] = 1
    even, odd = tables
    return jnp.asarray(np.stack([even, odd, even.T, odd.T, order, order.T]))


def dot(left, right):
    return jnp.dot(left, right, preferred_element_type=F32)


def fractions(code):
    return (code // 4).astype(F32) * 0.25, (code % 4).astype(F32) * 0.25


def in_stage(places, slot, bounds, stage, size):
    end = places[1, slot] + size + 1
    here = end <= bounds[stage + 1]
    if stage > 0:
        here = jnp.logical_and(here, end > bounds[stage])
    return jnp.logical_and(slot < places[3, 0], here)


def project_kernel(size, width, bounds, stage, places, *refs):
    first_stage, last_stage = stage == 0, stage == len(bounds) - 2
    refs = list(refs)
    own, rim = refs[:2]
    rim_before = None if first_stage else refs[2]
    refs = refs[2:] if first_stage else refs[3:]
    probe_in, measured_in, tables_in = refs[:3]
    refs = refs[3:]
    if not first_stage:
        moved_in, sums_in = refs[:2]
        refs = refs[2:]
    moved, grads = refs[:2]
    refs = refs[2:]
    sums_out = refs.pop(0)
    cells, mixed, patch, folded, half_u, half_v, far, error, back, probe, measured, tables, probe_acc, held = refs[:14]
    sems, slot_sems = refs[14:16]
    if last_stage and not first_stage:
        sums, given = refs[16:]
    elif last_stage:
        given = refs[16]
    even, odd, even_t, odd_t, order, order_t = [tables.at[i] for i in range(6)]
    half = size // 2
    modes = probe.shape[0]
    slots = measured.shape[0]
    rows = own.shape[0]
    low, high = bounds[stage], bounds[stage + 1]
    base = 0 if first_stage else low - size
    extent = high - base
    count = places[3, 0]
    copies = []

    def load(source, target):
        copies.append(pltpu.make_async_copy(source, target, sems.at[len(copies)]))

    for part in range(2):
        load(
            own.at[:, pl.ds(part * width + base, extent)],
            cells.at[pl.ds(0, rows), pl.ds(part * extent, extent)],
        )
        load(
            rim.at[:, pl.ds(part * (high - low), high - low)],
            cells.at[pl.ds(rows, size), pl.ds(part * extent + low - base, high - low)],
        )
        if not first_stage:
            before = low - bounds[stage - 1]
            load(
                rim_before.at[:, pl.ds((part + 1) * before - size, size)],
                cells.at[pl.ds(rows, size), pl.ds(part * extent, size)],
            )
    n_cells = len(copies)
    load(tables_in, tables)
    load(probe_in, probe)
    load(measured_in, measured)
    n_later = len(copies)
    if not first_stage:
        load(sums_in, sums if last_stage else probe_acc)
    for copy in copies:
        copy.start()
    if last_stage or first_stage:
        probe_acc[...] = jnp.zeros_like(probe_acc)
    cells[rows + size :] = jnp.zeros((cells.shape[0] - rows - size, cells.shape[1]), BF16)
    for slot in range(slots):
        for axis in range(2):
            moved[axis, slot] = 0.0 if first_stage else moved_in[axis, slot]
    for copy in copies[:n_cells]:
        copy.wait()

    def wait_later():
        for copy in copies[n_cells : n_later if last_stage else len(copies)]:
            copy.wait()

    def mine(slot):
        return in_stage(places, slot, bounds, stage, size)

    def sent_out(slot):
        return pltpu.make_async_copy(held.at[slot], grads.at[slot], slot_sems.at[slot])

    first_slot = jnp.int32(slots)
    for slot in reversed(range(slots)):
        first_slot = jnp.where(mine(slot), slot, first_slot)

    block = 16
    blocks = size // block
    lift_rows = half + 8
    lift_from = half + 32

    def one_slot(slot):
        top = places[0, slot]
        left = places[1, slot]
        frac_y, frac_x = fractions(places[2, slot])
        row0 = pl.multiple_of((top // 16) * 16, 16)
        col0 = pl.multiple_of((left // LANES) * LANES - base, LANES)
        down = top - row0
        across = left - base - col0
        source = lax.broadcasted_iota(jnp.int32, (2 * LANES, LANES), 0)
        target = lax.broadcasted_iota(jnp.int32, (2 * LANES, LANES), 1) + across
        here = (source == target).astype(F32)
        after = (source == target + 1).astype(F32)
        blend = jnp.concatenate([(1.0 - frac_x) * here + frac_x * after, after - here], axis=1).astype(BF16)
        source = lax.broadcasted_iota(jnp.int32, (lift_rows, lift_from), 1)
        target = lax.broadcasted_iota(jnp.int32, (lift_rows, lift_from), 0) + down
        lifts = [(source == target + shift).astype(F32).astype(BF16) for shift in (0, 8)]
        for part in range(2):
            start = pl.multiple_of(col0 + part * extent, LANES)
            for piece in range(2):
                taken = pl.ds(pl.multiple_of(row0 + piece * half, 16), lift_from)
                window = dot(lifts[piece], cells[taken, pl.ds(start, size + LANES)]).astype(BF16)
                for h in range(size // LANES):
                    mixed[part, pl.ds(piece * lift_rows, lift_rows), h * size : (h + 1) * size] = dot(
                        window[:, h * LANES : (h + 2) * LANES], blend
                    )
        for part in range(2):
            for h in range(size // LANES):
                cols = slice(h * size, h * size + LANES)
                for b in range(0, size, block):
                    upper = mixed[part, pl.ds(b, block), cols]
                    lower = mixed[part, pl.ds(b + 1, block), cols]
                    to = slice(part * size + h * LANES, part * size + (h + 1) * LANES)
                    patch[pl.ds(b, block), to] = (1.0 - frac_y) * upper + frac_y * lower
        pl.when(slot == first_slot)(wait_later)

        for mode in range(modes):
            for b in range(blocks):
                at = slice(b * block, (b + 1) * block)
                spot = (2 * b if b < blocks // 2 else 2 * b + 1 - blocks) * block
                to = slice(spot, spot + block)
                preal, pimag = probe[mode, at, :size], probe[mode, at, size:]
                oreal, oimag = patch[at, :size], patch[at, size:]
                wreal = preal * oreal - pimag * oimag
                wimag = preal * oimag + pimag * oreal
                for part, wave in enumerate((wreal, wimag)):
                    folded[mode, to, part * half : (part + 1) * half] = (wave[:, :half] + wave[:, half:]).astype(BF16)
                    folded[mode, to, size + part * half : size + (part + 1) * half] = (
                        wave[:, :half] - wave[:, half:]
                    ).astype(BF16)
        for mode in range(modes):
            for k, table in enumerate((even, odd)):
                out = dot(folded[mode, :, k * size : (k + 1) * size], table[...])
                for b in range(blocks // 2):
                    upper = out[2 * b * block : (2 * b + 1) * block]
                    lower = out[(2 * b + 1) * block : (2 * b + 2) * block]
                    plus, minus = (upper + lower).astype(BF16), (upper - lower).astype(BF16)
                    for part in range(2):
                        to = slice(part * half + b * block, part * half + (b + 1) * block)
                        cols = slice(part * half, (part + 1) * half)
                        half_u[mode, to, k * half : (k + 1) * half] = plus[:, cols]
                        half_v[mode, to, k * half : (k + 1) * half] = minus[:, cols]
        for mode in range(modes):
            far[mode, 0] = dot(even_t[...], half_u[mode])
            far[mode, 1] = dot(odd_t[...], half_v[mode])

        amplitude = dot(dot(order_t[...], measured[slot]).astype(BF16), order[...])
        for k in range(2):
            for b in range(0, half, block):
                pieces = [
                    [far[mode, k, part * half + b : part * half + b + block, :] for part in range(2)]
                    for mode in range(modes)
                ]
                power = sum(p * p for pair in pieces for p in pair)
                level = amplitude[k * half + b : k * half + b + block]
                ratio = 1.0 - level / jnp.maximum(jnp.sqrt(power), 0.5)
                for mode in range(modes):
                    for part in range(2):
                        to = slice(part * half + b, part * half + b + block)
                        error[mode, k, to, :] = (pieces[mode][part] * ratio).astype(BF16)

        for mode in range(modes):
            first = dot(even[...], error[mode, 0])
            second = dot(odd[...], error[mode, 1])
            plus, minus = (first + second).astype(BF16), (first - second).astype(BF16)
            for part in range(2):
                for b in range(blocks):
                    pick = part * half + (b % (blocks // 2)) * block
                    piece = (plus if b < blocks // 2 else minus)[pick : pick + block]
                    to = slice((b * modes + mode) * block, (b * modes + mode + 1) * block)
                    for c in range(2):
                        cols = slice(c * size + part * half, c * size + (part + 1) * half)
                        back[to, cols] = piece[:, c * half : (c + 1) * half]

        total_y = jnp.zeros((block, half), F32)
        total_x = jnp.zeros((block, half), F32)
        group = size // (modes * block)
        for g in range(blocks // group):
            span = slice(g * size, (g + 1) * size)
            first = dot(back[span, :size], even_t[...])
            second = dot(back[span, size:], odd_t[...])
            for r in range(group):
                at = slice((g * group + r) * block, (g * group + r + 1) * block)
                below = slice(at.start + 1, at.stop + 1)
                for h in range(2):
                    re = slice(h * half, (h + 1) * half)
                    im = slice(size + h * half, size + (h + 1) * half)
                    oreal, oimag = patch[at, re], patch[at, im]
                    greal = jnp.zeros((block, half), F32)
                    gimag = jnp.zeros((block, half), F32)
                    for mode in range(modes):
                        part = slice((r * modes + mode) * block, (r * modes + mode + 1) * block)
                        piece = first[part] + second[part] if h == 0 else first[part] - second[part]
                        ureal, uimag = piece[:, :half], piece[:, half:]
                        preal, pimag = probe[mode, at, re], probe[mode, at, im]
                        greal += preal * ureal + pimag * uimag
                        gimag += preal * uimag - pimag * ureal
                        probe_acc[mode, at, re] += oreal * ureal + oimag * uimag
                        probe_acc[mode, at, im] += oreal * uimag - oimag * ureal
                    held[slot, at, re] = greal.astype(BF16)
                    held[slot, at, im] = gimag.astype(BF16)
                    for part, grad in enumerate((greal, gimag)):
                        cols = slice(h * size, h * size + LANES)
                        total_y += grad * (mixed[part, below, cols] - mixed[part, at, cols])
                        cols = slice(h * size + LANES, (h + 1) * size)
                        total_x += grad * ((1.0 - frac_y) * mixed[part, at, cols] + frac_y * mixed[part, below, cols])
        moved[0, slot] = jnp.sum(total_y) / size
        moved[1, slot] = jnp.sum(total_x) / size

        sent_out(slot).start()

    @pl.loop(0, slots)
    def _(slot):
        pl.when(mine(slot))(functools.partial(one_slot, slot))

    pl.when(first_slot == slots)(wait_later)
    outs = []

    def store(source, target):
        outs.append(pltpu.make_async_copy(source, target, sems.at[len(outs)]))
        outs[-1].start()

    if last_stage:
        if first_stage:
            given[...] = probe_acc[...].astype(BF16)
        else:
            copies[-1].wait()
            for mode in range(modes):
                given[mode] = (probe_acc[mode] + sums[mode]).astype(BF16)
        store(given, sums_out)
    else:
        store(probe_acc, sums_out)

    @pl.loop(0, slots)
    def _(slot):
        @pl.when(mine(slot))
        def _():
            sent_out(slot).wait()

    for out in outs:
        out.wait()


def project(stage, bounds, places, own, rims, probe, measured, tables, width, carried):
    slots, size, _ = measured.shape
    modes = probe.shape[0]
    rows = own.shape[0]
    smem = pl.BlockSpec(memory_space=pltpu.SMEM)
    hbm = pl.BlockSpec(memory_space=pl.ANY)
    first_stage, last_stage = stage == 0, stage == len(bounds) - 2
    low, high = bounds[stage], bounds[stage + 1]
    extent = high - (0 if first_stage else low - size)
    inputs = [places, own, rims[stage]] + ([] if first_stage else [rims[stage - 1]]) + [probe, measured, tables]
    specs = [smem] + [hbm] * (len(inputs) - 1)
    outs = [
        jax.ShapeDtypeStruct((2, slots), F32),
        jax.ShapeDtypeStruct((slots, size, 2 * size), BF16),
        jax.ShapeDtypeStruct(probe.shape, BF16 if last_stage else F32),
    ]
    if not first_stage:
        inputs += list(carried)
        specs += [smem, hbm]
    scratch = [
        pltpu.VMEM((rows + size + 32, 2 * extent), BF16),
        pltpu.VMEM((2, size + 16, 2 * size), F32),
        pltpu.VMEM((size, 2 * size), F32),
        pltpu.VMEM((modes, size, 2 * size), BF16),
        pltpu.VMEM((modes, size, size), BF16),
        pltpu.VMEM((modes, size, size), BF16),
        pltpu.VMEM((modes, 2, size, size), F32),
        pltpu.VMEM((modes, 2, size, size), BF16),
        pltpu.VMEM((modes * size, 2 * size), BF16),
        pltpu.VMEM(probe.shape, F32),
        pltpu.VMEM(measured.shape, BF16),
        pltpu.VMEM(tables.shape, BF16),
        pltpu.VMEM(probe.shape, F32),
        pltpu.VMEM((slots, size, 2 * size), BF16),
        pltpu.SemaphoreType.DMA((12,)),
        pltpu.SemaphoreType.DMA((slots,)),
    ]
    if last_stage and not first_stage:
        scratch.append(pltpu.VMEM(probe.shape, F32))
    if last_stage:
        scratch.append(pltpu.VMEM(probe.shape, BF16))
    return pl.pallas_call(
        functools.partial(project_kernel, size, width, bounds, stage),
        in_specs=specs,
        out_specs=[smem] + [hbm] * (len(outs) - 1),
        out_shape=outs,
        scratch_shapes=scratch,
        compiler_params=pltpu.CompilerParams(vmem_limit_bytes=VMEM_BYTES),
        cost_estimate=pl.CostEstimate(flops=8 * 10**9, bytes_accessed=16 * 2**20, transcendentals=0),
        name=f"project_{stage}",
    )(*inputs)


def settle_kernel(size, bounds, low, high, shift, places, *refs):
    grads = refs[: len(refs) - 5]
    out, total, held, sems, out_sems = refs[len(refs) - 5 :]
    slots = held.shape[0]
    reach = size + LANES
    base = max(low - size, 0)
    extent = total.shape[1] // 2
    length = high - low

    def taken(stage, slot):
        left = places[1, slot]
        within = jnp.logical_and(left < high, left + size + 1 > low)
        return jnp.logical_and(within, in_stage(places, slot, bounds, stage, size))

    def fetch(stage, slot):
        return pltpu.make_async_copy(grads[stage].at[slot], held.at[slot], sems.at[slot])

    for stage in range(len(grads)):

        @pl.loop(0, slots)
        def _(slot, stage=stage):
            @pl.when(taken(stage, slot))
            def _():
                fetch(stage, slot).start()

    total[...] = jnp.zeros_like(total)

    def one_slot(stage, slot):
        left = places[1, slot]
        frac_y, frac_x = fractions(places[2, slot])
        col0 = (left // LANES) * LANES
        ahead = lax.broadcasted_iota(jnp.int32, (size, reach), 1) - lax.broadcasted_iota(jnp.int32, (size, reach), 0)
        ahead = ahead - (left - col0)
        along = jnp.where(ahead == 0, 1.0 - frac_x, jnp.where(ahead == 1, frac_x, 0.0)).astype(BF16)
        ahead = lax.broadcasted_iota(jnp.int32, (size, size), 0) - lax.broadcasted_iota(jnp.int32, (size, size), 1)
        ahead = ahead - (places[0, slot] - shift)
        down = jnp.where(ahead == 0, 1.0 - frac_y, jnp.where(ahead == 1, frac_y, 0.0)).astype(BF16)
        fetch(stage, slot).wait()
        for part in range(2):
            wide = dot(held[slot, :, part * size : (part + 1) * size], along).astype(BF16)
            start = pl.multiple_of(col0 - base + part * extent, LANES)
            total[:, pl.ds(start, reach)] += dot(down, wide)

    for stage in range(len(grads)):

        @pl.loop(0, slots)
        def _(slot, stage=stage):
            pl.when(taken(stage, slot))(functools.partial(one_slot, stage, slot))

    copies = []
    for part in range(2):
        here = slice(part * extent + low - base, part * extent + low - base + length)
        there = slice(part * length, (part + 1) * length)
        if out.dtype == F32:
            copies.append(
                pltpu.make_async_copy(
                    total.at[:, pl.ds(here.start, length)], out.at[:, pl.ds(there.start, length)], out_sems.at[part]
                )
            )
            copies[-1].start()
        else:
            out[:, there] = total[:, here].astype(out.dtype)
    for copy in copies:
        copy.wait()


def settle(places, grads, bounds, low, high, shift, dtype, width, name):
    slots, size, _ = grads[0].shape
    base, end = max(low - size, 0), min(high + size, width)
    hbm = pl.BlockSpec(memory_space=pl.ANY)
    return pl.pallas_call(
        functools.partial(settle_kernel, size, bounds, low, high, shift),
        in_specs=[pl.BlockSpec(memory_space=pltpu.SMEM)] + [hbm] * len(grads),
        out_specs=hbm if dtype == F32 else pl.BlockSpec(memory_space=pltpu.VMEM),
        out_shape=jax.ShapeDtypeStruct((size, 2 * (high - low)), dtype),
        scratch_shapes=[
            pltpu.VMEM((size, 2 * (end - base)), F32),
            pltpu.VMEM(grads[0].shape, BF16),
            pltpu.SemaphoreType.DMA((slots,)),
            pltpu.SemaphoreType.DMA((2,)),
        ],
        compiler_params=pltpu.CompilerParams(vmem_limit_bytes=VMEM_SMALL),
        cost_estimate=pl.CostEstimate(flops=10**9, bytes_accessed=8 * 2**20, transcendentals=0),
        name=name,
    )(places, *grads)


def finish_kernel(edges, n, own, *refs):
    aboves, out = refs[:n], refs[n]
    wides, adds, sems = refs[n + 1 : 2 * n + 1], refs[2 * n + 1 : 3 * n + 1], refs[3 * n + 1]
    width = out.shape[2]
    loads, outs = [], []

    def copied(source, target, to):
        to.append(pltpu.make_async_copy(source, target, sems.at[len(loads) + len(outs)]))
        to[-1].start()

    for i in range(n):
        length = edges[i + 1] - edges[i]
        for part in range(2):
            copied(
                own.at[:, pl.ds(part * width + edges[i], length)], wides[i].at[:, pl.ds(part * length, length)], loads
            )
        copied(aboves[i], adds[i], loads)
    for i in range(n):
        for copy in loads[3 * i : 3 * i + 3]:
            copy.wait()
        length = edges[i + 1] - edges[i]
        for part in range(2):
            cols = slice(part * length, (part + 1) * length)
            wides[i][:, cols] += adds[i][:, cols].astype(F32)
            copied(wides[i].at[:, pl.ds(part * length, length)], out.at[:, part, pl.ds(edges[i], length)], outs)
    for copy in outs:
        copy.wait()


def finish(own, aboves, edges, width):
    n = len(aboves)
    hbm = pl.BlockSpec(memory_space=pl.ANY)
    return pl.pallas_call(
        functools.partial(finish_kernel, edges, n),
        in_specs=[hbm] * (n + 1),
        out_specs=hbm,
        out_shape=jax.ShapeDtypeStruct((own.shape[0], 2, width), F32),
        scratch_shapes=[pltpu.VMEM(x.shape, F32) for x in aboves]
        + [pltpu.VMEM(x.shape, BF16) for x in aboves]
        + [pltpu.SemaphoreType.DMA((5 * n,))],
        compiler_params=pltpu.CompilerParams(vmem_limit_bytes=VMEM_SMALL),
        cost_estimate=pl.CostEstimate(flops=10**6, bytes_accessed=10 * 2**20, transcendentals=0),
        name="finish",
    )(own, *aboves)


def passed_along(x, axis, by):
    length = lax.axis_size(axis)
    pairs = [(i, i + by) for i in range(length) if 0 <= i + by < length]
    return lax.ppermute(x, axis, pairs)


def unpack_kernel(order, *refs):
    n = (len(refs) - 4) // 2
    out, wide, narrow, sems = refs[2 * n :]
    rows = wide.shape[1]
    size = out.shape[1]
    span = min(rows, size)
    for core in range(2):

        @pl.when(order[n] == core)
        def _():
            for i in range(n):
                pltpu.make_async_copy(refs[core * n + i], narrow.at[i], sems.at[0, i]).start()

    copies = []
    for i in range(n):
        pltpu.make_async_copy(refs[i], narrow.at[i], sems.at[0, i]).wait()
        wide[i] = narrow[i].astype(F32)
        for j in range(rows // span):
            line = order[i] * rows + j * span
            mode = line // size
            at = pl.multiple_of(line % size, 8)
            for part in range(2):
                copies.append(
                    pltpu.make_async_copy(
                        wide.at[i, pl.ds(j * span, span), pl.ds(part * size, size)],
                        out.at[mode, pl.ds(at, span), part, :],
                        sems.at[1, len(copies)],
                    )
                )
                copies[-1].start()
    for copy in copies:
        copy.wait()


def unpacked(pieces, others, order, shape):
    n = len(pieces)
    rows, columns = pieces[0].shape
    hbm = pl.BlockSpec(memory_space=pl.ANY)
    return pl.pallas_call(
        unpack_kernel,
        in_specs=[pl.BlockSpec(memory_space=pltpu.SMEM)] + [hbm] * (2 * n),
        out_specs=hbm,
        out_shape=jax.ShapeDtypeStruct(shape, F32),
        scratch_shapes=[
            pltpu.VMEM((n, rows, columns), F32),
            pltpu.VMEM((n, rows, columns), BF16),
            pltpu.SemaphoreType.DMA((2, 2 * n * max(1, rows // shape[1]))),
        ],
        compiler_params=pltpu.CompilerParams(vmem_limit_bytes=VMEM_SMALL),
        cost_estimate=pl.CostEstimate(flops=10**6, bytes_accessed=4 * 2**20, transcendentals=0),
        name="unpack",
    )(order, *pieces, *others)


def near_chips(axis):
    return min(4, lax.axis_size(axis) // 2)


def piece_order(axis):
    near = near_chips(axis)
    me = lax.axis_index(axis)
    core, spot = me % 2, me // 2 % near
    return jnp.stack([spot ^ s for s in range(near)] + [core])


def hop(axis, shift, stride):
    return [(i, i ^ (2 * stride * shift)) for i in range(0, lax.axis_size(axis), 2)]


def summed(given, axis, shape, order, beside, between):
    length = lax.axis_size(axis)
    near = near_chips(axis)
    far = length // 2 // near
    inward = [(i + 1, i) for i in range(0, length, 2)]
    outward = [(i, i + 1) for i in range(0, length, 2)]
    modes, size, columns = given.shape
    spot = lax.axis_index(axis) // 2 % near
    sibling = beside(lax.ppermute(given, axis, inward))
    parts = (given.astype(F32) + sibling.astype(F32)).astype(BF16).reshape(near, modes * size // near, columns)
    got = [
        lax.ppermute(lax.dynamic_index_in_dim(parts, spot ^ s, 0, False), axis, hop(axis, s, 1)) for s in range(1, near)
    ]
    total = lax.dynamic_index_in_dim(parts, spot, 0, False).astype(F32)
    for piece in got:
        total = total + piece.astype(F32)
    sent = total.astype(BF16)
    others = [lax.ppermute(sent, axis, hop(axis, s, near)) for s in range(1, far)]
    if others:
        others[0] = between(others[0])
    for piece in others:
        total = total + piece.astype(F32)
    total = total.astype(BF16)
    pieces = [total] + [lax.ppermute(total, axis, hop(axis, s, 1)) for s in range(1, near)]
    others = [lax.ppermute(piece, axis, outward) for piece in pieces]
    return unpacked(pieces, others, order, shape)


def column_bounds(width, shares):
    return tuple([0] + [round(width * share / LANES) * LANES for share in shares] + [width])


def shards(object_tiles, probe, measured, offset_row, offset_col, subpixel, live_count):
    rows, _, width = object_tiles.shape
    modes, size = probe.shape[:2]
    tables = dft_tables(size)
    bounds = column_bounds(width, (0.5625,))
    stages = len(bounds) - 1
    rims = [
        passed_along(object_tiles[:size, :, low:high].reshape(size, 2 * (high - low)), "row", -1)
        for low, high in zip(bounds[:-1], bounds[1:])
    ]
    core = lax.axis_index("row") % 2
    places = jnp.stack(
        [offset_row, offset_col, subpixel] + [jnp.broadcast_to(x, offset_row.shape) for x in (live_count, core)]
    )
    places, order = lax.optimization_barrier((places, piece_order("row")))
    own = object_tiles.reshape(rows, 2 * width)
    flat = probe.reshape(modes, size, 2 * size)
    carried = None
    grads, aboves = [], []
    edges = [0] + [bound - size for bound in bounds[1:-1]] + [width]
    for stage in range(stages):
        moved, grad, *rest = project(stage, bounds, places, own, rims, flat, measured, tables, width, carried)
        grads.append(grad)
        carried = [moved] + rest
        if stage < stages - 1:
            early = settle(places, grads, bounds, edges[stage], edges[stage + 1], size, BF16, width, f"below_{stage}")
            places, early = lax.optimization_barrier((places, early))
            aboves.append(passed_along(early, "row", 1))
    given = carried[1]
    given, aboves = lax.optimization_barrier((given, aboves))
    late = settle(places, grads, bounds, edges[-2], edges[-1], size, BF16, width, "below_last")
    held = {}

    def beside(x):
        x, held["late"] = lax.optimization_barrier((x, late))
        return x

    def between(x):
        own_rows = settle(places, grads, bounds, 0, width, 0, F32, width, "own_rows")
        x, held["own"] = lax.optimization_barrier((x, own_rows))
        return x

    probe_grad = summed(given, "row", probe.shape, order, beside, between)
    aboves = list(aboves) + [passed_along(held["late"], "row", 1)]
    object_grad = finish(held["own"], aboves, edges, width)
    return object_grad, probe_grad, moved


def solution(mesh):
    in_specs = (
        P(("groups", "row"), None, None),
        P(),
        P(("groups", "row"), None, None),
        P(("groups", "row")),
        P(("groups", "row")),
        P(("groups", "row")),
        P(("groups", "row")),
    )
    out_specs = (
        P(("groups", "row"), None, None),
        P("groups", None, None, None),
        P(None, ("groups", "row")),
    )
    return jax.shard_map(shards, mesh=mesh, in_specs=in_specs, out_specs=out_specs, check_vma=False)
```

```python
import functools
import math

import jax
import jax.numpy as jnp
import ml_dtypes
import numpy as np
from jax import lax
from jax.experimental import pallas as pl
from jax.experimental.pallas import tpu as pltpu
from jax.sharding import PartitionSpec as P

F32 = jnp.float32
BF16 = jnp.bfloat16
LANES = 128
VMEM_BYTES = 26 * 2**20
VMEM_SMALL = 16 * 2**20


def dft_tables(size):
    half = size // 2
    index = np.arange(size)
    angle = (index[:, None] * index[None, :] % size) * (2.0 * math.pi / size)
    scale = 1.0 / math.sqrt(size)
    cosine = (np.cos(angle) * scale).astype(ml_dtypes.bfloat16)
    sine = (np.sin(angle) * scale).astype(ml_dtypes.bfloat16)
    tables = []
    for parity in (0, 1):
        c, s = cosine[:half, parity::2], sine[:half, parity::2]
        tables.append(np.block([[c, -s], [s, c]]))
    order = np.zeros((size, size), ml_dtypes.bfloat16)
    order[2 * index[:half], index[:half]] = 1
    order[2 * index[:half] + 1, half + index[:half]] = 1
    even, odd = tables
    return jnp.asarray(np.stack([even, odd, even.T, odd.T, order, order.T]))


def dot(left, right):
    return jnp.dot(left, right, preferred_element_type=F32)


def fractions(code):
    return (code // 4).astype(F32) * 0.25, (code % 4).astype(F32) * 0.25


def in_stage(places, slot, bounds, stage, size):
    end = places[1, slot] + size + 1
    here = end <= bounds[stage + 1]
    if stage > 0:
        here = jnp.logical_and(here, end > bounds[stage])
    return jnp.logical_and(slot < places[3, 0], here)


def project_kernel(size, width, bounds, stage, places, *refs):
    first_stage, last_stage = stage == 0, stage == len(bounds) - 2
    refs = list(refs)
    own, rim = refs[:2]
    rim_before = None if first_stage else refs[2]
    refs = refs[2:] if first_stage else refs[3:]
    probe_in, measured_in, tables_in = refs[:3]
    refs = refs[3:]
    if not first_stage:
        moved_in, sums_in = refs[:2]
        refs = refs[2:]
    moved, grads = refs[:2]
    refs = refs[2:]
    sums_out = refs.pop(0)
    cells, mixed, patch, folded, half_u, half_v, far, error, back, probe, measured, tables, probe_acc, held = refs[:14]
    sems, slot_sems = refs[14:16]
    if last_stage and not first_stage:
        sums, given = refs[16:]
    elif last_stage:
        given = refs[16]
    even, odd, even_t, odd_t, order, order_t = [tables.at[i] for i in range(6)]
    half = size // 2
    modes = probe.shape[0]
    slots = measured.shape[0]
    rows = own.shape[0]
    low, high = bounds[stage], bounds[stage + 1]
    base = 0 if first_stage else low - size
    extent = high - base
    count = places[3, 0]
    copies = []

    def load(source, target):
        copies.append(pltpu.make_async_copy(source, target, sems.at[len(copies)]))

    for part in range(2):
        load(
            own.at[:, pl.ds(part * width + base, extent)],
            cells.at[pl.ds(0, rows), pl.ds(part * extent, extent)],
        )
        load(
            rim.at[:, pl.ds(part * (high - low), high - low)],
            cells.at[pl.ds(rows, size), pl.ds(part * extent + low - base, high - low)],
        )
        if not first_stage:
            before = low - bounds[stage - 1]
            load(
                rim_before.at[:, pl.ds((part + 1) * before - size, size)],
                cells.at[pl.ds(rows, size), pl.ds(part * extent, size)],
            )
    n_cells = len(copies)
    load(tables_in, tables)
    load(probe_in, probe)
    load(measured_in, measured)
    n_later = len(copies)
    if not first_stage:
        load(sums_in, sums if last_stage else probe_acc)
    for copy in copies:
        copy.start()
    if last_stage or first_stage:
        probe_acc[...] = jnp.zeros_like(probe_acc)
    cells[rows + size :] = jnp.zeros((cells.shape[0] - rows - size, cells.shape[1]), BF16)
    for slot in range(slots):
        for axis in range(2):
            moved[axis, slot] = 0.0 if first_stage else moved_in[axis, slot]
    for copy in copies[:n_cells]:
        copy.wait()

    def wait_later():
        for copy in copies[n_cells : n_later if last_stage else len(copies)]:
            copy.wait()

    def mine(slot):
        return in_stage(places, slot, bounds, stage, size)

    def sent_out(slot):
        return pltpu.make_async_copy(held.at[slot], grads.at[slot], slot_sems.at[slot])

    first_slot = jnp.int32(slots)
    for slot in reversed(range(slots)):
        first_slot = jnp.where(mine(slot), slot, first_slot)

    block = 16
    blocks = size // block
    lift_rows = half + 8
    lift_from = half + 32

    def one_slot(slot):
        top = places[0, slot]
        left = places[1, slot]
        frac_y, frac_x = fractions(places[2, slot])
        row0 = pl.multiple_of((top // 16) * 16, 16)
        col0 = pl.multiple_of((left // LANES) * LANES - base, LANES)
        down = top - row0
        across = left - base - col0
        source = lax.broadcasted_iota(jnp.int32, (2 * LANES, LANES), 0)
        target = lax.broadcasted_iota(jnp.int32, (2 * LANES, LANES), 1) + across
        here = (source == target).astype(F32)
        after = (source == target + 1).astype(F32)
        blend = jnp.concatenate([(1.0 - frac_x) * here + frac_x * after, after - here], axis=1).astype(BF16)
        source = lax.broadcasted_iota(jnp.int32, (lift_rows, lift_from), 1)
        target = lax.broadcasted_iota(jnp.int32, (lift_rows, lift_from), 0) + down
        lifts = [(source == target + shift).astype(F32).astype(BF16) for shift in (0, 8)]
        for part in range(2):
            start = pl.multiple_of(col0 + part * extent, LANES)
            for piece in range(2):
                taken = pl.ds(pl.multiple_of(row0 + piece * half, 16), lift_from)
                window = dot(lifts[piece], cells[taken, pl.ds(start, size + LANES)]).astype(BF16)
                for h in range(size // LANES):
                    mixed[part, pl.ds(piece * lift_rows, lift_rows), h * size : (h + 1) * size] = dot(
                        window[:, h * LANES : (h + 2) * LANES], blend
                    )
        for part in range(2):
            for h in range(size // LANES):
                cols = slice(h * size, h * size + LANES)
                for b in range(0, size, block):
                    upper = mixed[part, pl.ds(b, block), cols]
                    lower = mixed[part, pl.ds(b + 1, block), cols]
                    to = slice(part * size + h * LANES, part * size + (h + 1) * LANES)
                    patch[pl.ds(b, block), to] = (1.0 - frac_y) * upper + frac_y * lower
        pl.when(slot == first_slot)(wait_later)

        for mode in range(modes):
            for b in range(blocks):
                at = slice(b * block, (b + 1) * block)
                spot = (2 * b if b < blocks // 2 else 2 * b + 1 - blocks) * block
                to = slice(spot, spot + block)
                preal, pimag = probe[mode, at, :size], probe[mode, at, size:]
                oreal, oimag = patch[at, :size], patch[at, size:]
                wreal = preal * oreal - pimag * oimag
                wimag = preal * oimag + pimag * oreal
                for part, wave in enumerate((wreal, wimag)):
                    folded[mode, to, part * half : (part + 1) * half] = (wave[:, :half] + wave[:, half:]).astype(BF16)
                    folded[mode, to, size + part * half : size + (part + 1) * half] = (
                        wave[:, :half] - wave[:, half:]
                    ).astype(BF16)
        for mode in range(modes):
            for k, table in enumerate((even, odd)):
                out = dot(folded[mode, :, k * size : (k + 1) * size], table[...])
                for b in range(blocks // 2):
                    upper = out[2 * b * block : (2 * b + 1) * block]
                    lower = out[(2 * b + 1) * block : (2 * b + 2) * block]
                    plus, minus = (upper + lower).astype(BF16), (upper - lower).astype(BF16)
                    for part in range(2):
                        to = slice(part * half + b * block, part * half + (b + 1) * block)
                        cols = slice(part * half, (part + 1) * half)
                        half_u[mode, to, k * half : (k + 1) * half] = plus[:, cols]
                        half_v[mode, to, k * half : (k + 1) * half] = minus[:, cols]
        for mode in range(modes):
            far[mode, 0] = dot(even_t[...], half_u[mode])
            far[mode, 1] = dot(odd_t[...], half_v[mode])

        amplitude = dot(dot(order_t[...], measured[slot]).astype(BF16), order[...])
        for k in range(2):
            for b in range(0, half, block):
                pieces = [
                    [far[mode, k, part * half + b : part * half + b + block, :] for part in range(2)]
                    for mode in range(modes)
                ]
                power = sum(p * p for pair in pieces for p in pair)
                level = amplitude[k * half + b : k * half + b + block]
                ratio = 1.0 - level / jnp.maximum(jnp.sqrt(power), 0.5)
                for mode in range(modes):
                    for part in range(2):
                        to = slice(part * half + b, part * half + b + block)
                        error[mode, k, to, :] = (pieces[mode][part] * ratio).astype(BF16)

        for mode in range(modes):
            first = dot(even[...], error[mode, 0])
            second = dot(odd[...], error[mode, 1])
            plus, minus = (first + second).astype(BF16), (first - second).astype(BF16)
            for part in range(2):
                for b in range(blocks):
                    pick = part * half + (b % (blocks // 2)) * block
                    piece = (plus if b < blocks // 2 else minus)[pick : pick + block]
                    to = slice((b * modes + mode) * block, (b * modes + mode + 1) * block)
                    for c in range(2):
                        cols = slice(c * size + part * half, c * size + (part + 1) * half)
                        back[to, cols] = piece[:, c * half : (c + 1) * half]

        total_y = jnp.zeros((block, half), F32)
        total_x = jnp.zeros((block, half), F32)
        group = size // (modes * block)
        for g in range(blocks // group):
            span = slice(g * size, (g + 1) * size)
            first = dot(back[span, :size], even_t[...])
            second = dot(back[span, size:], odd_t[...])
            for r in range(group):
                at = slice((g * group + r) * block, (g * group + r + 1) * block)
                below = slice(at.start + 1, at.stop + 1)
                for h in range(2):
                    re = slice(h * half, (h + 1) * half)
                    im = slice(size + h * half, size + (h + 1) * half)
                    oreal, oimag = patch[at, re], patch[at, im]
                    greal = jnp.zeros((block, half), F32)
                    gimag = jnp.zeros((block, half), F32)
                    for mode in range(modes):
                        part = slice((r * modes + mode) * block, (r * modes + mode + 1) * block)
                        piece = first[part] + second[part] if h == 0 else first[part] - second[part]
                        ureal, uimag = piece[:, :half], piece[:, half:]
                        preal, pimag = probe[mode, at, re], probe[mode, at, im]
                        greal += preal * ureal + pimag * uimag
                        gimag += preal * uimag - pimag * ureal
                        probe_acc[mode, at, re] += oreal * ureal + oimag * uimag
                        probe_acc[mode, at, im] += oreal * uimag - oimag * ureal
                    held[slot, at, re] = greal.astype(BF16)
                    held[slot, at, im] = gimag.astype(BF16)
                    for part, grad in enumerate((greal, gimag)):
                        cols = slice(h * size, h * size + LANES)
                        total_y += grad * (mixed[part, below, cols] - mixed[part, at, cols])
                        cols = slice(h * size + LANES, (h + 1) * size)
                        total_x += grad * ((1.0 - frac_y) * mixed[part, at, cols] + frac_y * mixed[part, below, cols])
        moved[0, slot] = jnp.sum(total_y) / size
        moved[1, slot] = jnp.sum(total_x) / size

        sent_out(slot).start()

    @pl.loop(0, slots)
    def _(slot):
        pl.when(mine(slot))(functools.partial(one_slot, slot))

    pl.when(first_slot == slots)(wait_later)
    outs = []

    def store(source, target):
        outs.append(pltpu.make_async_copy(source, target, sems.at[len(outs)]))
        outs[-1].start()

    if last_stage:
        if first_stage:
            given[...] = probe_acc[...].astype(BF16)
        else:
            copies[-1].wait()
            for mode in range(modes):
                given[mode] = (probe_acc[mode] + sums[mode]).astype(BF16)
        store(given, sums_out)
    else:
        store(probe_acc, sums_out)

    @pl.loop(0, slots)
    def _(slot):
        @pl.when(mine(slot))
        def _():
            sent_out(slot).wait()

    for out in outs:
        out.wait()


def project(stage, bounds, places, own, rims, probe, measured, tables, width, carried):
    slots, size, _ = measured.shape
    modes = probe.shape[0]
    rows = own.shape[0]
    smem = pl.BlockSpec(memory_space=pltpu.SMEM)
    hbm = pl.BlockSpec(memory_space=pl.ANY)
    first_stage, last_stage = stage == 0, stage == len(bounds) - 2
    low, high = bounds[stage], bounds[stage + 1]
    extent = high - (0 if first_stage else low - size)
    inputs = [places, own, rims[stage]] + ([] if first_stage else [rims[stage - 1]]) + [probe, measured, tables]
    specs = [smem] + [hbm] * (len(inputs) - 1)
    outs = [
        jax.ShapeDtypeStruct((2, slots), F32),
        jax.ShapeDtypeStruct((slots, size, 2 * size), BF16),
        jax.ShapeDtypeStruct(probe.shape, BF16 if last_stage else F32),
    ]
    if not first_stage:
        inputs += list(carried)
        specs += [smem, hbm]
    scratch = [
        pltpu.VMEM((rows + size + 32, 2 * extent), BF16),
        pltpu.VMEM((2, size + 16, 2 * size), F32),
        pltpu.VMEM((size, 2 * size), F32),
        pltpu.VMEM((modes, size, 2 * size), BF16),
        pltpu.VMEM((modes, size, size), BF16),
        pltpu.VMEM((modes, size, size), BF16),
        pltpu.VMEM((modes, 2, size, size), F32),
        pltpu.VMEM((modes, 2, size, size), BF16),
        pltpu.VMEM((modes * size, 2 * size), BF16),
        pltpu.VMEM(probe.shape, F32),
        pltpu.VMEM(measured.shape, BF16),
        pltpu.VMEM(tables.shape, BF16),
        pltpu.VMEM(probe.shape, F32),
        pltpu.VMEM((slots, size, 2 * size), BF16),
        pltpu.SemaphoreType.DMA((12,)),
        pltpu.SemaphoreType.DMA((slots,)),
    ]
    if last_stage and not first_stage:
        scratch.append(pltpu.VMEM(probe.shape, F32))
    if last_stage:
        scratch.append(pltpu.VMEM(probe.shape, BF16))
    return pl.pallas_call(
        functools.partial(project_kernel, size, width, bounds, stage),
        in_specs=specs,
        out_specs=[smem] + [hbm] * (len(outs) - 1),
        out_shape=outs,
        scratch_shapes=scratch,
        compiler_params=pltpu.CompilerParams(vmem_limit_bytes=VMEM_BYTES),
        cost_estimate=pl.CostEstimate(flops=8 * 10**9, bytes_accessed=16 * 2**20, transcendentals=0),
        name=f"project_{stage}",
    )(*inputs)


def settle_kernel(size, bounds, low, high, shift, places, *refs):
    grads = refs[: len(refs) - 5]
    out, total, held, sems, out_sems = refs[len(refs) - 5 :]
    slots = held.shape[0]
    reach = size + LANES
    base = max(low - size, 0)
    extent = total.shape[1] // 2
    length = high - low

    def taken(stage, slot):
        left = places[1, slot]
        within = jnp.logical_and(left < high, left + size + 1 > low)
        return jnp.logical_and(within, in_stage(places, slot, bounds, stage, size))

    def fetch(stage, slot):
        return pltpu.make_async_copy(grads[stage].at[slot], held.at[slot], sems.at[slot])

    for stage in range(len(grads)):

        @pl.loop(0, slots)
        def _(slot, stage=stage):
            @pl.when(taken(stage, slot))
            def _():
                fetch(stage, slot).start()

    total[...] = jnp.zeros_like(total)

    def one_slot(stage, slot):
        left = places[1, slot]
        frac_y, frac_x = fractions(places[2, slot])
        col0 = (left // LANES) * LANES
        ahead = lax.broadcasted_iota(jnp.int32, (size, reach), 1) - lax.broadcasted_iota(jnp.int32, (size, reach), 0)
        ahead = ahead - (left - col0)
        along = jnp.where(ahead == 0, 1.0 - frac_x, jnp.where(ahead == 1, frac_x, 0.0)).astype(BF16)
        ahead = lax.broadcasted_iota(jnp.int32, (size, size), 0) - lax.broadcasted_iota(jnp.int32, (size, size), 1)
        ahead = ahead - (places[0, slot] - shift)
        down = jnp.where(ahead == 0, 1.0 - frac_y, jnp.where(ahead == 1, frac_y, 0.0)).astype(BF16)
        fetch(stage, slot).wait()
        for part in range(2):
            wide = dot(held[slot, :, part * size : (part + 1) * size], along).astype(BF16)
            start = pl.multiple_of(col0 - base + part * extent, LANES)
            total[:, pl.ds(start, reach)] += dot(down, wide)

    for stage in range(len(grads)):

        @pl.loop(0, slots)
        def _(slot, stage=stage):
            pl.when(taken(stage, slot))(functools.partial(one_slot, stage, slot))

    copies = []
    for part in range(2):
        here = slice(part * extent + low - base, part * extent + low - base + length)
        there = slice(part * length, (part + 1) * length)
        if out.dtype == F32:
            copies.append(
                pltpu.make_async_copy(
                    total.at[:, pl.ds(here.start, length)], out.at[:, pl.ds(there.start, length)], out_sems.at[part]
                )
            )
            copies[-1].start()
        else:
            out[:, there] = total[:, here].astype(out.dtype)
    for copy in copies:
        copy.wait()


def settle(places, grads, bounds, low, high, shift, dtype, width, name):
    slots, size, _ = grads[0].shape
    base, end = max(low - size, 0), min(high + size, width)
    hbm = pl.BlockSpec(memory_space=pl.ANY)
    return pl.pallas_call(
        functools.partial(settle_kernel, size, bounds, low, high, shift),
        in_specs=[pl.BlockSpec(memory_space=pltpu.SMEM)] + [hbm] * len(grads),
        out_specs=hbm if dtype == F32 else pl.BlockSpec(memory_space=pltpu.VMEM),
        out_shape=jax.ShapeDtypeStruct((size, 2 * (high - low)), dtype),
        scratch_shapes=[
            pltpu.VMEM((size, 2 * (end - base)), F32),
            pltpu.VMEM(grads[0].shape, BF16),
            pltpu.SemaphoreType.DMA((slots,)),
            pltpu.SemaphoreType.DMA((2,)),
        ],
        compiler_params=pltpu.CompilerParams(vmem_limit_bytes=VMEM_SMALL),
        cost_estimate=pl.CostEstimate(flops=10**9, bytes_accessed=8 * 2**20, transcendentals=0),
        name=name,
    )(places, *grads)


def finish_kernel(edges, n, own, *refs):
    aboves, out = refs[:n], refs[n]
    wides, adds, sems = refs[n + 1 : 2 * n + 1], refs[2 * n + 1 : 3 * n + 1], refs[3 * n + 1]
    width = out.shape[2]
    loads, outs = [], []

    def copied(source, target, to):
        to.append(pltpu.make_async_copy(source, target, sems.at[len(loads) + len(outs)]))
        to[-1].start()

    for i in range(n):
        length = edges[i + 1] - edges[i]
        for part in range(2):
            copied(
                own.at[:, pl.ds(part * width + edges[i], length)], wides[i].at[:, pl.ds(part * length, length)], loads
            )
        copied(aboves[i], adds[i], loads)
    for i in range(n):
        for copy in loads[3 * i : 3 * i + 3]:
            copy.wait()
        length = edges[i + 1] - edges[i]
        for part in range(2):
            cols = slice(part * length, (part + 1) * length)
            wides[i][:, cols] += adds[i][:, cols].astype(F32)
            copied(wides[i].at[:, pl.ds(part * length, length)], out.at[:, part, pl.ds(edges[i], length)], outs)
    for copy in outs:
        copy.wait()


def finish(own, aboves, edges, width):
    n = len(aboves)
    hbm = pl.BlockSpec(memory_space=pl.ANY)
    return pl.pallas_call(
        functools.partial(finish_kernel, edges, n),
        in_specs=[hbm] * (n + 1),
        out_specs=hbm,
        out_shape=jax.ShapeDtypeStruct((own.shape[0], 2, width), F32),
        scratch_shapes=[pltpu.VMEM(x.shape, F32) for x in aboves]
        + [pltpu.VMEM(x.shape, BF16) for x in aboves]
        + [pltpu.SemaphoreType.DMA((5 * n,))],
        compiler_params=pltpu.CompilerParams(vmem_limit_bytes=VMEM_SMALL),
        cost_estimate=pl.CostEstimate(flops=10**6, bytes_accessed=10 * 2**20, transcendentals=0),
        name="finish",
    )(own, *aboves)


def passed_along(x, axis, by):
    length = lax.axis_size(axis)
    pairs = [(i, i + by) for i in range(length) if 0 <= i + by < length]
    return lax.ppermute(x, axis, pairs)


def unpack_kernel(order, *refs):
    n = (len(refs) - 4) // 2
    out, wide, narrow, sems = refs[2 * n :]
    rows = wide.shape[1]
    size = out.shape[1]
    span = min(rows, size)
    for core in range(2):

        @pl.when(order[n] == core)
        def _():
            for i in range(n):
                pltpu.make_async_copy(refs[core * n + i], narrow.at[i], sems.at[0, i]).start()

    copies = []
    for i in range(n):
        pltpu.make_async_copy(refs[i], narrow.at[i], sems.at[0, i]).wait()
        wide[i] = narrow[i].astype(F32)
        for j in range(rows // span):
            line = order[i] * rows + j * span
            mode = line // size
            at = pl.multiple_of(line % size, 8)
            for part in range(2):
                copies.append(
                    pltpu.make_async_copy(
                        wide.at[i, pl.ds(j * span, span), pl.ds(part * size, size)],
                        out.at[mode, pl.ds(at, span), part, :],
                        sems.at[1, len(copies)],
                    )
                )
                copies[-1].start()
    for copy in copies:
        copy.wait()


def unpacked(pieces, others, order, shape):
    n = len(pieces)
    rows, columns = pieces[0].shape
    hbm = pl.BlockSpec(memory_space=pl.ANY)
    return pl.pallas_call(
        unpack_kernel,
        in_specs=[pl.BlockSpec(memory_space=pltpu.SMEM)] + [hbm] * (2 * n),
        out_specs=hbm,
        out_shape=jax.ShapeDtypeStruct(shape, F32),
        scratch_shapes=[
            pltpu.VMEM((n, rows, columns), F32),
            pltpu.VMEM((n, rows, columns), BF16),
            pltpu.SemaphoreType.DMA((2, 2 * n * max(1, rows // shape[1]))),
        ],
        compiler_params=pltpu.CompilerParams(vmem_limit_bytes=VMEM_SMALL),
        cost_estimate=pl.CostEstimate(flops=10**6, bytes_accessed=4 * 2**20, transcendentals=0),
        name="unpack",
    )(order, *pieces, *others)


def near_chips(axis):
    return min(4, lax.axis_size(axis) // 2)


def piece_order(axis):
    near = near_chips(axis)
    me = lax.axis_index(axis)
    core, spot = me % 2, me // 2 % near
    return jnp.stack([spot ^ s for s in range(near)] + [core])


def hop(axis, shift, stride):
    return [(i, i ^ (2 * stride * shift)) for i in range(0, lax.axis_size(axis), 2)]


def paired_kernel(order, given, sibling, *refs):
    n = len(refs) - 3
    outs, mine, other, sems = refs[:n], refs[-3], refs[-2], refs[-1]
    rows = mine.shape[1]
    copies = []
    for i in range(n):
        at = pl.ds(pl.multiple_of(order[i] * rows, 16), rows)
        copies.append(
            [
                pltpu.make_async_copy(given.at[at], mine.at[i], sems.at[0, i]),
                pltpu.make_async_copy(sibling.at[at], other.at[i], sems.at[1, i]),
            ]
        )
        for copy in copies[-1]:
            copy.start()
    for i in range(n):
        for copy in copies[i]:
            copy.wait()
        outs[i][...] = (mine[i].astype(F32) + other[i].astype(F32)).astype(BF16)


def paired(given, sibling, order, n):
    rows, columns = given.shape[0] // n, given.shape[1]
    hbm = pl.BlockSpec(memory_space=pl.ANY)
    return pl.pallas_call(
        paired_kernel,
        in_specs=[pl.BlockSpec(memory_space=pltpu.SMEM), hbm, hbm],
        out_specs=[pl.BlockSpec(memory_space=pltpu.VMEM)] * n,
        out_shape=[jax.ShapeDtypeStruct((rows, columns), BF16)] * n,
        scratch_shapes=[
            pltpu.VMEM((n, rows, columns), BF16),
            pltpu.VMEM((n, rows, columns), BF16),
            pltpu.SemaphoreType.DMA((2, n)),
        ],
        compiler_params=pltpu.CompilerParams(vmem_limit_bytes=VMEM_SMALL),
        cost_estimate=pl.CostEstimate(flops=10**6, bytes_accessed=3 * 2**20, transcendentals=0),
        name="paired",
    )(order, given, sibling)


def summed(given, axis, shape, order, beside, during, between):
    length = lax.axis_size(axis)
    near = near_chips(axis)
    far = length // 2 // near
    inward = [(i + 1, i) for i in range(0, length, 2)]
    outward = [(i, i + 1) for i in range(0, length, 2)]
    modes, size, columns = given.shape
    sibling = beside(lax.ppermute(given, axis, inward))
    flat = (modes * size, columns)
    parts = paired(given.reshape(flat), sibling.reshape(flat), order, near)
    got = [lax.ppermute(parts[s], axis, hop(axis, s, 1)) for s in range(1, near)]
    got[0] = during(got[0])
    total = parts[0].astype(F32)
    for piece in got:
        total = total + piece.astype(F32)
    sent = total.astype(BF16)
    others = [lax.ppermute(sent, axis, hop(axis, s, near)) for s in range(1, far)]
    if others:
        others[0] = between(others[0])
    for piece in others:
        total = total + piece.astype(F32)
    total = total.astype(BF16)
    pieces = [total] + [lax.ppermute(total, axis, hop(axis, s, 1)) for s in range(1, near)]
    others = [lax.ppermute(piece, axis, outward) for piece in pieces]
    return unpacked(pieces, others, order, shape)


def column_bounds(width, shares):
    return tuple([0] + [round(width * share / LANES) * LANES for share in shares] + [width])


def shards(object_tiles, probe, measured, offset_row, offset_col, subpixel, live_count):
    rows, _, width = object_tiles.shape
    modes, size = probe.shape[:2]
    tables = dft_tables(size)
    bounds = column_bounds(width, (0.3125, 0.625))
    stages = len(bounds) - 1
    rims = [
        passed_along(object_tiles[:size, :, low:high].reshape(size, 2 * (high - low)), "row", -1)
        for low, high in zip(bounds[:-1], bounds[1:])
    ]
    core = lax.axis_index("row") % 2
    places = jnp.stack(
        [offset_row, offset_col, subpixel] + [jnp.broadcast_to(x, offset_row.shape) for x in (live_count, core)]
    )
    places, order = lax.optimization_barrier((places, piece_order("row")))
    own = object_tiles.reshape(rows, 2 * width)
    flat = probe.reshape(modes, size, 2 * size)
    carried = None
    grads = []
    for stage in range(stages):
        moved, grad, *rest = project(stage, bounds, places, own, rims, flat, measured, tables, width, carried)
        grads.append(grad)
        carried = [moved] + rest
    given = carried[1]
    edges = (0, width // 2 // LANES * LANES, width)
    belows = [
        settle(places, grads, bounds, low, high, size, BF16, width, f"below_{low}")
        for low, high in zip(edges[:-1], edges[1:])
    ]
    held = {}

    def beside(x):
        x, held[0] = lax.optimization_barrier((x, belows[0]))
        return x

    def during(x):
        x, held[1] = lax.optimization_barrier((x, belows[1]))
        return x

    def between(x):
        own_rows = settle(places, grads, bounds, 0, width, 0, F32, width, "own_rows")
        x, held["own"] = lax.optimization_barrier((x, own_rows))
        return x

    probe_grad = summed(given, "row", probe.shape, order, beside, during, between)
    aboves = [passed_along(held[i], "row", 1) for i in range(2)]
    object_grad = finish(held["own"], aboves, edges, width)
    return object_grad, probe_grad, moved


def solution(mesh):
    in_specs = (
        P(("groups", "row"), None, None),
        P(),
        P(("groups", "row"), None, None),
        P(("groups", "row")),
        P(("groups", "row")),
        P(("groups", "row")),
        P(("groups", "row")),
    )
    out_specs = (
        P(("groups", "row"), None, None),
        P("groups", None, None, None),
        P(None, ("groups", "row")),
    )
    return jax.shard_map(shards, mesh=mesh, in_specs=in_specs, out_specs=out_specs, check_vma=False)
```

```python
import functools
import math

import jax
import jax.numpy as jnp
import ml_dtypes
import numpy as np
from jax import lax
from jax.experimental import pallas as pl
from jax.experimental.pallas import tpu as pltpu
from jax.sharding import PartitionSpec as P

F32 = jnp.float32
BF16 = jnp.bfloat16
LANES = 128
VMEM_BYTES = 26 * 2**20
VMEM_SMALL = 16 * 2**20


def dft_tables(size):
    half = size // 2
    index = np.arange(size)
    angle = (index[:, None] * index[None, :] % size) * (2.0 * math.pi / size)
    scale = 1.0 / math.sqrt(size)
    cosine = (np.cos(angle) * scale).astype(ml_dtypes.bfloat16)
    sine = (np.sin(angle) * scale).astype(ml_dtypes.bfloat16)
    tables = []
    for parity in (0, 1):
        c, s = cosine[:half, parity::2], sine[:half, parity::2]
        tables.append(np.block([[c, -s], [s, c]]))
    order = np.zeros((size, size), ml_dtypes.bfloat16)
    order[2 * index[:half], index[:half]] = 1
    order[2 * index[:half] + 1, half + index[:half]] = 1
    even, odd = tables
    return jnp.asarray(np.stack([even, odd, even.T, odd.T, order, order.T]))


def dot(left, right):
    return jnp.dot(left, right, preferred_element_type=F32)


def fractions(code):
    return (code // 4).astype(F32) * 0.25, (code % 4).astype(F32) * 0.25


def in_stage(places, slot, bounds, stage, size):
    end = places[1, slot] + size + 1
    here = end <= bounds[stage + 1]
    if stage > 0:
        here = jnp.logical_and(here, end > bounds[stage])
    return jnp.logical_and(slot < places[3, 0], here)


def project_kernel(size, width, bounds, stage, places, *refs):
    first_stage, last_stage = stage == 0, stage == len(bounds) - 2
    refs = list(refs)
    own, rim = refs[:2]
    rim_before = None if first_stage else refs[2]
    refs = refs[2:] if first_stage else refs[3:]
    probe_in, measured_in, tables_in = refs[:3]
    refs = refs[3:]
    if not first_stage:
        moved_in, sums_in = refs[:2]
        refs = refs[2:]
    moved, grads = refs[:2]
    refs = refs[2:]
    sums_out = refs.pop(0)
    cells, mixed, patch, folded, half_u, half_v, far, error, back, probe, measured, tables, probe_acc, held = refs[:14]
    sems, slot_sems = refs[14:16]
    if last_stage and not first_stage:
        sums, given = refs[16:]
    elif last_stage:
        given = refs[16]
    even, odd, even_t, odd_t, order, order_t = [tables.at[i] for i in range(6)]
    half = size // 2
    modes = probe.shape[0]
    slots = measured.shape[0]
    rows = own.shape[0]
    low, high = bounds[stage], bounds[stage + 1]
    base = 0 if first_stage else low - size
    extent = high - base
    count = places[3, 0]
    copies = []

    def load(source, target):
        copies.append(pltpu.make_async_copy(source, target, sems.at[len(copies)]))

    for part in range(2):
        load(
            own.at[:, pl.ds(part * width + base, extent)],
            cells.at[pl.ds(0, rows), pl.ds(part * extent, extent)],
        )
        load(
            rim.at[:, pl.ds(part * (high - low), high - low)],
            cells.at[pl.ds(rows, size), pl.ds(part * extent + low - base, high - low)],
        )
        if not first_stage:
            before = low - bounds[stage - 1]
            load(
                rim_before.at[:, pl.ds((part + 1) * before - size, size)],
                cells.at[pl.ds(rows, size), pl.ds(part * extent, size)],
            )
    n_cells = len(copies)
    load(tables_in, tables)
    load(probe_in, probe)
    load(measured_in, measured)
    n_later = len(copies)
    if not first_stage:
        load(sums_in, sums if last_stage else probe_acc)
    for copy in copies:
        copy.start()
    if last_stage or first_stage:
        probe_acc[...] = jnp.zeros_like(probe_acc)
    cells[rows + size :] = jnp.zeros((cells.shape[0] - rows - size, cells.shape[1]), BF16)
    for slot in range(slots):
        for axis in range(2):
            moved[axis, slot] = 0.0 if first_stage else moved_in[axis, slot]
    for copy in copies[:n_cells]:
        copy.wait()

    def wait_later():
        for copy in copies[n_cells : n_later if last_stage else len(copies)]:
            copy.wait()

    def mine(slot):
        return in_stage(places, slot, bounds, stage, size)

    def sent_out(slot):
        return pltpu.make_async_copy(held.at[slot], grads.at[slot], slot_sems.at[slot])

    first_slot = jnp.int32(slots)
    for slot in reversed(range(slots)):
        first_slot = jnp.where(mine(slot), slot, first_slot)

    block = 16
    blocks = size // block
    lift_rows = half + 8
    lift_from = half + 32

    def one_slot(slot):
        top = places[0, slot]
        left = places[1, slot]
        frac_y, frac_x = fractions(places[2, slot])
        row0 = pl.multiple_of((top // 16) * 16, 16)
        col0 = pl.multiple_of((left // LANES) * LANES - base, LANES)
        down = top - row0
        across = left - base - col0
        source = lax.broadcasted_iota(jnp.int32, (2 * LANES, LANES), 0)
        target = lax.broadcasted_iota(jnp.int32, (2 * LANES, LANES), 1) + across
        here = (source == target).astype(F32)
        after = (source == target + 1).astype(F32)
        blend = jnp.concatenate([(1.0 - frac_x) * here + frac_x * after, after - here], axis=1).astype(BF16)
        source = lax.broadcasted_iota(jnp.int32, (lift_rows, lift_from), 1)
        target = lax.broadcasted_iota(jnp.int32, (lift_rows, lift_from), 0) + down
        lifts = [(source == target + shift).astype(F32).astype(BF16) for shift in (0, 8)]
        for part in range(2):
            start = pl.multiple_of(col0 + part * extent, LANES)
            for piece in range(2):
                taken = pl.ds(pl.multiple_of(row0 + piece * half, 16), lift_from)
                window = dot(lifts[piece], cells[taken, pl.ds(start, size + LANES)]).astype(BF16)
                for h in range(size // LANES):
                    mixed[part, pl.ds(piece * lift_rows, lift_rows), h * size : (h + 1) * size] = dot(
                        window[:, h * LANES : (h + 2) * LANES], blend
                    )
        for part in range(2):
            for h in range(size // LANES):
                cols = slice(h * size, h * size + LANES)
                for b in range(0, size, block):
                    upper = mixed[part, pl.ds(b, block), cols]
                    lower = mixed[part, pl.ds(b + 1, block), cols]
                    to = slice(part * size + h * LANES, part * size + (h + 1) * LANES)
                    patch[pl.ds(b, block), to] = (1.0 - frac_y) * upper + frac_y * lower
        pl.when(slot == first_slot)(wait_later)

        for mode in range(modes):
            for b in range(blocks):
                at = slice(b * block, (b + 1) * block)
                spot = (2 * b if b < blocks // 2 else 2 * b + 1 - blocks) * block
                to = slice(spot, spot + block)
                preal, pimag = probe[mode, at, :size], probe[mode, at, size:]
                oreal, oimag = patch[at, :size], patch[at, size:]
                wreal = preal * oreal - pimag * oimag
                wimag = preal * oimag + pimag * oreal
                for part, wave in enumerate((wreal, wimag)):
                    folded[mode, to, part * half : (part + 1) * half] = (wave[:, :half] + wave[:, half:]).astype(BF16)
                    folded[mode, to, size + part * half : size + (part + 1) * half] = (
                        wave[:, :half] - wave[:, half:]
                    ).astype(BF16)
        for mode in range(modes):
            for k, table in enumerate((even, odd)):
                out = dot(folded[mode, :, k * size : (k + 1) * size], table[...])
                for b in range(blocks // 2):
                    upper = out[2 * b * block : (2 * b + 1) * block]
                    lower = out[(2 * b + 1) * block : (2 * b + 2) * block]
                    plus, minus = (upper + lower).astype(BF16), (upper - lower).astype(BF16)
                    for part in range(2):
                        to = slice(part * half + b * block, part * half + (b + 1) * block)
                        cols = slice(part * half, (part + 1) * half)
                        half_u[mode, to, k * half : (k + 1) * half] = plus[:, cols]
                        half_v[mode, to, k * half : (k + 1) * half] = minus[:, cols]
        for mode in range(modes):
            far[mode, 0] = dot(even_t[...], half_u[mode])
            far[mode, 1] = dot(odd_t[...], half_v[mode])

        amplitude = dot(dot(order_t[...], measured[slot]).astype(BF16), order[...])
        for k in range(2):
            for b in range(0, half, block):
                pieces = [
                    [far[mode, k, part * half + b : part * half + b + block, :] for part in range(2)]
                    for mode in range(modes)
                ]
                power = sum(p * p for pair in pieces for p in pair)
                level = amplitude[k * half + b : k * half + b + block]
                ratio = 1.0 - level / jnp.maximum(jnp.sqrt(power), 0.5)
                for mode in range(modes):
                    for part in range(2):
                        to = slice(part * half + b, part * half + b + block)
                        error[mode, k, to, :] = (pieces[mode][part] * ratio).astype(BF16)

        for mode in range(modes):
            first = dot(even[...], error[mode, 0])
            second = dot(odd[...], error[mode, 1])
            plus, minus = (first + second).astype(BF16), (first - second).astype(BF16)
            for part in range(2):
                for b in range(blocks):
                    pick = part * half + (b % (blocks // 2)) * block
                    piece = (plus if b < blocks // 2 else minus)[pick : pick + block]
                    to = slice((b * modes + mode) * block, (b * modes + mode + 1) * block)
                    for c in range(2):
                        cols = slice(c * size + part * half, c * size + (part + 1) * half)
                        back[to, cols] = piece[:, c * half : (c + 1) * half]

        total_y = jnp.zeros((block, half), F32)
        total_x = jnp.zeros((block, half), F32)
        group = size // (modes * block)
        for g in range(blocks // group):
            span = slice(g * size, (g + 1) * size)
            first = dot(back[span, :size], even_t[...])
            second = dot(back[span, size:], odd_t[...])
            for r in range(group):
                at = slice((g * group + r) * block, (g * group + r + 1) * block)
                below = slice(at.start + 1, at.stop + 1)
                for h in range(2):
                    re = slice(h * half, (h + 1) * half)
                    im = slice(size + h * half, size + (h + 1) * half)
                    oreal, oimag = patch[at, re], patch[at, im]
                    greal = jnp.zeros((block, half), F32)
                    gimag = jnp.zeros((block, half), F32)
                    for mode in range(modes):
                        part = slice((r * modes + mode) * block, (r * modes + mode + 1) * block)
                        piece = first[part] + second[part] if h == 0 else first[part] - second[part]
                        ureal, uimag = piece[:, :half], piece[:, half:]
                        preal, pimag = probe[mode, at, re], probe[mode, at, im]
                        greal += preal * ureal + pimag * uimag
                        gimag += preal * uimag - pimag * ureal
                        probe_acc[mode, at, re] += oreal * ureal + oimag * uimag
                        probe_acc[mode, at, im] += oreal * uimag - oimag * ureal
                    held[slot, at, re] = greal.astype(BF16)
                    held[slot, at, im] = gimag.astype(BF16)
                    for part, grad in enumerate((greal, gimag)):
                        cols = slice(h * size, h * size + LANES)
                        total_y += grad * (mixed[part, below, cols] - mixed[part, at, cols])
                        cols = slice(h * size + LANES, (h + 1) * size)
                        total_x += grad * ((1.0 - frac_y) * mixed[part, at, cols] + frac_y * mixed[part, below, cols])
        moved[0, slot] = jnp.sum(total_y) / size
        moved[1, slot] = jnp.sum(total_x) / size

        sent_out(slot).start()

    @pl.loop(0, slots)
    def _(slot):
        pl.when(mine(slot))(functools.partial(one_slot, slot))

    pl.when(first_slot == slots)(wait_later)
    outs = []

    def store(source, target):
        outs.append(pltpu.make_async_copy(source, target, sems.at[len(outs)]))
        outs[-1].start()

    if last_stage:
        if first_stage:
            given[...] = probe_acc[...].astype(BF16)
        else:
            copies[-1].wait()
            for mode in range(modes):
                given[mode] = (probe_acc[mode] + sums[mode]).astype(BF16)
        store(given, sums_out)
    else:
        store(probe_acc, sums_out)

    @pl.loop(0, slots)
    def _(slot):
        @pl.when(mine(slot))
        def _():
            sent_out(slot).wait()

    for out in outs:
        out.wait()


def project(stage, bounds, places, own, rims, probe, measured, tables, width, carried):
    slots, size, _ = measured.shape
    modes = probe.shape[0]
    rows = own.shape[0]
    smem = pl.BlockSpec(memory_space=pltpu.SMEM)
    hbm = pl.BlockSpec(memory_space=pl.ANY)
    first_stage, last_stage = stage == 0, stage == len(bounds) - 2
    low, high = bounds[stage], bounds[stage + 1]
    extent = high - (0 if first_stage else low - size)
    inputs = [places, own, rims[stage]] + ([] if first_stage else [rims[stage - 1]]) + [probe, measured, tables]
    specs = [smem] + [hbm] * (len(inputs) - 1)
    outs = [
        jax.ShapeDtypeStruct((2, slots), F32),
        jax.ShapeDtypeStruct((slots, size, 2 * size), BF16),
        jax.ShapeDtypeStruct(probe.shape, BF16 if last_stage else F32),
    ]
    if not first_stage:
        inputs += list(carried)
        specs += [smem, hbm]
    scratch = [
        pltpu.VMEM((rows + size + 32, 2 * extent), BF16),
        pltpu.VMEM((2, size + 16, 2 * size), F32),
        pltpu.VMEM((size, 2 * size), F32),
        pltpu.VMEM((modes, size, 2 * size), BF16),
        pltpu.VMEM((modes, size, size), BF16),
        pltpu.VMEM((modes, size, size), BF16),
        pltpu.VMEM((modes, 2, size, size), F32),
        pltpu.VMEM((modes, 2, size, size), BF16),
        pltpu.VMEM((modes * size, 2 * size), BF16),
        pltpu.VMEM(probe.shape, F32),
        pltpu.VMEM(measured.shape, BF16),
        pltpu.VMEM(tables.shape, BF16),
        pltpu.VMEM(probe.shape, F32),
        pltpu.VMEM((slots, size, 2 * size), BF16),
        pltpu.SemaphoreType.DMA((12,)),
        pltpu.SemaphoreType.DMA((slots,)),
    ]
    if last_stage and not first_stage:
        scratch.append(pltpu.VMEM(probe.shape, F32))
    if last_stage:
        scratch.append(pltpu.VMEM(probe.shape, BF16))
    return pl.pallas_call(
        functools.partial(project_kernel, size, width, bounds, stage),
        in_specs=specs,
        out_specs=[smem] + [hbm] * (len(outs) - 1),
        out_shape=outs,
        scratch_shapes=scratch,
        compiler_params=pltpu.CompilerParams(vmem_limit_bytes=VMEM_BYTES),
        cost_estimate=pl.CostEstimate(flops=8 * 10**9, bytes_accessed=16 * 2**20, transcendentals=0),
        name=f"project_{stage}",
    )(*inputs)


def settle_kernel(size, bounds, low, high, shift, places, *refs):
    grads = refs[: len(refs) - 5]
    out, total, held, sems, out_sems = refs[len(refs) - 5 :]
    slots = held.shape[0]
    reach = size + LANES
    base = max(low - size, 0)
    extent = total.shape[1] // 2
    length = high - low

    def taken(stage, slot):
        left = places[1, slot]
        within = jnp.logical_and(left < high, left + size + 1 > low)
        return jnp.logical_and(within, in_stage(places, slot, bounds, stage, size))

    def fetch(stage, slot):
        return pltpu.make_async_copy(grads[stage].at[slot], held.at[slot], sems.at[slot])

    for stage in range(len(grads)):

        @pl.loop(0, slots)
        def _(slot, stage=stage):
            @pl.when(taken(stage, slot))
            def _():
                fetch(stage, slot).start()

    total[...] = jnp.zeros_like(total)

    def one_slot(stage, slot):
        left = places[1, slot]
        frac_y, frac_x = fractions(places[2, slot])
        col0 = (left // LANES) * LANES
        ahead = lax.broadcasted_iota(jnp.int32, (size, reach), 1) - lax.broadcasted_iota(jnp.int32, (size, reach), 0)
        ahead = ahead - (left - col0)
        along = jnp.where(ahead == 0, 1.0 - frac_x, jnp.where(ahead == 1, frac_x, 0.0)).astype(BF16)
        ahead = lax.broadcasted_iota(jnp.int32, (size, size), 0) - lax.broadcasted_iota(jnp.int32, (size, size), 1)
        ahead = ahead - (places[0, slot] - shift)
        down = jnp.where(ahead == 0, 1.0 - frac_y, jnp.where(ahead == 1, frac_y, 0.0)).astype(BF16)
        fetch(stage, slot).wait()
        for part in range(2):
            wide = dot(held[slot, :, part * size : (part + 1) * size], along).astype(BF16)
            start = pl.multiple_of(col0 - base + part * extent, LANES)
            total[:, pl.ds(start, reach)] += dot(down, wide)

    for stage in range(len(grads)):

        @pl.loop(0, slots)
        def _(slot, stage=stage):
            pl.when(taken(stage, slot))(functools.partial(one_slot, stage, slot))

    copies = []
    for part in range(2):
        here = slice(part * extent + low - base, part * extent + low - base + length)
        there = slice(part * length, (part + 1) * length)
        if out.dtype == F32:
            copies.append(
                pltpu.make_async_copy(
                    total.at[:, pl.ds(here.start, length)], out.at[:, pl.ds(there.start, length)], out_sems.at[part]
                )
            )
            copies[-1].start()
        else:
            out[:, there] = total[:, here].astype(out.dtype)
    for copy in copies:
        copy.wait()


def settle(places, grads, bounds, low, high, shift, dtype, width, name):
    slots, size, _ = grads[0].shape
    base, end = max(low - size, 0), min(high + size, width)
    hbm = pl.BlockSpec(memory_space=pl.ANY)
    return pl.pallas_call(
        functools.partial(settle_kernel, size, bounds, low, high, shift),
        in_specs=[pl.BlockSpec(memory_space=pltpu.SMEM)] + [hbm] * len(grads),
        out_specs=hbm if dtype == F32 else pl.BlockSpec(memory_space=pltpu.VMEM),
        out_shape=jax.ShapeDtypeStruct((size, 2 * (high - low)), dtype),
        scratch_shapes=[
            pltpu.VMEM((size, 2 * (end - base)), F32),
            pltpu.VMEM(grads[0].shape, BF16),
            pltpu.SemaphoreType.DMA((slots,)),
            pltpu.SemaphoreType.DMA((2,)),
        ],
        compiler_params=pltpu.CompilerParams(vmem_limit_bytes=VMEM_SMALL),
        cost_estimate=pl.CostEstimate(flops=10**9, bytes_accessed=8 * 2**20, transcendentals=0),
        name=name,
    )(places, *grads)


def finish_kernel(edges, n, own, *refs):
    aboves, out = refs[:n], refs[n]
    wides, adds, sems = refs[n + 1 : 2 * n + 1], refs[2 * n + 1 : 3 * n + 1], refs[3 * n + 1]
    width = out.shape[2]
    loads, outs = [], []

    def copied(source, target, to):
        to.append(pltpu.make_async_copy(source, target, sems.at[len(loads) + len(outs)]))
        to[-1].start()

    for i in range(n):
        length = edges[i + 1] - edges[i]
        for part in range(2):
            copied(
                own.at[:, pl.ds(part * width + edges[i], length)], wides[i].at[:, pl.ds(part * length, length)], loads
            )
        copied(aboves[i], adds[i], loads)
    for i in range(n):
        for copy in loads[3 * i : 3 * i + 3]:
            copy.wait()
        length = edges[i + 1] - edges[i]
        for part in range(2):
            cols = slice(part * length, (part + 1) * length)
            wides[i][:, cols] += adds[i][:, cols].astype(F32)
            copied(wides[i].at[:, pl.ds(part * length, length)], out.at[:, part, pl.ds(edges[i], length)], outs)
    for copy in outs:
        copy.wait()


def finish(own, aboves, edges, width):
    n = len(aboves)
    hbm = pl.BlockSpec(memory_space=pl.ANY)
    return pl.pallas_call(
        functools.partial(finish_kernel, edges, n),
        in_specs=[hbm] * (n + 1),
        out_specs=hbm,
        out_shape=jax.ShapeDtypeStruct((own.shape[0], 2, width), F32),
        scratch_shapes=[pltpu.VMEM(x.shape, F32) for x in aboves]
        + [pltpu.VMEM(x.shape, BF16) for x in aboves]
        + [pltpu.SemaphoreType.DMA((5 * n,))],
        compiler_params=pltpu.CompilerParams(vmem_limit_bytes=VMEM_SMALL),
        cost_estimate=pl.CostEstimate(flops=10**6, bytes_accessed=10 * 2**20, transcendentals=0),
        name="finish",
    )(own, *aboves)


def passed_along(x, axis, by):
    length = lax.axis_size(axis)
    pairs = [(i, i + by) for i in range(length) if 0 <= i + by < length]
    return lax.ppermute(x, axis, pairs)


def unpack_kernel(order, *refs):
    n = (len(refs) - 4) // 2
    out, wide, narrow, sems = refs[2 * n :]
    rows = wide.shape[1]
    size = out.shape[1]
    span = min(rows, size)
    for core in range(2):

        @pl.when(order[n] == core)
        def _():
            for i in range(n):
                pltpu.make_async_copy(refs[core * n + i], narrow.at[i], sems.at[0, i]).start()

    copies = []
    for i in range(n):
        pltpu.make_async_copy(refs[i], narrow.at[i], sems.at[0, i]).wait()
        wide[i] = narrow[i].astype(F32)
        for j in range(rows // span):
            line = order[i] * rows + j * span
            mode = line // size
            at = pl.multiple_of(line % size, 8)
            for part in range(2):
                copies.append(
                    pltpu.make_async_copy(
                        wide.at[i, pl.ds(j * span, span), pl.ds(part * size, size)],
                        out.at[mode, pl.ds(at, span), part, :],
                        sems.at[1, len(copies)],
                    )
                )
                copies[-1].start()
    for copy in copies:
        copy.wait()


def unpacked(pieces, others, order, shape):
    n = len(pieces)
    rows, columns = pieces[0].shape
    hbm = pl.BlockSpec(memory_space=pl.ANY)
    return pl.pallas_call(
        unpack_kernel,
        in_specs=[pl.BlockSpec(memory_space=pltpu.SMEM)] + [hbm] * (2 * n),
        out_specs=hbm,
        out_shape=jax.ShapeDtypeStruct(shape, F32),
        scratch_shapes=[
            pltpu.VMEM((n, rows, columns), F32),
            pltpu.VMEM((n, rows, columns), BF16),
            pltpu.SemaphoreType.DMA((2, 2 * n * max(1, rows // shape[1]))),
        ],
        compiler_params=pltpu.CompilerParams(vmem_limit_bytes=VMEM_SMALL),
        cost_estimate=pl.CostEstimate(flops=10**6, bytes_accessed=4 * 2**20, transcendentals=0),
        name="unpack",
    )(order, *pieces, *others)


def near_chips(axis):
    return min(4, lax.axis_size(axis) // 2)


def piece_order(axis):
    near = near_chips(axis)
    me = lax.axis_index(axis)
    core, spot = me % 2, me // 2 % near
    return jnp.stack([spot ^ s for s in range(near)] + [core])


def hop(axis, shift, stride):
    return [(i, i ^ (2 * stride * shift)) for i in range(0, lax.axis_size(axis), 2)]


def paired_kernel(order, given, sibling, *refs):
    n = len(refs) - 3
    outs, mine, other, sems = refs[:n], refs[-3], refs[-2], refs[-1]
    rows = mine.shape[1]
    copies = []
    for i in range(n):
        at = pl.ds(pl.multiple_of(order[i] * rows, 16), rows)
        copies.append(
            [
                pltpu.make_async_copy(given.at[at], mine.at[i], sems.at[0, i]),
                pltpu.make_async_copy(sibling.at[at], other.at[i], sems.at[1, i]),
            ]
        )
        for copy in copies[-1]:
            copy.start()
    for i in range(n):
        for copy in copies[i]:
            copy.wait()
        outs[i][...] = (mine[i].astype(F32) + other[i].astype(F32)).astype(BF16)


def paired(given, sibling, order, n):
    rows, columns = given.shape[0] // n, given.shape[1]
    hbm = pl.BlockSpec(memory_space=pl.ANY)
    return pl.pallas_call(
        paired_kernel,
        in_specs=[pl.BlockSpec(memory_space=pltpu.SMEM), hbm, hbm],
        out_specs=[pl.BlockSpec(memory_space=pltpu.VMEM)] * n,
        out_shape=[jax.ShapeDtypeStruct((rows, columns), BF16)] * n,
        scratch_shapes=[
            pltpu.VMEM((n, rows, columns), BF16),
            pltpu.VMEM((n, rows, columns), BF16),
            pltpu.SemaphoreType.DMA((2, n)),
        ],
        compiler_params=pltpu.CompilerParams(vmem_limit_bytes=VMEM_SMALL),
        cost_estimate=pl.CostEstimate(flops=10**6, bytes_accessed=3 * 2**20, transcendentals=0),
        name="paired",
    )(order, given, sibling)


def summed(given, axis, shape, order, beside, during, between, last):
    length = lax.axis_size(axis)
    near = near_chips(axis)
    far = length // 2 // near
    inward = [(i + 1, i) for i in range(0, length, 2)]
    outward = [(i, i + 1) for i in range(0, length, 2)]
    modes, size, columns = given.shape
    sibling = beside(lax.ppermute(given, axis, inward))
    flat = (modes * size, columns)
    parts = paired(given.reshape(flat), sibling.reshape(flat), order, near)
    got = [lax.ppermute(parts[s], axis, hop(axis, s, 1)) for s in range(1, near)]
    got = during(got)
    total = parts[0].astype(F32)
    for piece in got:
        total = total + piece.astype(F32)
    sent = total.astype(BF16)
    others = [lax.ppermute(sent, axis, hop(axis, s, near)) for s in range(1, far)]
    if others:
        others[0] = between(others[0])
    for piece in others:
        total = total + piece.astype(F32)
    total = total.astype(BF16)
    pieces = [total] + [lax.ppermute(total, axis, hop(axis, s, 1)) for s in range(1, near)]
    others = [lax.ppermute(piece, axis, outward) for piece in pieces]
    return unpacked(pieces, others, last(order), shape)


def column_bounds(width, shares):
    return tuple([0] + [round(width * share / LANES) * LANES for share in shares] + [width])


def shards(object_tiles, probe, measured, offset_row, offset_col, subpixel, live_count):
    rows, _, width = object_tiles.shape
    modes, size = probe.shape[:2]
    tables = dft_tables(size)
    bounds = column_bounds(width, (0.4375, 0.75))
    stages = len(bounds) - 1
    rims = [
        passed_along(object_tiles[:size, :, low:high].reshape(size, 2 * (high - low)), "row", -1)
        for low, high in zip(bounds[:-1], bounds[1:])
    ]
    core = lax.axis_index("row") % 2
    places = jnp.stack(
        [offset_row, offset_col, subpixel] + [jnp.broadcast_to(x, offset_row.shape) for x in (live_count, core)]
    )
    places, order = lax.optimization_barrier((places, piece_order("row")))
    own = object_tiles.reshape(rows, 2 * width)
    flat = probe.reshape(modes, size, 2 * size)
    carried = None
    grads = []
    for stage in range(stages):
        moved, grad, *rest = project(stage, bounds, places, own, rims, flat, measured, tables, width, carried)
        grads.append(grad)
        carried = [moved] + rest
    given = carried[1]
    edges = (0, width // 2 // LANES * LANES, width)
    belows = [
        settle(places, grads, bounds, low, high, size, BF16, width, f"below_{low}")
        for low, high in zip(edges[:-1], edges[1:])
    ]
    aboves = [passed_along(belows[0], "row", 1)]
    held = {}

    def beside(x):
        return lax.optimization_barrier((x, belows[0]))[0]

    def during(x):
        x, aboves[0], held["below"] = lax.optimization_barrier((x, aboves[0], belows[1]))
        return x

    def between(x):
        aboves.append(passed_along(held["below"], "row", 1))
        own_rows = settle(places, grads, bounds, 0, width, 0, F32, width, "own_rows")
        x, aboves[1], held["own"] = lax.optimization_barrier((x, aboves[1], own_rows))
        return x

    def last(x):
        object_grad = finish(held["own"], aboves, edges, width)
        x, held["object_grad"] = lax.optimization_barrier((x, object_grad))
        return x

    probe_grad = summed(given, "row", probe.shape, order, beside, during, between, last)
    object_grad = held["object_grad"]
    return object_grad, probe_grad, moved


def solution(mesh):
    in_specs = (
        P(("groups", "row"), None, None),
        P(),
        P(("groups", "row"), None, None),
        P(("groups", "row")),
        P(("groups", "row")),
        P(("groups", "row")),
        P(("groups", "row")),
    )
    out_specs = (
        P(("groups", "row"), None, None),
        P("groups", None, None, None),
        P(None, ("groups", "row")),
    )
    return jax.shard_map(shards, mesh=mesh, in_specs=in_specs, out_specs=out_specs, check_vma=False)
```

```python
import functools
import math

import jax
import jax.numpy as jnp
import ml_dtypes
import numpy as np
from jax import lax
from jax.experimental import pallas as pl
from jax.experimental.pallas import tpu as pltpu
from jax.sharding import PartitionSpec as P

F32 = jnp.float32
BF16 = jnp.bfloat16
LANES = 128
VMEM_BYTES = 26 * 2**20
VMEM_SMALL = 16 * 2**20


def dft_tables(size):
    half = size // 2
    index = np.arange(size)
    angle = (index[:, None] * index[None, :] % size) * (2.0 * math.pi / size)
    scale = 1.0 / math.sqrt(size)
    cosine = (np.cos(angle) * scale).astype(ml_dtypes.bfloat16)
    sine = (np.sin(angle) * scale).astype(ml_dtypes.bfloat16)
    tables = []
    for parity in (0, 1):
        c, s = cosine[:half, parity::2], sine[:half, parity::2]
        tables.append(np.block([[c, -s], [s, c]]))
    order = np.zeros((size, size), ml_dtypes.bfloat16)
    order[2 * index[:half], index[:half]] = 1
    order[2 * index[:half] + 1, half + index[:half]] = 1
    even, odd = tables
    return jnp.asarray(np.stack([even, odd, even.T, odd.T, order, order.T]))


def dot(left, right):
    return jnp.dot(left, right, preferred_element_type=F32)


def fractions(code):
    return (code // 4).astype(F32) * 0.25, (code % 4).astype(F32) * 0.25


def in_stage(places, slot, bounds, stage, size):
    end = places[1, slot] + size + 1
    here = end <= bounds[stage + 1]
    if stage > 0:
        here = jnp.logical_and(here, end > bounds[stage])
    return jnp.logical_and(slot < places[3, 0], here)


def project_kernel(size, width, bounds, stage, places, *refs):
    first_stage, last_stage = stage == 0, stage == len(bounds) - 2
    refs = list(refs)
    own, rim = refs[:2]
    rim_before = None if first_stage else refs[2]
    refs = refs[2:] if first_stage else refs[3:]
    probe_in, measured_in, tables_in = refs[:3]
    refs = refs[3:]
    if not first_stage:
        moved_in, sums_in = refs[:2]
        refs = refs[2:]
    moved, grads = refs[:2]
    refs = refs[2:]
    sums_out = refs.pop(0)
    cells, mixed, patch, folded, half_u, half_v, far, error, back, probe, measured, tables, probe_acc, held = refs[:14]
    sems, slot_sems = refs[14:16]
    if last_stage and not first_stage:
        sums, given = refs[16:]
    elif last_stage:
        given = refs[16]
    even, odd, even_t, odd_t, order, order_t = [tables.at[i] for i in range(6)]
    half = size // 2
    modes = probe.shape[0]
    slots = measured.shape[0]
    rows = own.shape[0]
    low, high = bounds[stage], bounds[stage + 1]
    base = 0 if first_stage else low - size
    extent = high - base
    count = places[3, 0]
    copies = []

    def load(source, target):
        copies.append(pltpu.make_async_copy(source, target, sems.at[len(copies)]))

    for part in range(2):
        load(
            own.at[:, pl.ds(part * width + base, extent)],
            cells.at[pl.ds(0, rows), pl.ds(part * extent, extent)],
        )
        load(
            rim.at[:, pl.ds(part * (high - low), high - low)],
            cells.at[pl.ds(rows, size), pl.ds(part * extent + low - base, high - low)],
        )
        if not first_stage:
            before = low - bounds[stage - 1]
            load(
                rim_before.at[:, pl.ds((part + 1) * before - size, size)],
                cells.at[pl.ds(rows, size), pl.ds(part * extent, size)],
            )
    n_cells = len(copies)
    load(tables_in, tables)
    load(probe_in, probe)
    load(measured_in, measured)
    n_later = len(copies)
    if not first_stage:
        load(sums_in, sums if last_stage else probe_acc)
    for copy in copies:
        copy.start()
    if last_stage or first_stage:
        probe_acc[...] = jnp.zeros_like(probe_acc)
    cells[rows + size :] = jnp.zeros((cells.shape[0] - rows - size, cells.shape[1]), BF16)
    for slot in range(slots):
        for axis in range(2):
            moved[axis, slot] = 0.0 if first_stage else moved_in[axis, slot]
    for copy in copies[:n_cells]:
        copy.wait()

    def wait_later():
        for copy in copies[n_cells : n_later if last_stage else len(copies)]:
            copy.wait()

    def mine(slot):
        return in_stage(places, slot, bounds, stage, size)

    def sent_out(slot):
        return pltpu.make_async_copy(held.at[slot], grads.at[slot], slot_sems.at[slot])

    first_slot = jnp.int32(slots)
    for slot in reversed(range(slots)):
        first_slot = jnp.where(mine(slot), slot, first_slot)

    block = 16
    blocks = size // block
    lift_rows = half + 8
    lift_from = half + 32

    def one_slot(slot):
        top = places[0, slot]
        left = places[1, slot]
        frac_y, frac_x = fractions(places[2, slot])
        row0 = pl.multiple_of((top // 16) * 16, 16)
        col0 = pl.multiple_of((left // LANES) * LANES - base, LANES)
        down = top - row0
        across = left - base - col0
        source = lax.broadcasted_iota(jnp.int32, (2 * LANES, LANES), 0)
        target = lax.broadcasted_iota(jnp.int32, (2 * LANES, LANES), 1) + across
        here = (source == target).astype(F32)
        after = (source == target + 1).astype(F32)
        blend = jnp.concatenate([(1.0 - frac_x) * here + frac_x * after, after - here], axis=1).astype(BF16)
        source = lax.broadcasted_iota(jnp.int32, (lift_rows, lift_from), 1)
        target = lax.broadcasted_iota(jnp.int32, (lift_rows, lift_from), 0) + down
        lifts = [(source == target + shift).astype(F32).astype(BF16) for shift in (0, 8)]
        for part in range(2):
            start = pl.multiple_of(col0 + part * extent, LANES)
            for piece in range(2):
                taken = pl.ds(pl.multiple_of(row0 + piece * half, 16), lift_from)
                window = dot(lifts[piece], cells[taken, pl.ds(start, size + LANES)]).astype(BF16)
                for h in range(size // LANES):
                    mixed[part, pl.ds(piece * lift_rows, lift_rows), h * size : (h + 1) * size] = dot(
                        window[:, h * LANES : (h + 2) * LANES], blend
                    )
        for part in range(2):
            for h in range(size // LANES):
                cols = slice(h * size, h * size + LANES)
                for b in range(0, size, block):
                    upper = mixed[part, pl.ds(b, block), cols]
                    lower = mixed[part, pl.ds(b + 1, block), cols]
                    to = slice(part * size + h * LANES, part * size + (h + 1) * LANES)
                    patch[pl.ds(b, block), to] = (1.0 - frac_y) * upper + frac_y * lower
        pl.when(slot == first_slot)(wait_later)

        for mode in range(modes):
            for b in range(blocks):
                at = slice(b * block, (b + 1) * block)
                spot = (2 * b if b < blocks // 2 else 2 * b + 1 - blocks) * block
                to = slice(spot, spot + block)
                preal, pimag = probe[mode, at, :size], probe[mode, at, size:]
                oreal, oimag = patch[at, :size], patch[at, size:]
                wreal = preal * oreal - pimag * oimag
                wimag = preal * oimag + pimag * oreal
                for part, wave in enumerate((wreal, wimag)):
                    folded[mode, to, part * half : (part + 1) * half] = (wave[:, :half] + wave[:, half:]).astype(BF16)
                    folded[mode, to, size + part * half : size + (part + 1) * half] = (
                        wave[:, :half] - wave[:, half:]
                    ).astype(BF16)
        for mode in range(modes):
            for k, table in enumerate((even, odd)):
                out = dot(folded[mode, :, k * size : (k + 1) * size], table[...])
                for b in range(blocks // 2):
                    upper = out[2 * b * block : (2 * b + 1) * block]
                    lower = out[(2 * b + 1) * block : (2 * b + 2) * block]
                    plus, minus = (upper + lower).astype(BF16), (upper - lower).astype(BF16)
                    for part in range(2):
                        to = slice(part * half + b * block, part * half + (b + 1) * block)
                        cols = slice(part * half, (part + 1) * half)
                        half_u[mode, to, k * half : (k + 1) * half] = plus[:, cols]
                        half_v[mode, to, k * half : (k + 1) * half] = minus[:, cols]
        for mode in range(modes):
            far[mode, 0] = dot(even_t[...], half_u[mode])
            far[mode, 1] = dot(odd_t[...], half_v[mode])

        amplitude = dot(dot(order_t[...], measured[slot]).astype(BF16), order[...])
        for k in range(2):
            for b in range(0, half, block):
                pieces = [
                    [far[mode, k, part * half + b : part * half + b + block, :] for part in range(2)]
                    for mode in range(modes)
                ]
                power = sum(p * p for pair in pieces for p in pair)
                level = amplitude[k * half + b : k * half + b + block]
                ratio = 1.0 - level / jnp.maximum(jnp.sqrt(power), 0.5)
                for mode in range(modes):
                    for part in range(2):
                        to = slice(part * half + b, part * half + b + block)
                        error[mode, k, to, :] = (pieces[mode][part] * ratio).astype(BF16)

        for mode in range(modes):
            first = dot(even[...], error[mode, 0])
            second = dot(odd[...], error[mode, 1])
            plus, minus = (first + second).astype(BF16), (first - second).astype(BF16)
            for part in range(2):
                for b in range(blocks):
                    pick = part * half + (b % (blocks // 2)) * block
                    piece = (plus if b < blocks // 2 else minus)[pick : pick + block]
                    to = slice((b * modes + mode) * block, (b * modes + mode + 1) * block)
                    for c in range(2):
                        cols = slice(c * size + part * half, c * size + (part + 1) * half)
                        back[to, cols] = piece[:, c * half : (c + 1) * half]

        total_y = jnp.zeros((block, half), F32)
        total_x = jnp.zeros((block, half), F32)
        group = size // (modes * block)
        for g in range(blocks // group):
            span = slice(g * size, (g + 1) * size)
            first = dot(back[span, :size], even_t[...])
            second = dot(back[span, size:], odd_t[...])
            for r in range(group):
                at = slice((g * group + r) * block, (g * group + r + 1) * block)
                below = slice(at.start + 1, at.stop + 1)
                for h in range(2):
                    re = slice(h * half, (h + 1) * half)
                    im = slice(size + h * half, size + (h + 1) * half)
                    oreal, oimag = patch[at, re], patch[at, im]
                    greal = jnp.zeros((block, half), F32)
                    gimag = jnp.zeros((block, half), F32)
                    for mode in range(modes):
                        part = slice((r * modes + mode) * block, (r * modes + mode + 1) * block)
                        piece = first[part] + second[part] if h == 0 else first[part] - second[part]
                        ureal, uimag = piece[:, :half], piece[:, half:]
                        preal, pimag = probe[mode, at, re], probe[mode, at, im]
                        greal += preal * ureal + pimag * uimag
                        gimag += preal * uimag - pimag * ureal
                        probe_acc[mode, at, re] += oreal * ureal + oimag * uimag
                        probe_acc[mode, at, im] += oreal * uimag - oimag * ureal
                    held[slot, at, re] = greal.astype(BF16)
                    held[slot, at, im] = gimag.astype(BF16)
                    for part, grad in enumerate((greal, gimag)):
                        cols = slice(h * size, h * size + LANES)
                        total_y += grad * (mixed[part, below, cols] - mixed[part, at, cols])
                        cols = slice(h * size + LANES, (h + 1) * size)
                        total_x += grad * ((1.0 - frac_y) * mixed[part, at, cols] + frac_y * mixed[part, below, cols])
        moved[0, slot] = jnp.sum(total_y) / size
        moved[1, slot] = jnp.sum(total_x) / size

        sent_out(slot).start()

    @pl.loop(0, slots)
    def _(slot):
        pl.when(mine(slot))(functools.partial(one_slot, slot))

    pl.when(first_slot == slots)(wait_later)
    outs = []

    def store(source, target):
        outs.append(pltpu.make_async_copy(source, target, sems.at[len(outs)]))
        outs[-1].start()

    if last_stage:
        if first_stage:
            given[...] = probe_acc[...].astype(BF16)
        else:
            copies[-1].wait()
            for mode in range(modes):
                given[mode] = (probe_acc[mode] + sums[mode]).astype(BF16)
        store(given, sums_out)
    else:
        store(probe_acc, sums_out)

    @pl.loop(0, slots)
    def _(slot):
        @pl.when(mine(slot))
        def _():
            sent_out(slot).wait()

    for out in outs:
        out.wait()


def project(stage, bounds, places, own, rims, probe, measured, tables, width, carried):
    slots, size, _ = measured.shape
    modes = probe.shape[0]
    rows = own.shape[0]
    smem = pl.BlockSpec(memory_space=pltpu.SMEM)
    hbm = pl.BlockSpec(memory_space=pl.ANY)
    first_stage, last_stage = stage == 0, stage == len(bounds) - 2
    low, high = bounds[stage], bounds[stage + 1]
    extent = high - (0 if first_stage else low - size)
    inputs = [places, own, rims[stage]] + ([] if first_stage else [rims[stage - 1]]) + [probe, measured, tables]
    specs = [smem] + [hbm] * (len(inputs) - 1)
    outs = [
        jax.ShapeDtypeStruct((2, slots), F32),
        jax.ShapeDtypeStruct((slots, size, 2 * size), BF16),
        jax.ShapeDtypeStruct(probe.shape, BF16 if last_stage else F32),
    ]
    if not first_stage:
        inputs += list(carried)
        specs += [smem, hbm]
    scratch = [
        pltpu.VMEM((rows + size + 32, 2 * extent), BF16),
        pltpu.VMEM((2, size + 16, 2 * size), F32),
        pltpu.VMEM((size, 2 * size), F32),
        pltpu.VMEM((modes, size, 2 * size), BF16),
        pltpu.VMEM((modes, size, size), BF16),
        pltpu.VMEM((modes, size, size), BF16),
        pltpu.VMEM((modes, 2, size, size), F32),
        pltpu.VMEM((modes, 2, size, size), BF16),
        pltpu.VMEM((modes * size, 2 * size), BF16),
        pltpu.VMEM(probe.shape, F32),
        pltpu.VMEM(measured.shape, BF16),
        pltpu.VMEM(tables.shape, BF16),
        pltpu.VMEM(probe.shape, F32),
        pltpu.VMEM((slots, size, 2 * size), BF16),
        pltpu.SemaphoreType.DMA((12,)),
        pltpu.SemaphoreType.DMA((slots,)),
    ]
    if last_stage and not first_stage:
        scratch.append(pltpu.VMEM(probe.shape, F32))
    if last_stage:
        scratch.append(pltpu.VMEM(probe.shape, BF16))
    return pl.pallas_call(
        functools.partial(project_kernel, size, width, bounds, stage),
        in_specs=specs,
        out_specs=[smem] + [hbm] * (len(outs) - 1),
        out_shape=outs,
        scratch_shapes=scratch,
        compiler_params=pltpu.CompilerParams(vmem_limit_bytes=VMEM_BYTES),
        cost_estimate=pl.CostEstimate(flops=8 * 10**9, bytes_accessed=16 * 2**20, transcendentals=0),
        name=f"project_{stage}",
    )(*inputs)


def settle_kernel(size, bounds, low, high, shift, places, *refs):
    grads = refs[: len(refs) - 5]
    out, total, held, sems, out_sems = refs[len(refs) - 5 :]
    slots = held.shape[0]
    reach = size + LANES
    base = max(low - size, 0)
    extent = total.shape[1] // 2
    length = high - low

    def taken(stage, slot):
        left = places[1, slot]
        within = jnp.logical_and(left < high, left + size + 1 > low)
        return jnp.logical_and(within, in_stage(places, slot, bounds, stage, size))

    def fetch(stage, slot):
        return pltpu.make_async_copy(grads[stage].at[slot], held.at[slot], sems.at[slot])

    for stage in range(len(grads)):

        @pl.loop(0, slots)
        def _(slot, stage=stage):
            @pl.when(taken(stage, slot))
            def _():
                fetch(stage, slot).start()

    total[...] = jnp.zeros_like(total)

    def one_slot(stage, slot):
        left = places[1, slot]
        frac_y, frac_x = fractions(places[2, slot])
        col0 = (left // LANES) * LANES
        ahead = lax.broadcasted_iota(jnp.int32, (size, reach), 1) - lax.broadcasted_iota(jnp.int32, (size, reach), 0)
        ahead = ahead - (left - col0)
        along = jnp.where(ahead == 0, 1.0 - frac_x, jnp.where(ahead == 1, frac_x, 0.0)).astype(BF16)
        ahead = lax.broadcasted_iota(jnp.int32, (size, size), 0) - lax.broadcasted_iota(jnp.int32, (size, size), 1)
        ahead = ahead - (places[0, slot] - shift)
        down = jnp.where(ahead == 0, 1.0 - frac_y, jnp.where(ahead == 1, frac_y, 0.0)).astype(BF16)
        fetch(stage, slot).wait()
        for part in range(2):
            wide = dot(held[slot, :, part * size : (part + 1) * size], along).astype(BF16)
            start = pl.multiple_of(col0 - base + part * extent, LANES)
            total[:, pl.ds(start, reach)] += dot(down, wide)

    for stage in range(len(grads)):

        @pl.loop(0, slots)
        def _(slot, stage=stage):
            pl.when(taken(stage, slot))(functools.partial(one_slot, stage, slot))

    copies = []
    for part in range(2):
        here = slice(part * extent + low - base, part * extent + low - base + length)
        there = slice(part * length, (part + 1) * length)
        if out.dtype == F32:
            copies.append(
                pltpu.make_async_copy(
                    total.at[:, pl.ds(here.start, length)], out.at[:, pl.ds(there.start, length)], out_sems.at[part]
                )
            )
            copies[-1].start()
        else:
            out[:, there] = total[:, here].astype(out.dtype)
    for copy in copies:
        copy.wait()


def settle(places, grads, bounds, low, high, shift, dtype, width, name):
    slots, size, _ = grads[0].shape
    base, end = max(low - size, 0), min(high + size, width)
    hbm = pl.BlockSpec(memory_space=pl.ANY)
    return pl.pallas_call(
        functools.partial(settle_kernel, size, bounds, low, high, shift),
        in_specs=[pl.BlockSpec(memory_space=pltpu.SMEM)] + [hbm] * len(grads),
        out_specs=hbm if dtype == F32 else pl.BlockSpec(memory_space=pltpu.VMEM),
        out_shape=jax.ShapeDtypeStruct((size, 2 * (high - low)), dtype),
        scratch_shapes=[
            pltpu.VMEM((size, 2 * (end - base)), F32),
            pltpu.VMEM(grads[0].shape, BF16),
            pltpu.SemaphoreType.DMA((slots,)),
            pltpu.SemaphoreType.DMA((2,)),
        ],
        compiler_params=pltpu.CompilerParams(vmem_limit_bytes=VMEM_SMALL),
        cost_estimate=pl.CostEstimate(flops=10**9, bytes_accessed=8 * 2**20, transcendentals=0),
        name=name,
    )(places, *grads)


def finish_kernel(edges, n, own, *refs):
    aboves, out = refs[:n], refs[n]
    wides, adds, sems = refs[n + 1 : 2 * n + 1], refs[2 * n + 1 : 3 * n + 1], refs[3 * n + 1]
    width = out.shape[2]
    loads, outs = [], []

    def copied(source, target, to):
        to.append(pltpu.make_async_copy(source, target, sems.at[len(loads) + len(outs)]))
        to[-1].start()

    for i in range(n):
        length = edges[i + 1] - edges[i]
        for part in range(2):
            copied(
                own.at[:, pl.ds(part * width + edges[i], length)], wides[i].at[:, pl.ds(part * length, length)], loads
            )
        copied(aboves[i], adds[i], loads)
    for i in range(n):
        for copy in loads[3 * i : 3 * i + 3]:
            copy.wait()
        length = edges[i + 1] - edges[i]
        for part in range(2):
            cols = slice(part * length, (part + 1) * length)
            wides[i][:, cols] += adds[i][:, cols].astype(F32)
            copied(wides[i].at[:, pl.ds(part * length, length)], out.at[:, part, pl.ds(edges[i], length)], outs)
    for copy in outs:
        copy.wait()


def finish(own, aboves, edges, width):
    n = len(aboves)
    hbm = pl.BlockSpec(memory_space=pl.ANY)
    return pl.pallas_call(
        functools.partial(finish_kernel, edges, n),
        in_specs=[hbm] * (n + 1),
        out_specs=hbm,
        out_shape=jax.ShapeDtypeStruct((own.shape[0], 2, width), F32),
        scratch_shapes=[pltpu.VMEM(x.shape, F32) for x in aboves]
        + [pltpu.VMEM(x.shape, BF16) for x in aboves]
        + [pltpu.SemaphoreType.DMA((5 * n,))],
        compiler_params=pltpu.CompilerParams(vmem_limit_bytes=VMEM_SMALL),
        cost_estimate=pl.CostEstimate(flops=10**6, bytes_accessed=10 * 2**20, transcendentals=0),
        name="finish",
    )(own, *aboves)


def passed_along(x, axis, by):
    length = lax.axis_size(axis)
    pairs = [(i, i + by) for i in range(length) if 0 <= i + by < length]
    return lax.ppermute(x, axis, pairs)


def unpack_kernel(order, *refs):
    n = (len(refs) - 4) // 2
    out, wide, narrow, sems = refs[2 * n :]
    rows = wide.shape[1]
    size = out.shape[1]
    span = min(rows, size)
    for core in range(2):

        @pl.when(order[n] == core)
        def _():
            for i in range(n):
                pltpu.make_async_copy(refs[core * n + i], narrow.at[i], sems.at[0, i]).start()

    copies = []
    for i in range(n):
        pltpu.make_async_copy(refs[i], narrow.at[i], sems.at[0, i]).wait()
        wide[i] = narrow[i].astype(F32)
        for j in range(rows // span):
            line = order[i] * rows + j * span
            mode = line // size
            at = pl.multiple_of(line % size, 8)
            for part in range(2):
                copies.append(
                    pltpu.make_async_copy(
                        wide.at[i, pl.ds(j * span, span), pl.ds(part * size, size)],
                        out.at[mode, pl.ds(at, span), part, :],
                        sems.at[1, len(copies)],
                    )
                )
                copies[-1].start()
    for copy in copies:
        copy.wait()


def unpacked(pieces, others, order, shape):
    n = len(pieces)
    rows, columns = pieces[0].shape
    hbm = pl.BlockSpec(memory_space=pl.ANY)
    return pl.pallas_call(
        unpack_kernel,
        in_specs=[pl.BlockSpec(memory_space=pltpu.SMEM)] + [hbm] * (2 * n),
        out_specs=hbm,
        out_shape=jax.ShapeDtypeStruct(shape, F32),
        scratch_shapes=[
            pltpu.VMEM((n, rows, columns), F32),
            pltpu.VMEM((n, rows, columns), BF16),
            pltpu.SemaphoreType.DMA((2, 2 * n * max(1, rows // shape[1]))),
        ],
        compiler_params=pltpu.CompilerParams(vmem_limit_bytes=VMEM_SMALL),
        cost_estimate=pl.CostEstimate(flops=10**6, bytes_accessed=4 * 2**20, transcendentals=0),
        name="unpack",
    )(order, *pieces, *others)


def near_chips(axis):
    return min(4, lax.axis_size(axis) // 2)


def piece_order(axis):
    near = near_chips(axis)
    me = lax.axis_index(axis)
    core, spot = me % 2, me // 2 % near
    return jnp.stack([spot ^ s for s in range(near)] + [core])


def hop(axis, shift, stride):
    return [(i, i ^ (2 * stride * shift)) for i in range(0, lax.axis_size(axis), 2)]


def paired_kernel(order, given, sibling, *refs):
    n = len(refs) - 3
    outs, mine, other, sems = refs[:n], refs[-3], refs[-2], refs[-1]
    rows = mine.shape[1]
    copies = []
    for i in range(n):
        at = pl.ds(pl.multiple_of(order[i] * rows, 16), rows)
        copies.append(
            [
                pltpu.make_async_copy(given.at[at], mine.at[i], sems.at[0, i]),
                pltpu.make_async_copy(sibling.at[at], other.at[i], sems.at[1, i]),
            ]
        )
        for copy in copies[-1]:
            copy.start()
    for i in range(n):
        for copy in copies[i]:
            copy.wait()
        outs[i][...] = (mine[i].astype(F32) + other[i].astype(F32)).astype(BF16)


def paired(given, sibling, order, n):
    rows, columns = given.shape[0] // n, given.shape[1]
    hbm = pl.BlockSpec(memory_space=pl.ANY)
    return pl.pallas_call(
        paired_kernel,
        in_specs=[pl.BlockSpec(memory_space=pltpu.SMEM), hbm, hbm],
        out_specs=[pl.BlockSpec(memory_space=pltpu.VMEM)] * n,
        out_shape=[jax.ShapeDtypeStruct((rows, columns), BF16)] * n,
        scratch_shapes=[
            pltpu.VMEM((n, rows, columns), BF16),
            pltpu.VMEM((n, rows, columns), BF16),
            pltpu.SemaphoreType.DMA((2, n)),
        ],
        compiler_params=pltpu.CompilerParams(vmem_limit_bytes=VMEM_SMALL),
        cost_estimate=pl.CostEstimate(flops=10**6, bytes_accessed=3 * 2**20, transcendentals=0),
        name="paired",
    )(order, given, sibling)


def summed(given, axis, shape, order, during, between, gathered, last):
    length = lax.axis_size(axis)
    near = near_chips(axis)
    far = length // 2 // near
    inward = [(i + 1, i) for i in range(0, length, 2)]
    outward = [(i, i + 1) for i in range(0, length, 2)]
    modes, size, columns = given.shape
    sibling = lax.ppermute(given, axis, inward)
    flat = (modes * size, columns)
    parts = paired(given.reshape(flat), sibling.reshape(flat), order, near)
    got = [lax.ppermute(parts[s], axis, hop(axis, s, 1)) for s in range(1, near)]
    got = during(got)
    total = parts[0].astype(F32)
    for piece in got:
        total = total + piece.astype(F32)
    sent = total.astype(BF16)
    others = [lax.ppermute(sent, axis, hop(axis, s, near)) for s in range(1, far)]
    others = between(others)
    for piece in others:
        total = total + piece.astype(F32)
    total = gathered(total.astype(BF16))
    pieces = [total] + [lax.ppermute(total, axis, hop(axis, s, 1)) for s in range(1, near)]
    pieces, order = last(pieces, order)
    others = [lax.ppermute(piece, axis, outward) for piece in pieces]
    return unpacked(pieces, others, order, shape)


def column_bounds(width, shares):
    return tuple([0] + [round(width * share / LANES) * LANES for share in shares] + [width])


def shards(object_tiles, probe, measured, offset_row, offset_col, subpixel, live_count):
    rows, _, width = object_tiles.shape
    modes, size = probe.shape[:2]
    tables = dft_tables(size)
    bounds = column_bounds(width, (0.4375, 0.75))
    stages = len(bounds) - 1
    rims = [
        passed_along(object_tiles[:size, :, low:high].reshape(size, 2 * (high - low)), "row", -1)
        for low, high in zip(bounds[:-1], bounds[1:])
    ]
    core = lax.axis_index("row") % 2
    places = jnp.stack(
        [offset_row, offset_col, subpixel] + [jnp.broadcast_to(x, offset_row.shape) for x in (live_count, core)]
    )
    places, order = lax.optimization_barrier((places, piece_order("row")))
    own = object_tiles.reshape(rows, 2 * width)
    flat = probe.reshape(modes, size, 2 * size)
    carried = None
    grads = []
    for stage in range(stages):
        moved, grad, *rest = project(stage, bounds, places, own, rims, flat, measured, tables, width, carried)
        grads.append(grad)
        carried = [moved] + rest
    given = carried[1]
    edges = (0, width // 2 // LANES * LANES, width)
    belows = [
        settle(places, grads, bounds, low, high, size, BF16, width, f"below_{low}")
        for low, high in zip(edges[:-1], edges[1:])
    ]
    aboves, held = [], {}

    def during(got):
        got, held["low"] = lax.optimization_barrier((got, belows[0]))
        return got

    def between(x):
        aboves.append(passed_along(held["low"], "row", 1))
        x, held["high"] = lax.optimization_barrier((x, belows[1]))
        return x

    def gathered(x):
        x, aboves[0] = lax.optimization_barrier((x, aboves[0]))
        return x

    def last(pieces, order):
        pieces, high, held["places"] = lax.optimization_barrier((pieces, held["high"], places))
        aboves.append(passed_along(high, "row", 1))
        return pieces, order

    probe_grad = summed(given, "row", probe.shape, order, during, between, gathered, last)
    own_rows = settle(held["places"], grads, bounds, 0, width, 0, F32, width, "own_rows")
    object_grad = finish(own_rows, aboves, edges, width)
    return object_grad, probe_grad, moved


def solution(mesh):
    in_specs = (
        P(("groups", "row"), None, None),
        P(),
        P(("groups", "row"), None, None),
        P(("groups", "row")),
        P(("groups", "row")),
        P(("groups", "row")),
        P(("groups", "row")),
    )
    out_specs = (
        P(("groups", "row"), None, None),
        P("groups", None, None, None),
        P(None, ("groups", "row")),
    )
    return jax.shard_map(shards, mesh=mesh, in_specs=in_specs, out_specs=out_specs, check_vma=False)
```

```python
import functools
import math

import jax
import jax.numpy as jnp
import ml_dtypes
import numpy as np
from jax import lax
from jax.experimental import pallas as pl
from jax.experimental.pallas import tpu as pltpu
from jax.sharding import PartitionSpec as P

F32 = jnp.float32
BF16 = jnp.bfloat16
LANES = 128
VMEM_BYTES = 26 * 2**20
VMEM_SMALL = 16 * 2**20


def dft_tables(size):
    half = size // 2
    index = np.arange(size)
    angle = (index[:, None] * index[None, :] % size) * (2.0 * math.pi / size)
    scale = 1.0 / math.sqrt(size)
    cosine = (np.cos(angle) * scale).astype(ml_dtypes.bfloat16)
    sine = (np.sin(angle) * scale).astype(ml_dtypes.bfloat16)
    tables = []
    for parity in (0, 1):
        c, s = cosine[:half, parity::2], sine[:half, parity::2]
        tables.append(np.block([[c, -s], [s, c]]))
    order = np.zeros((size, size), ml_dtypes.bfloat16)
    order[2 * index[:half], index[:half]] = 1
    order[2 * index[:half] + 1, half + index[:half]] = 1
    even, odd = tables
    return jnp.asarray(np.stack([even, odd, even.T, odd.T, order, order.T]))


def dot(left, right):
    return jnp.dot(left, right, preferred_element_type=F32)


def fractions(code):
    return (code // 4).astype(F32) * 0.25, (code % 4).astype(F32) * 0.25


def in_stage(places, slot, bounds, stage, size):
    end = places[1, slot] + size + 1
    here = end <= bounds[stage + 1]
    if stage > 0:
        here = jnp.logical_and(here, end > bounds[stage])
    return jnp.logical_and(slot < places[3, 0], here)


def project_kernel(size, width, bounds, stage, places, *refs):
    first_stage, last_stage = stage == 0, stage == len(bounds) - 2
    refs = list(refs)
    own, rim = refs[:2]
    rim_before = None if first_stage else refs[2]
    refs = refs[2:] if first_stage else refs[3:]
    probe_in, measured_in, tables_in = refs[:3]
    refs = refs[3:]
    if not first_stage:
        moved_in, sums_in = refs[:2]
        refs = refs[2:]
    moved, grads = refs[:2]
    refs = refs[2:]
    sums_out = refs.pop(0)
    cells, mixed, patch, folded, half_u, half_v, far, error, back, probe, measured, tables, probe_acc, held = refs[:14]
    sems, slot_sems = refs[14:16]
    if last_stage and not first_stage:
        sums, given = refs[16:]
    elif last_stage:
        given = refs[16]
    even, odd, even_t, odd_t, order, order_t = [tables.at[i] for i in range(6)]
    half = size // 2
    modes = probe.shape[0]
    slots = measured.shape[0]
    rows = own.shape[0]
    low, high = bounds[stage], bounds[stage + 1]
    base = 0 if first_stage else low - size
    extent = high - base
    count = places[3, 0]
    copies = []

    def load(source, target):
        copies.append(pltpu.make_async_copy(source, target, sems.at[len(copies)]))

    for part in range(2):
        load(
            own.at[:, pl.ds(part * width + base, extent)],
            cells.at[pl.ds(0, rows), pl.ds(part * extent, extent)],
        )
        load(
            rim.at[:, pl.ds(part * (high - low), high - low)],
            cells.at[pl.ds(rows, size), pl.ds(part * extent + low - base, high - low)],
        )
        if not first_stage:
            before = low - bounds[stage - 1]
            load(
                rim_before.at[:, pl.ds((part + 1) * before - size, size)],
                cells.at[pl.ds(rows, size), pl.ds(part * extent, size)],
            )
    n_cells = len(copies)
    load(tables_in, tables)
    load(probe_in, probe)
    load(measured_in, measured)
    n_later = len(copies)
    if not first_stage:
        load(sums_in, sums if last_stage else probe_acc)
    for copy in copies:
        copy.start()
    if last_stage or first_stage:
        probe_acc[...] = jnp.zeros_like(probe_acc)
    cells[rows + size :] = jnp.zeros((cells.shape[0] - rows - size, cells.shape[1]), BF16)
    for slot in range(slots):
        for axis in range(2):
            moved[axis, slot] = 0.0 if first_stage else moved_in[axis, slot]
    for copy in copies[:n_cells]:
        copy.wait()

    def wait_later():
        for copy in copies[n_cells : n_later if last_stage else len(copies)]:
            copy.wait()

    def mine(slot):
        return in_stage(places, slot, bounds, stage, size)

    def sent_out(slot):
        return pltpu.make_async_copy(held.at[slot], grads.at[slot], slot_sems.at[slot])

    first_slot = jnp.int32(slots)
    for slot in reversed(range(slots)):
        first_slot = jnp.where(mine(slot), slot, first_slot)

    block = 16
    blocks = size // block
    lift_rows = half + 8
    lift_from = half + 32

    def one_slot(slot):
        top = places[0, slot]
        left = places[1, slot]
        frac_y, frac_x = fractions(places[2, slot])
        row0 = pl.multiple_of((top // 16) * 16, 16)
        col0 = pl.multiple_of((left // LANES) * LANES - base, LANES)
        down = top - row0
        across = left - base - col0
        source = lax.broadcasted_iota(jnp.int32, (2 * LANES, LANES), 0)
        target = lax.broadcasted_iota(jnp.int32, (2 * LANES, LANES), 1) + across
        here = (source == target).astype(F32)
        after = (source == target + 1).astype(F32)
        blend = jnp.concatenate([(1.0 - frac_x) * here + frac_x * after, after - here], axis=1).astype(BF16)
        source = lax.broadcasted_iota(jnp.int32, (lift_rows, lift_from), 1)
        target = lax.broadcasted_iota(jnp.int32, (lift_rows, lift_from), 0) + down
        lifts = [(source == target + shift).astype(F32).astype(BF16) for shift in (0, 8)]
        for part in range(2):
            start = pl.multiple_of(col0 + part * extent, LANES)
            for piece in range(2):
                taken = pl.ds(pl.multiple_of(row0 + piece * half, 16), lift_from)
                window = dot(lifts[piece], cells[taken, pl.ds(start, size + LANES)]).astype(BF16)
                for h in range(size // LANES):
                    mixed[part, pl.ds(piece * lift_rows, lift_rows), h * size : (h + 1) * size] = dot(
                        window[:, h * LANES : (h + 2) * LANES], blend
                    )
        for part in range(2):
            for h in range(size // LANES):
                cols = slice(h * size, h * size + LANES)
                for b in range(0, size, block):
                    upper = mixed[part, pl.ds(b, block), cols]
                    lower = mixed[part, pl.ds(b + 1, block), cols]
                    to = slice(part * size + h * LANES, part * size + (h + 1) * LANES)
                    patch[pl.ds(b, block), to] = (1.0 - frac_y) * upper + frac_y * lower
        pl.when(slot == first_slot)(wait_later)

        for mode in range(modes):
            for b in range(blocks):
                at = slice(b * block, (b + 1) * block)
                spot = (2 * b if b < blocks // 2 else 2 * b + 1 - blocks) * block
                to = slice(spot, spot + block)
                preal, pimag = probe[mode, at, :size], probe[mode, at, size:]
                oreal, oimag = patch[at, :size], patch[at, size:]
                wreal = preal * oreal - pimag * oimag
                wimag = preal * oimag + pimag * oreal
                for part, wave in enumerate((wreal, wimag)):
                    folded[mode, to, part * half : (part + 1) * half] = (wave[:, :half] + wave[:, half:]).astype(BF16)
                    folded[mode, to, size + part * half : size + (part + 1) * half] = (
                        wave[:, :half] - wave[:, half:]
                    ).astype(BF16)
        for mode in range(modes):
            for k, table in enumerate((even, odd)):
                out = dot(folded[mode, :, k * size : (k + 1) * size], table[...])
                for b in range(blocks // 2):
                    upper = out[2 * b * block : (2 * b + 1) * block]
                    lower = out[(2 * b + 1) * block : (2 * b + 2) * block]
                    plus, minus = (upper + lower).astype(BF16), (upper - lower).astype(BF16)
                    for part in range(2):
                        to = slice(part * half + b * block, part * half + (b + 1) * block)
                        cols = slice(part * half, (part + 1) * half)
                        half_u[mode, to, k * half : (k + 1) * half] = plus[:, cols]
                        half_v[mode, to, k * half : (k + 1) * half] = minus[:, cols]
        for mode in range(modes):
            far[mode, 0] = dot(even_t[...], half_u[mode])
            far[mode, 1] = dot(odd_t[...], half_v[mode])

        amplitude = dot(dot(order_t[...], measured[slot]).astype(BF16), order[...])
        for k in range(2):
            for b in range(0, half, block):
                pieces = [
                    [far[mode, k, part * half + b : part * half + b + block, :] for part in range(2)]
                    for mode in range(modes)
                ]
                power = sum(p * p for pair in pieces for p in pair)
                level = amplitude[k * half + b : k * half + b + block]
                ratio = 1.0 - level / jnp.maximum(jnp.sqrt(power), 0.5)
                for mode in range(modes):
                    for part in range(2):
                        to = slice(part * half + b, part * half + b + block)
                        error[mode, k, to, :] = (pieces[mode][part] * ratio).astype(BF16)

        for mode in range(modes):
            first = dot(even[...], error[mode, 0])
            second = dot(odd[...], error[mode, 1])
            plus, minus = (first + second).astype(BF16), (first - second).astype(BF16)
            for part in range(2):
                for b in range(blocks):
                    pick = part * half + (b % (blocks // 2)) * block
                    piece = (plus if b < blocks // 2 else minus)[pick : pick + block]
                    to = slice((b * modes + mode) * block, (b * modes + mode + 1) * block)
                    for c in range(2):
                        cols = slice(c * size + part * half, c * size + (part + 1) * half)
                        back[to, cols] = piece[:, c * half : (c + 1) * half]

        total_y = jnp.zeros((block, half), F32)
        total_x = jnp.zeros((block, half), F32)
        group = size // (modes * block)
        for g in range(blocks // group):
            span = slice(g * size, (g + 1) * size)
            first = dot(back[span, :size], even_t[...])
            second = dot(back[span, size:], odd_t[...])
            for r in range(group):
                at = slice((g * group + r) * block, (g * group + r + 1) * block)
                below = slice(at.start + 1, at.stop + 1)
                for h in range(2):
                    re = slice(h * half, (h + 1) * half)
                    im = slice(size + h * half, size + (h + 1) * half)
                    oreal, oimag = patch[at, re], patch[at, im]
                    greal = jnp.zeros((block, half), F32)
                    gimag = jnp.zeros((block, half), F32)
                    for mode in range(modes):
                        part = slice((r * modes + mode) * block, (r * modes + mode + 1) * block)
                        piece = first[part] + second[part] if h == 0 else first[part] - second[part]
                        ureal, uimag = piece[:, :half], piece[:, half:]
                        preal, pimag = probe[mode, at, re], probe[mode, at, im]
                        greal += preal * ureal + pimag * uimag
                        gimag += preal * uimag - pimag * ureal
                        probe_acc[mode, at, re] += oreal * ureal + oimag * uimag
                        probe_acc[mode, at, im] += oreal * uimag - oimag * ureal
                    held[slot, at, re] = greal.astype(BF16)
                    held[slot, at, im] = gimag.astype(BF16)
                    for part, grad in enumerate((greal, gimag)):
                        cols = slice(h * size, h * size + LANES)
                        total_y += grad * (mixed[part, below, cols] - mixed[part, at, cols])
                        cols = slice(h * size + LANES, (h + 1) * size)
                        total_x += grad * ((1.0 - frac_y) * mixed[part, at, cols] + frac_y * mixed[part, below, cols])
        moved[0, slot] = jnp.sum(total_y) / size
        moved[1, slot] = jnp.sum(total_x) / size

        sent_out(slot).start()

    @pl.loop(0, slots)
    def _(slot):
        pl.when(mine(slot))(functools.partial(one_slot, slot))

    pl.when(first_slot == slots)(wait_later)
    outs = []

    def store(source, target):
        outs.append(pltpu.make_async_copy(source, target, sems.at[len(outs)]))
        outs[-1].start()

    if last_stage:
        if first_stage:
            given[...] = probe_acc[...].astype(BF16)
        else:
            copies[-1].wait()
            for mode in range(modes):
                given[mode] = (probe_acc[mode] + sums[mode]).astype(BF16)
        store(given, sums_out)
    else:
        store(probe_acc, sums_out)

    @pl.loop(0, slots)
    def _(slot):
        @pl.when(mine(slot))
        def _():
            sent_out(slot).wait()

    for out in outs:
        out.wait()


def project(stage, bounds, places, own, rims, probe, measured, tables, width, carried):
    slots, size, _ = measured.shape
    modes = probe.shape[0]
    rows = own.shape[0]
    smem = pl.BlockSpec(memory_space=pltpu.SMEM)
    hbm = pl.BlockSpec(memory_space=pl.ANY)
    first_stage, last_stage = stage == 0, stage == len(bounds) - 2
    low, high = bounds[stage], bounds[stage + 1]
    extent = high - (0 if first_stage else low - size)
    inputs = [places, own, rims[stage]] + ([] if first_stage else [rims[stage - 1]]) + [probe, measured, tables]
    specs = [smem] + [hbm] * (len(inputs) - 1)
    outs = [
        jax.ShapeDtypeStruct((2, slots), F32),
        jax.ShapeDtypeStruct((slots, size, 2 * size), BF16),
        jax.ShapeDtypeStruct(probe.shape, BF16 if last_stage else F32),
    ]
    if not first_stage:
        inputs += list(carried)
        specs += [smem, hbm]
    scratch = [
        pltpu.VMEM((rows + size + 32, 2 * extent), BF16),
        pltpu.VMEM((2, size + 16, 2 * size), F32),
        pltpu.VMEM((size, 2 * size), F32),
        pltpu.VMEM((modes, size, 2 * size), BF16),
        pltpu.VMEM((modes, size, size), BF16),
        pltpu.VMEM((modes, size, size), BF16),
        pltpu.VMEM((modes, 2, size, size), F32),
        pltpu.VMEM((modes, 2, size, size), BF16),
        pltpu.VMEM((modes * size, 2 * size), BF16),
        pltpu.VMEM(probe.shape, F32),
        pltpu.VMEM(measured.shape, BF16),
        pltpu.VMEM(tables.shape, BF16),
        pltpu.VMEM(probe.shape, F32),
        pltpu.VMEM((slots, size, 2 * size), BF16),
        pltpu.SemaphoreType.DMA((12,)),
        pltpu.SemaphoreType.DMA((slots,)),
    ]
    if last_stage and not first_stage:
        scratch.append(pltpu.VMEM(probe.shape, F32))
    if last_stage:
        scratch.append(pltpu.VMEM(probe.shape, BF16))
    return pl.pallas_call(
        functools.partial(project_kernel, size, width, bounds, stage),
        in_specs=specs,
        out_specs=[smem] + [hbm] * (len(outs) - 1),
        out_shape=outs,
        scratch_shapes=scratch,
        compiler_params=pltpu.CompilerParams(vmem_limit_bytes=VMEM_BYTES),
        cost_estimate=pl.CostEstimate(flops=8 * 10**9, bytes_accessed=16 * 2**20, transcendentals=0),
        name=f"project_{stage}",
    )(*inputs)


def settle_kernel(size, bounds, low, high, shift, places, *refs):
    grads = refs[: len(refs) - 5]
    out, total, held, sems, out_sems = refs[len(refs) - 5 :]
    slots = held.shape[0]
    reach = size + LANES
    base = max(low - size, 0)
    extent = total.shape[1] // 2
    length = high - low

    def taken(stage, slot):
        left = places[1, slot]
        within = jnp.logical_and(left < high, left + size + 1 > low)
        return jnp.logical_and(within, in_stage(places, slot, bounds, stage, size))

    def fetch(stage, slot):
        return pltpu.make_async_copy(grads[stage].at[slot], held.at[slot], sems.at[slot])

    for stage in range(len(grads)):

        @pl.loop(0, slots)
        def _(slot, stage=stage):
            @pl.when(taken(stage, slot))
            def _():
                fetch(stage, slot).start()

    total[...] = jnp.zeros_like(total)

    def one_slot(stage, slot):
        left = places[1, slot]
        frac_y, frac_x = fractions(places[2, slot])
        col0 = (left // LANES) * LANES
        ahead = lax.broadcasted_iota(jnp.int32, (size, reach), 1) - lax.broadcasted_iota(jnp.int32, (size, reach), 0)
        ahead = ahead - (left - col0)
        along = jnp.where(ahead == 0, 1.0 - frac_x, jnp.where(ahead == 1, frac_x, 0.0)).astype(BF16)
        ahead = lax.broadcasted_iota(jnp.int32, (size, size), 0) - lax.broadcasted_iota(jnp.int32, (size, size), 1)
        ahead = ahead - (places[0, slot] - shift)
        down = jnp.where(ahead == 0, 1.0 - frac_y, jnp.where(ahead == 1, frac_y, 0.0)).astype(BF16)
        fetch(stage, slot).wait()
        for part in range(2):
            wide = dot(held[slot, :, part * size : (part + 1) * size], along).astype(BF16)
            start = pl.multiple_of(col0 - base + part * extent, LANES)
            total[:, pl.ds(start, reach)] += dot(down, wide)

    for stage in range(len(grads)):

        @pl.loop(0, slots)
        def _(slot, stage=stage):
            pl.when(taken(stage, slot))(functools.partial(one_slot, stage, slot))

    copies = []
    for part in range(2):
        here = slice(part * extent + low - base, part * extent + low - base + length)
        there = slice(part * length, (part + 1) * length)
        if out.dtype == F32:
            copies.append(
                pltpu.make_async_copy(
                    total.at[:, pl.ds(here.start, length)], out.at[:, pl.ds(there.start, length)], out_sems.at[part]
                )
            )
            copies[-1].start()
        else:
            out[:, there] = total[:, here].astype(out.dtype)
    for copy in copies:
        copy.wait()


def settle(places, grads, bounds, low, high, shift, dtype, width, name):
    slots, size, _ = grads[0].shape
    base, end = max(low - size, 0), min(high + size, width)
    hbm = pl.BlockSpec(memory_space=pl.ANY)
    return pl.pallas_call(
        functools.partial(settle_kernel, size, bounds, low, high, shift),
        in_specs=[pl.BlockSpec(memory_space=pltpu.SMEM)] + [hbm] * len(grads),
        out_specs=hbm if dtype == F32 else pl.BlockSpec(memory_space=pltpu.VMEM),
        out_shape=jax.ShapeDtypeStruct((size, 2 * (high - low)), dtype),
        scratch_shapes=[
            pltpu.VMEM((size, 2 * (end - base)), F32),
            pltpu.VMEM(grads[0].shape, BF16),
            pltpu.SemaphoreType.DMA((slots,)),
            pltpu.SemaphoreType.DMA((2,)),
        ],
        compiler_params=pltpu.CompilerParams(vmem_limit_bytes=VMEM_SMALL),
        cost_estimate=pl.CostEstimate(flops=10**9, bytes_accessed=8 * 2**20, transcendentals=0),
        name=name,
    )(places, *grads)


def finish_kernel(edges, n, own, *refs):
    aboves, out = refs[:n], refs[n]
    wides, adds, sems = refs[n + 1 : 2 * n + 1], refs[2 * n + 1 : 3 * n + 1], refs[3 * n + 1]
    width = out.shape[2]
    loads, outs = [], []

    def copied(source, target, to):
        to.append(pltpu.make_async_copy(source, target, sems.at[len(loads) + len(outs)]))
        to[-1].start()

    for i in range(n):
        length = edges[i + 1] - edges[i]
        for part in range(2):
            copied(
                own.at[:, pl.ds(part * width + edges[i], length)], wides[i].at[:, pl.ds(part * length, length)], loads
            )
        copied(aboves[i], adds[i], loads)
    for i in range(n):
        for copy in loads[3 * i : 3 * i + 3]:
            copy.wait()
        length = edges[i + 1] - edges[i]
        for part in range(2):
            cols = slice(part * length, (part + 1) * length)
            wides[i][:, cols] += adds[i][:, cols].astype(F32)
            copied(wides[i].at[:, pl.ds(part * length, length)], out.at[:, part, pl.ds(edges[i], length)], outs)
    for copy in outs:
        copy.wait()


def finish(own, aboves, edges, width):
    n = len(aboves)
    hbm = pl.BlockSpec(memory_space=pl.ANY)
    return pl.pallas_call(
        functools.partial(finish_kernel, edges, n),
        in_specs=[hbm] * (n + 1),
        out_specs=hbm,
        out_shape=jax.ShapeDtypeStruct((own.shape[0], 2, width), F32),
        scratch_shapes=[pltpu.VMEM(x.shape, F32) for x in aboves]
        + [pltpu.VMEM(x.shape, BF16) for x in aboves]
        + [pltpu.SemaphoreType.DMA((5 * n,))],
        compiler_params=pltpu.CompilerParams(vmem_limit_bytes=VMEM_SMALL),
        cost_estimate=pl.CostEstimate(flops=10**6, bytes_accessed=10 * 2**20, transcendentals=0),
        name="finish",
    )(own, *aboves)


def passed_along(x, axis, by):
    length = lax.axis_size(axis)
    pairs = [(i, i + by) for i in range(length) if 0 <= i + by < length]
    return lax.ppermute(x, axis, pairs)


def unpack_kernel(order, *refs):
    n = (len(refs) - 4) // 2
    out, wide, narrow, sems = refs[2 * n :]
    rows = wide.shape[1]
    size = out.shape[1]
    span = min(rows, size)
    for core in range(2):

        @pl.when(order[n] == core)
        def _():
            for i in range(n):
                pltpu.make_async_copy(refs[core * n + i], narrow.at[i], sems.at[0, i]).start()

    copies = []
    for i in range(n):
        pltpu.make_async_copy(refs[i], narrow.at[i], sems.at[0, i]).wait()
        wide[i] = narrow[i].astype(F32)
        for j in range(rows // span):
            line = order[i] * rows + j * span
            mode = line // size
            at = pl.multiple_of(line % size, 8)
            for part in range(2):
                copies.append(
                    pltpu.make_async_copy(
                        wide.at[i, pl.ds(j * span, span), pl.ds(part * size, size)],
                        out.at[mode, pl.ds(at, span), part, :],
                        sems.at[1, len(copies)],
                    )
                )
                copies[-1].start()
    for copy in copies:
        copy.wait()


def unpacked(pieces, others, order, shape):
    n = len(pieces)
    rows, columns = pieces[0].shape
    hbm = pl.BlockSpec(memory_space=pl.ANY)
    return pl.pallas_call(
        unpack_kernel,
        in_specs=[pl.BlockSpec(memory_space=pltpu.SMEM)] + [hbm] * (2 * n),
        out_specs=hbm,
        out_shape=jax.ShapeDtypeStruct(shape, F32),
        scratch_shapes=[
            pltpu.VMEM((n, rows, columns), F32),
            pltpu.VMEM((n, rows, columns), BF16),
            pltpu.SemaphoreType.DMA((2, 2 * n * max(1, rows // shape[1]))),
        ],
        compiler_params=pltpu.CompilerParams(vmem_limit_bytes=VMEM_SMALL),
        cost_estimate=pl.CostEstimate(flops=10**6, bytes_accessed=4 * 2**20, transcendentals=0),
        name="unpack",
    )(order, *pieces, *others)


def near_chips(axis):
    return min(4, lax.axis_size(axis) // 2)


def piece_order(axis):
    near = near_chips(axis)
    me = lax.axis_index(axis)
    core, spot = me % 2, me // 2 % near
    return jnp.stack([spot ^ s for s in range(near)] + [core])


def hop(axis, shift, stride):
    return [(i, i ^ (2 * stride * shift)) for i in range(0, lax.axis_size(axis), 2)]


def paired_kernel(order, given, sibling, *refs):
    n = len(refs) - 3
    outs, mine, other, sems = refs[:n], refs[-3], refs[-2], refs[-1]
    rows = mine.shape[1]
    copies = []
    for i in range(n):
        at = pl.ds(pl.multiple_of(order[i] * rows, 16), rows)
        copies.append(
            [
                pltpu.make_async_copy(given.at[at], mine.at[i], sems.at[0, i]),
                pltpu.make_async_copy(sibling.at[at], other.at[i], sems.at[1, i]),
            ]
        )
        for copy in copies[-1]:
            copy.start()
    for i in range(n):
        for copy in copies[i]:
            copy.wait()
        outs[i][...] = (mine[i].astype(F32) + other[i].astype(F32)).astype(BF16)


def paired(given, sibling, order, n):
    rows, columns = given.shape[0] // n, given.shape[1]
    hbm = pl.BlockSpec(memory_space=pl.ANY)
    return pl.pallas_call(
        paired_kernel,
        in_specs=[pl.BlockSpec(memory_space=pltpu.SMEM), hbm, hbm],
        out_specs=[pl.BlockSpec(memory_space=pltpu.VMEM)] * n,
        out_shape=[jax.ShapeDtypeStruct((rows, columns), BF16)] * n,
        scratch_shapes=[
            pltpu.VMEM((n, rows, columns), BF16),
            pltpu.VMEM((n, rows, columns), BF16),
            pltpu.SemaphoreType.DMA((2, n)),
        ],
        compiler_params=pltpu.CompilerParams(vmem_limit_bytes=VMEM_SMALL),
        cost_estimate=pl.CostEstimate(flops=10**6, bytes_accessed=3 * 2**20, transcendentals=0),
        name="paired",
    )(order, given, sibling)


def summed(given, axis, shape, order, beside, during, between, last):
    length = lax.axis_size(axis)
    near = near_chips(axis)
    far = length // 2 // near
    inward = [(i + 1, i) for i in range(0, length, 2)]
    outward = [(i, i + 1) for i in range(0, length, 2)]
    modes, size, columns = given.shape
    sibling = beside(lax.ppermute(given, axis, inward))
    flat = (modes * size, columns)
    parts = paired(given.reshape(flat), sibling.reshape(flat), order, near)
    got = [lax.ppermute(parts[s], axis, hop(axis, s, 1)) for s in range(1, near)]
    got = during(got)
    total = parts[0].astype(F32)
    for piece in got:
        total = total + piece.astype(F32)
    sent = total.astype(BF16)
    others = [lax.ppermute(sent, axis, hop(axis, s, near)) for s in range(1, far)]
    if others:
        others[0] = between(others[0])
    for piece in others:
        total = total + piece.astype(F32)
    total = total.astype(BF16)
    pieces = [total] + [lax.ppermute(total, axis, hop(axis, s, 1)) for s in range(1, near)]
    others = [lax.ppermute(piece, axis, outward) for piece in pieces]
    return unpacked(pieces, others, last(order), shape)


def column_bounds(width, shares):
    return tuple([0] + [round(width * share / LANES) * LANES for share in shares] + [width])


def shards(object_tiles, probe, measured, offset_row, offset_col, subpixel, live_count):
    rows, _, width = object_tiles.shape
    modes, size = probe.shape[:2]
    tables = dft_tables(size)
    bounds = column_bounds(width, (0.4375, 0.75))
    stages = len(bounds) - 1
    rims = [
        passed_along(object_tiles[:size, :, low:high].reshape(size, 2 * (high - low)), "row", -1)
        for low, high in zip(bounds[:-1], bounds[1:])
    ]
    core = lax.axis_index("row") % 2
    places = jnp.stack(
        [offset_row, offset_col, subpixel] + [jnp.broadcast_to(x, offset_row.shape) for x in (live_count, core)]
    )
    places, order = lax.optimization_barrier((places, piece_order("row")))
    own = object_tiles.reshape(rows, 2 * width)
    flat = probe.reshape(modes, size, 2 * size)
    carried = None
    grads = []
    edges = (0, min(width // 2 // LANES * LANES, bounds[-2] - size), width)
    for stage in range(stages):
        if stage == stages - 1:
            early = settle(places, grads, bounds, edges[0], edges[1], size, BF16, width, "below_early")
            places, early = lax.optimization_barrier((places, early))
            aboves = [passed_along(early, "row", 1)]
        moved, grad, *rest = project(stage, bounds, places, own, rims, flat, measured, tables, width, carried)
        grads.append(grad)
        carried = [moved] + rest
    given, aboves = lax.optimization_barrier((carried[1], aboves))
    aboves = list(aboves)
    late = settle(places, grads, bounds, edges[1], edges[2], size, BF16, width, "below_late")
    held = {}

    def beside(x):
        return x

    def during(x):
        x, held["late"] = lax.optimization_barrier((x, late))
        return x

    def between(x):
        aboves.append(passed_along(held["late"], "row", 1))
        own_rows = settle(places, grads, bounds, 0, width, 0, F32, width, "own_rows")
        x, aboves[1], held["own"] = lax.optimization_barrier((x, aboves[1], own_rows))
        return x

    def last(x):
        object_grad = finish(held["own"], aboves, edges, width)
        x, held["object_grad"] = lax.optimization_barrier((x, object_grad))
        return x

    probe_grad = summed(given, "row", probe.shape, order, beside, during, between, last)
    object_grad = held["object_grad"]
    return object_grad, probe_grad, moved


def solution(mesh):
    in_specs = (
        P(("groups", "row"), None, None),
        P(),
        P(("groups", "row"), None, None),
        P(("groups", "row")),
        P(("groups", "row")),
        P(("groups", "row")),
        P(("groups", "row")),
    )
    out_specs = (
        P(("groups", "row"), None, None),
        P("groups", None, None, None),
        P(None, ("groups", "row")),
    )
    return jax.shard_map(shards, mesh=mesh, in_specs=in_specs, out_specs=out_specs, check_vma=False)
```

```python
import functools
import math

import jax
import jax.numpy as jnp
import ml_dtypes
import numpy as np
from jax import lax
from jax.experimental import pallas as pl
from jax.experimental.pallas import tpu as pltpu
from jax.sharding import PartitionSpec as P

F32 = jnp.float32
BF16 = jnp.bfloat16
LANES = 128
VMEM_BYTES = 26 * 2**20
VMEM_SMALL = 16 * 2**20


def dft_tables(size):
    half = size // 2
    index = np.arange(size)
    angle = (index[:, None] * index[None, :] % size) * (2.0 * math.pi / size)
    scale = 1.0 / math.sqrt(size)
    cosine = (np.cos(angle) * scale).astype(ml_dtypes.bfloat16)
    sine = (np.sin(angle) * scale).astype(ml_dtypes.bfloat16)
    tables = []
    for parity in (0, 1):
        c, s = cosine[:half, parity::2], sine[:half, parity::2]
        tables.append(np.block([[c, -s], [s, c]]))
    order = np.zeros((size, size), ml_dtypes.bfloat16)
    order[2 * index[:half], index[:half]] = 1
    order[2 * index[:half] + 1, half + index[:half]] = 1
    even, odd = tables
    return jnp.asarray(np.stack([even, odd, even.T, odd.T, order, order.T]))


def dot(left, right):
    return jnp.dot(left, right, preferred_element_type=F32)


def fractions(code):
    return (code // 4).astype(F32) * 0.25, (code % 4).astype(F32) * 0.25


def in_stage(places, slot, bounds, stage, size):
    end = places[1, slot] + size + 1
    here = end <= bounds[stage + 1]
    if stage > 0:
        here = jnp.logical_and(here, end > bounds[stage])
    return jnp.logical_and(slot < places[3, 0], here)


def project_kernel(size, width, bounds, stage, places, *refs):
    first_stage, last_stage = stage == 0, stage == len(bounds) - 2
    refs = list(refs)
    own, rim = refs[:2]
    rim_before = None if first_stage else refs[2]
    refs = refs[2:] if first_stage else refs[3:]
    probe_in, measured_in, tables_in = refs[:3]
    refs = refs[3:]
    if not first_stage:
        moved_in, sums_in = refs[:2]
        refs = refs[2:]
    moved, grads = refs[:2]
    refs = refs[2:]
    sums_out = refs.pop(0)
    cells, mixed, patch, folded, half_u, half_v, far, error, back, probe, measured, tables, probe_acc, held = refs[:14]
    sems, slot_sems = refs[14:16]
    if last_stage and not first_stage:
        sums, given = refs[16:]
    elif last_stage:
        given = refs[16]
    even, odd, even_t, odd_t, order, order_t = [tables.at[i] for i in range(6)]
    half = size // 2
    modes = probe.shape[0]
    slots = measured.shape[0]
    rows = own.shape[0]
    low, high = bounds[stage], bounds[stage + 1]
    base = 0 if first_stage else low - size
    extent = high - base
    count = places[3, 0]
    copies = []

    def load(source, target):
        copies.append(pltpu.make_async_copy(source, target, sems.at[len(copies)]))

    for part in range(2):
        load(
            own.at[:, pl.ds(part * width + base, extent)],
            cells.at[pl.ds(0, rows), pl.ds(part * extent, extent)],
        )
        load(
            rim.at[:, pl.ds(part * (high - low), high - low)],
            cells.at[pl.ds(rows, size), pl.ds(part * extent + low - base, high - low)],
        )
        if not first_stage:
            before = low - bounds[stage - 1]
            load(
                rim_before.at[:, pl.ds((part + 1) * before - size, size)],
                cells.at[pl.ds(rows, size), pl.ds(part * extent, size)],
            )
    n_cells = len(copies)
    load(tables_in, tables)
    load(probe_in, probe)
    load(measured_in, measured)
    n_later = len(copies)
    if not first_stage:
        load(sums_in, sums if last_stage else probe_acc)
    for copy in copies:
        copy.start()
    if last_stage or first_stage:
        probe_acc[...] = jnp.zeros_like(probe_acc)
    cells[rows + size :] = jnp.zeros((cells.shape[0] - rows - size, cells.shape[1]), BF16)
    for slot in range(slots):
        for axis in range(2):
            moved[axis, slot] = 0.0 if first_stage else moved_in[axis, slot]
    for copy in copies[:n_cells]:
        copy.wait()

    def wait_later():
        for copy in copies[n_cells : n_later if last_stage else len(copies)]:
            copy.wait()

    def mine(slot):
        return in_stage(places, slot, bounds, stage, size)

    def sent_out(slot):
        return pltpu.make_async_copy(held.at[slot], grads.at[slot], slot_sems.at[slot])

    first_slot = jnp.int32(slots)
    for slot in reversed(range(slots)):
        first_slot = jnp.where(mine(slot), slot, first_slot)

    block = 16
    blocks = size // block
    lift_rows = half + 8
    lift_from = half + 32

    def one_slot(slot):
        top = places[0, slot]
        left = places[1, slot]
        frac_y, frac_x = fractions(places[2, slot])
        row0 = pl.multiple_of((top // 16) * 16, 16)
        col0 = pl.multiple_of((left // LANES) * LANES - base, LANES)
        down = top - row0
        across = left - base - col0
        source = lax.broadcasted_iota(jnp.int32, (2 * LANES, LANES), 0)
        target = lax.broadcasted_iota(jnp.int32, (2 * LANES, LANES), 1) + across
        here = (source == target).astype(F32)
        after = (source == target + 1).astype(F32)
        blend = jnp.concatenate([(1.0 - frac_x) * here + frac_x * after, after - here], axis=1).astype(BF16)
        source = lax.broadcasted_iota(jnp.int32, (lift_rows, lift_from), 1)
        target = lax.broadcasted_iota(jnp.int32, (lift_rows, lift_from), 0) + down
        lifts = [(source == target + shift).astype(F32).astype(BF16) for shift in (0, 8)]
        for part in range(2):
            start = pl.multiple_of(col0 + part * extent, LANES)
            for piece in range(2):
                taken = pl.ds(pl.multiple_of(row0 + piece * half, 16), lift_from)
                window = dot(lifts[piece], cells[taken, pl.ds(start, size + LANES)]).astype(BF16)
                for h in range(size // LANES):
                    mixed[part, pl.ds(piece * lift_rows, lift_rows), h * size : (h + 1) * size] = dot(
                        window[:, h * LANES : (h + 2) * LANES], blend
                    )
        for part in range(2):
            for h in range(size // LANES):
                cols = slice(h * size, h * size + LANES)
                for b in range(0, size, block):
                    upper = mixed[part, pl.ds(b, block), cols]
                    lower = mixed[part, pl.ds(b + 1, block), cols]
                    to = slice(part * size + h * LANES, part * size + (h + 1) * LANES)
                    patch[pl.ds(b, block), to] = (1.0 - frac_y) * upper + frac_y * lower
        pl.when(slot == first_slot)(wait_later)

        for mode in range(modes):
            for b in range(blocks):
                at = slice(b * block, (b + 1) * block)
                spot = (2 * b if b < blocks // 2 else 2 * b + 1 - blocks) * block
                to = slice(spot, spot + block)
                preal, pimag = probe[mode, at, :size], probe[mode, at, size:]
                oreal, oimag = patch[at, :size], patch[at, size:]
                wreal = preal * oreal - pimag * oimag
                wimag = preal * oimag + pimag * oreal
                for part, wave in enumerate((wreal, wimag)):
                    folded[mode, to, part * half : (part + 1) * half] = (wave[:, :half] + wave[:, half:]).astype(BF16)
                    folded[mode, to, size + part * half : size + (part + 1) * half] = (
                        wave[:, :half] - wave[:, half:]
                    ).astype(BF16)
        for mode in range(modes):
            for k, table in enumerate((even, odd)):
                out = dot(folded[mode, :, k * size : (k + 1) * size], table[...])
                for b in range(blocks // 2):
                    upper = out[2 * b * block : (2 * b + 1) * block]
                    lower = out[(2 * b + 1) * block : (2 * b + 2) * block]
                    plus, minus = (upper + lower).astype(BF16), (upper - lower).astype(BF16)
                    for part in range(2):
                        to = slice(part * half + b * block, part * half + (b + 1) * block)
                        cols = slice(part * half, (part + 1) * half)
                        half_u[mode, to, k * half : (k + 1) * half] = plus[:, cols]
                        half_v[mode, to, k * half : (k + 1) * half] = minus[:, cols]
        for mode in range(modes):
            far[mode, 0] = dot(even_t[...], half_u[mode])
            far[mode, 1] = dot(odd_t[...], half_v[mode])

        amplitude = dot(dot(order_t[...], measured[slot]).astype(BF16), order[...])
        for k in range(2):
            for b in range(0, half, block):
                pieces = [
                    [far[mode, k, part * half + b : part * half + b + block, :] for part in range(2)]
                    for mode in range(modes)
                ]
                power = sum(p * p for pair in pieces for p in pair)
                level = amplitude[k * half + b : k * half + b + block]
                ratio = 1.0 - level / jnp.maximum(jnp.sqrt(power), 0.5)
                for mode in range(modes):
                    for part in range(2):
                        to = slice(part * half + b, part * half + b + block)
                        error[mode, k, to, :] = (pieces[mode][part] * ratio).astype(BF16)

        for mode in range(modes):
            first = dot(even[...], error[mode, 0])
            second = dot(odd[...], error[mode, 1])
            plus, minus = (first + second).astype(BF16), (first - second).astype(BF16)
            for part in range(2):
                for b in range(blocks):
                    pick = part * half + (b % (blocks // 2)) * block
                    piece = (plus if b < blocks // 2 else minus)[pick : pick + block]
                    to = slice((b * modes + mode) * block, (b * modes + mode + 1) * block)
                    for c in range(2):
                        cols = slice(c * size + part * half, c * size + (part + 1) * half)
                        back[to, cols] = piece[:, c * half : (c + 1) * half]

        total_y = jnp.zeros((block, half), F32)
        total_x = jnp.zeros((block, half), F32)
        group = size // (modes * block)
        for g in range(blocks // group):
            span = slice(g * size, (g + 1) * size)
            first = dot(back[span, :size], even_t[...])
            second = dot(back[span, size:], odd_t[...])
            for r in range(group):
                at = slice((g * group + r) * block, (g * group + r + 1) * block)
                below = slice(at.start + 1, at.stop + 1)
                for h in range(2):
                    re = slice(h * half, (h + 1) * half)
                    im = slice(size + h * half, size + (h + 1) * half)
                    oreal, oimag = patch[at, re], patch[at, im]
                    greal = jnp.zeros((block, half), F32)
                    gimag = jnp.zeros((block, half), F32)
                    for mode in range(modes):
                        part = slice((r * modes + mode) * block, (r * modes + mode + 1) * block)
                        piece = first[part] + second[part] if h == 0 else first[part] - second[part]
                        ureal, uimag = piece[:, :half], piece[:, half:]
                        preal, pimag = probe[mode, at, re], probe[mode, at, im]
                        greal += preal * ureal + pimag * uimag
                        gimag += preal * uimag - pimag * ureal
                        probe_acc[mode, at, re] += oreal * ureal + oimag * uimag
                        probe_acc[mode, at, im] += oreal * uimag - oimag * ureal
                    held[slot, at, re] = greal.astype(BF16)
                    held[slot, at, im] = gimag.astype(BF16)
                    for part, grad in enumerate((greal, gimag)):
                        cols = slice(h * size, h * size + LANES)
                        total_y += grad * (mixed[part, below, cols] - mixed[part, at, cols])
                        cols = slice(h * size + LANES, (h + 1) * size)
                        total_x += grad * ((1.0 - frac_y) * mixed[part, at, cols] + frac_y * mixed[part, below, cols])
        moved[0, slot] = jnp.sum(total_y) / size
        moved[1, slot] = jnp.sum(total_x) / size

        sent_out(slot).start()

    @pl.loop(0, slots)
    def _(slot):
        pl.when(mine(slot))(functools.partial(one_slot, slot))

    pl.when(first_slot == slots)(wait_later)
    outs = []

    def store(source, target):
        outs.append(pltpu.make_async_copy(source, target, sems.at[len(outs)]))
        outs[-1].start()

    if last_stage:
        if first_stage:
            given[...] = probe_acc[...].astype(BF16)
        else:
            copies[-1].wait()
            for mode in range(modes):
                given[mode] = (probe_acc[mode] + sums[mode]).astype(BF16)
        store(given, sums_out)
    else:
        store(probe_acc, sums_out)

    @pl.loop(0, slots)
    def _(slot):
        @pl.when(mine(slot))
        def _():
            sent_out(slot).wait()

    for out in outs:
        out.wait()


def project(stage, bounds, places, own, rims, probe, measured, tables, width, carried):
    slots, size, _ = measured.shape
    modes = probe.shape[0]
    rows = own.shape[0]
    smem = pl.BlockSpec(memory_space=pltpu.SMEM)
    hbm = pl.BlockSpec(memory_space=pl.ANY)
    first_stage, last_stage = stage == 0, stage == len(bounds) - 2
    low, high = bounds[stage], bounds[stage + 1]
    extent = high - (0 if first_stage else low - size)
    inputs = [places, own, rims[stage]] + ([] if first_stage else [rims[stage - 1]]) + [probe, measured, tables]
    specs = [smem] + [hbm] * (len(inputs) - 1)
    outs = [
        jax.ShapeDtypeStruct((2, slots), F32),
        jax.ShapeDtypeStruct((slots, size, 2 * size), BF16),
        jax.ShapeDtypeStruct(probe.shape, BF16 if last_stage else F32),
    ]
    if not first_stage:
        inputs += list(carried)
        specs += [smem, hbm]
    scratch = [
        pltpu.VMEM((rows + size + 32, 2 * extent), BF16),
        pltpu.VMEM((2, size + 16, 2 * size), F32),
        pltpu.VMEM((size, 2 * size), F32),
        pltpu.VMEM((modes, size, 2 * size), BF16),
        pltpu.VMEM((modes, size, size), BF16),
        pltpu.VMEM((modes, size, size), BF16),
        pltpu.VMEM((modes, 2, size, size), F32),
        pltpu.VMEM((modes, 2, size, size), BF16),
        pltpu.VMEM((modes * size, 2 * size), BF16),
        pltpu.VMEM(probe.shape, F32),
        pltpu.VMEM(measured.shape, BF16),
        pltpu.VMEM(tables.shape, BF16),
        pltpu.VMEM(probe.shape, F32),
        pltpu.VMEM((slots, size, 2 * size), BF16),
        pltpu.SemaphoreType.DMA((12,)),
        pltpu.SemaphoreType.DMA((slots,)),
    ]
    if last_stage and not first_stage:
        scratch.append(pltpu.VMEM(probe.shape, F32))
    if last_stage:
        scratch.append(pltpu.VMEM(probe.shape, BF16))
    return pl.pallas_call(
        functools.partial(project_kernel, size, width, bounds, stage),
        in_specs=specs,
        out_specs=[smem] + [hbm] * (len(outs) - 1),
        out_shape=outs,
        scratch_shapes=scratch,
        compiler_params=pltpu.CompilerParams(vmem_limit_bytes=VMEM_BYTES),
        cost_estimate=pl.CostEstimate(flops=8 * 10**9, bytes_accessed=16 * 2**20, transcendentals=0),
        name=f"project_{stage}",
    )(*inputs)


def settle_kernel(size, bounds, low, high, shift, places, *refs):
    grads = refs[: len(refs) - 5]
    out, total, held, sems, out_sems = refs[len(refs) - 5 :]
    slots = held.shape[0]
    reach = size + LANES
    base = max(low - size, 0)
    extent = total.shape[1] // 2
    length = high - low

    def taken(stage, slot):
        left = places[1, slot]
        within = jnp.logical_and(left < high, left + size + 1 > low)
        return jnp.logical_and(within, in_stage(places, slot, bounds, stage, size))

    def fetch(stage, slot):
        return pltpu.make_async_copy(grads[stage].at[slot], held.at[slot], sems.at[slot])

    for stage in range(len(grads)):

        @pl.loop(0, slots)
        def _(slot, stage=stage):
            @pl.when(taken(stage, slot))
            def _():
                fetch(stage, slot).start()

    total[...] = jnp.zeros_like(total)

    def one_slot(stage, slot):
        left = places[1, slot]
        frac_y, frac_x = fractions(places[2, slot])
        col0 = (left // LANES) * LANES
        ahead = lax.broadcasted_iota(jnp.int32, (size, reach), 1) - lax.broadcasted_iota(jnp.int32, (size, reach), 0)
        ahead = ahead - (left - col0)
        along = jnp.where(ahead == 0, 1.0 - frac_x, jnp.where(ahead == 1, frac_x, 0.0)).astype(BF16)
        ahead = lax.broadcasted_iota(jnp.int32, (size, size), 0) - lax.broadcasted_iota(jnp.int32, (size, size), 1)
        ahead = ahead - (places[0, slot] - shift)
        down = jnp.where(ahead == 0, 1.0 - frac_y, jnp.where(ahead == 1, frac_y, 0.0)).astype(BF16)
        fetch(stage, slot).wait()
        for part in range(2):
            wide = dot(held[slot, :, part * size : (part + 1) * size], along).astype(BF16)
            start = pl.multiple_of(col0 - base + part * extent, LANES)
            total[:, pl.ds(start, reach)] += dot(down, wide)

    for stage in range(len(grads)):

        @pl.loop(0, slots)
        def _(slot, stage=stage):
            pl.when(taken(stage, slot))(functools.partial(one_slot, stage, slot))

    copies = []
    for part in range(2):
        here = slice(part * extent + low - base, part * extent + low - base + length)
        there = slice(part * length, (part + 1) * length)
        if out.dtype == F32:
            copies.append(
                pltpu.make_async_copy(
                    total.at[:, pl.ds(here.start, length)], out.at[:, pl.ds(there.start, length)], out_sems.at[part]
                )
            )
            copies[-1].start()
        else:
            out[:, there] = total[:, here].astype(out.dtype)
    for copy in copies:
        copy.wait()


def settle(places, grads, bounds, low, high, shift, dtype, width, name):
    slots, size, _ = grads[0].shape
    base, end = max(low - size, 0), min(high + size, width)
    hbm = pl.BlockSpec(memory_space=pl.ANY)
    return pl.pallas_call(
        functools.partial(settle_kernel, size, bounds, low, high, shift),
        in_specs=[pl.BlockSpec(memory_space=pltpu.SMEM)] + [hbm] * len(grads),
        out_specs=hbm if dtype == F32 else pl.BlockSpec(memory_space=pltpu.VMEM),
        out_shape=jax.ShapeDtypeStruct((size, 2 * (high - low)), dtype),
        scratch_shapes=[
            pltpu.VMEM((size, 2 * (end - base)), F32),
            pltpu.VMEM(grads[0].shape, BF16),
            pltpu.SemaphoreType.DMA((slots,)),
            pltpu.SemaphoreType.DMA((2,)),
        ],
        compiler_params=pltpu.CompilerParams(vmem_limit_bytes=VMEM_SMALL),
        cost_estimate=pl.CostEstimate(flops=10**9, bytes_accessed=8 * 2**20, transcendentals=0),
        name=name,
    )(places, *grads)


def finish_kernel(edges, n, own, *refs):
    aboves, out = refs[:n], refs[n]
    wides, adds, sems = refs[n + 1 : 2 * n + 1], refs[2 * n + 1 : 3 * n + 1], refs[3 * n + 1]
    width = out.shape[2]
    loads, outs = [], []

    def copied(source, target, to):
        to.append(pltpu.make_async_copy(source, target, sems.at[len(loads) + len(outs)]))
        to[-1].start()

    for i in range(n):
        length = edges[i + 1] - edges[i]
        for part in range(2):
            copied(
                own.at[:, pl.ds(part * width + edges[i], length)], wides[i].at[:, pl.ds(part * length, length)], loads
            )
        copied(aboves[i], adds[i], loads)
    for i in range(n):
        for copy in loads[3 * i : 3 * i + 3]:
            copy.wait()
        length = edges[i + 1] - edges[i]
        for part in range(2):
            cols = slice(part * length, (part + 1) * length)
            wides[i][:, cols] += adds[i][:, cols].astype(F32)
            copied(wides[i].at[:, pl.ds(part * length, length)], out.at[:, part, pl.ds(edges[i], length)], outs)
    for copy in outs:
        copy.wait()


def finish(own, aboves, edges, width):
    n = len(aboves)
    hbm = pl.BlockSpec(memory_space=pl.ANY)
    return pl.pallas_call(
        functools.partial(finish_kernel, edges, n),
        in_specs=[hbm] * (n + 1),
        out_specs=hbm,
        out_shape=jax.ShapeDtypeStruct((own.shape[0], 2, width), F32),
        scratch_shapes=[pltpu.VMEM(x.shape, F32) for x in aboves]
        + [pltpu.VMEM(x.shape, BF16) for x in aboves]
        + [pltpu.SemaphoreType.DMA((5 * n,))],
        compiler_params=pltpu.CompilerParams(vmem_limit_bytes=VMEM_SMALL),
        cost_estimate=pl.CostEstimate(flops=10**6, bytes_accessed=10 * 2**20, transcendentals=0),
        name="finish",
    )(own, *aboves)


def passed_along(x, axis, by):
    length = lax.axis_size(axis)
    pairs = [(i, i + by) for i in range(length) if 0 <= i + by < length]
    return lax.ppermute(x, axis, pairs)


def unpack_kernel(order, *refs):
    pieces, out, wide, sems = refs[:-3], refs[-3], refs[-2], refs[-1]
    rows = pieces[0].shape[0]
    modes, size, _, _ = out.shape
    copies = []
    for i, piece in enumerate(pieces):
        wide[i * rows : (i + 1) * rows] = piece[...].astype(F32)
        mode = order[i] // (size // rows)
        at = pl.multiple_of(order[i] % (size // rows) * rows, 8)
        for part in range(2):
            copy = pltpu.make_async_copy(
                wide.at[pl.ds(i * rows, rows), pl.ds(part * size, size)],
                out.at[mode, pl.ds(at, rows), part, :],
                sems.at[2 * i + part],
            )
            copy.start()
            copies.append(copy)
    for copy in copies:
        copy.wait()


def unpacked(pieces, order, shape):
    vmem = pl.BlockSpec(memory_space=pltpu.VMEM)
    smem = pl.BlockSpec(memory_space=pltpu.SMEM)
    return pl.pallas_call(
        unpack_kernel,
        in_specs=[smem] + [vmem] * len(pieces),
        out_specs=pl.BlockSpec(memory_space=pl.ANY),
        out_shape=jax.ShapeDtypeStruct(shape, F32),
        scratch_shapes=[
            pltpu.VMEM((len(pieces) * pieces[0].shape[0], pieces[0].shape[1]), F32),
            pltpu.SemaphoreType.DMA((2 * len(pieces),)),
        ],
        compiler_params=pltpu.CompilerParams(vmem_limit_bytes=VMEM_BYTES),
        name="unpack",
    )(order, *pieces)


def piece_order(axis):
    length = lax.axis_size(axis)
    near = min(4, length // 2)
    me = lax.axis_index(axis)
    core, spot = me % 2, me // 2 % near
    return jnp.stack(
        [core * near + (spot ^ s) for s in range(near)] + [(1 - core) * near + (spot ^ s) for s in range(near)]
    )


def summed(given, axis, shape, order, beside, during, between, last):
    length = lax.axis_size(axis)
    chips = length // 2
    near = min(4, chips)
    far = chips // near
    me = lax.axis_index(axis)
    core, chip = me % 2, me // 2
    across = [(i, i ^ 1) for i in range(length)]

    def hop(shift, stride):
        return [(i, i ^ (2 * stride * shift)) for i in range(length)]

    size, columns = given.shape[1:]
    given = given.reshape((2, given.shape[0] // 2) + given.shape[1:])
    keep = lax.dynamic_index_in_dim(given, core, 0, False)
    give = lax.dynamic_index_in_dim(given, 1 - core, 0, False)
    mine = (keep.astype(F32) + beside(lax.ppermute(give, axis, across)).astype(F32)).astype(BF16)
    rows = mine.shape[0] * size // near
    mine = mine.reshape(near, rows, columns)
    parts = mine.astype(BF16)
    spot = chip % near
    got = [
        lax.ppermute(lax.dynamic_index_in_dim(parts, spot ^ s, 0, False), axis, hop(s, 1)) for s in range(1, near)
    ]
    got = during(got)
    total = lax.dynamic_index_in_dim(mine, spot, 0, False).astype(F32)
    for piece in got:
        total = total + piece.astype(F32)
    sent = total.astype(BF16)
    others = [lax.ppermute(sent, axis, hop(s, near)) for s in range(1, far)]
    if others:
        others[0] = between(others[0])
    for piece in others:
        total = total + piece.astype(F32)
    total = total.astype(BF16)
    pieces = [total] + [lax.ppermute(total, axis, hop(s, 1)) for s in range(1, near)]
    others = [lax.ppermute(piece, axis, across) for piece in pieces]
    return unpacked(pieces + others, last(order), shape)


def column_bounds(width, shares):
    return tuple([0] + [round(width * share / LANES) * LANES for share in shares] + [width])


def shards(object_tiles, probe, measured, offset_row, offset_col, subpixel, live_count):
    rows, _, width = object_tiles.shape
    modes, size = probe.shape[:2]
    tables = dft_tables(size)
    bounds = column_bounds(width, (0.5625,))
    stages = len(bounds) - 1
    rims = [
        passed_along(object_tiles[:size, :, low:high].reshape(size, 2 * (high - low)), "row", -1)
        for low, high in zip(bounds[:-1], bounds[1:])
    ]
    core = lax.axis_index("row") % 2
    places = jnp.stack(
        [offset_row, offset_col, subpixel] + [jnp.broadcast_to(x, offset_row.shape) for x in (live_count, core)]
    )
    places, order = lax.optimization_barrier((places, piece_order("row")))
    own = object_tiles.reshape(rows, 2 * width)
    flat = probe.reshape(modes, size, 2 * size)
    carried = None
    grads = []
    for stage in range(stages):
        moved, grad, *rest = project(stage, bounds, places, own, rims, flat, measured, tables, width, carried)
        grads.append(grad)
        carried = [moved] + rest
    given = carried[1]
    edges = (0, width // 2 // LANES * LANES, width)
    belows = [
        settle(places, grads, bounds, low, high, size, BF16, width, f"below_{low}")
        for low, high in zip(edges[:-1], edges[1:])
    ]
    aboves = [passed_along(belows[0], "row", 1)]
    held = {}

    def beside(x):
        return lax.optimization_barrier((x, belows[0]))[0]

    def during(x):
        x, aboves[0], held["below"] = lax.optimization_barrier((x, aboves[0], belows[1]))
        return x

    def between(x):
        aboves.append(passed_along(held["below"], "row", 1))
        own_rows = settle(places, grads, bounds, 0, width, 0, F32, width, "own_rows")
        x, aboves[1], held["own"] = lax.optimization_barrier((x, aboves[1], own_rows))
        return x

    def last(x):
        object_grad = finish(held["own"], aboves, edges, width)
        x, held["object_grad"] = lax.optimization_barrier((x, object_grad))
        return x

    probe_grad = summed(given, "row", probe.shape, order, beside, during, between, last)
    object_grad = held["object_grad"]
    return object_grad, probe_grad, moved


def solution(mesh):
    in_specs = (
        P(("groups", "row"), None, None),
        P(),
        P(("groups", "row"), None, None),
        P(("groups", "row")),
        P(("groups", "row")),
        P(("groups", "row")),
        P(("groups", "row")),
    )
    out_specs = (
        P(("groups", "row"), None, None),
        P("groups", None, None, None),
        P(None, ("groups", "row")),
    )
    return jax.shard_map(shards, mesh=mesh, in_specs=in_specs, out_specs=out_specs, check_vma=False)
```
